32 devices in a mesh: seq: 8 (over y, x, core), mem: 4 (over z).
Axes of the slice: x: 2, y: 2, z: 4, core: 2. Of those that a mesh axis runs over, the one named last changes fastest.
Arguments:
- tokens: bfloat16 [32, 1024, 768], P(('seq', 'mem')), may hold values from -6 to 6
- memory: bfloat16 [32, 1024, 768], P('seq', 'mem')
- cotangent: bfloat16 [32, 1024, 768], P(('seq', 'mem'))
- table_len: int32 [32], P(('seq', 'mem')), may hold values from 512 to 1024, as said below
- patch_count: int32 [32], P(('seq', 'mem')), may hold values from 512 to 1024, as said below
- attn_master: float32 [8, 768, 768], P(None, ('seq', 'mem'))
- attn_first: float32 [8, 768, 768], P(None, ('seq', 'mem')), may hold values from -0.00048828125 to 0.00048828125
- attn_second: float32 [8, 768, 768], P(None, ('seq', 'mem')), may hold values from 5.2968973e-11 to 8.4750357e-10
- mlp_master: float32 [3, 768, 2048], P(None, ('seq', 'mem'))
- mlp_first: float32 [3, 768, 2048], P(None, ('seq', 'mem')), may hold values from -0.00048828125 to 0.00048828125
- mlp_second: float32 [3, 768, 2048], P(None, ('seq', 'mem')), may hold values from 5.2968973e-11 to 8.4750357e-10
- gain_master: float32 [3, 768], P(None, ('seq', 'mem'))
- gain_first: float32 [3, 768], P(None, ('seq', 'mem')), may hold values from -0.0017089844 to 0.0017089844
- gain_second: float32 [3, 768], P(None, ('seq', 'mem')), may hold values from 4.767208e-10 to 7.627532e-09
Outputs:
- mixed_out: bfloat16 [32, 1024, 768], P(('seq', 'mem'))
- grad_tokens: float32 [32, 1024, 768], P(('seq', 'mem'))
- grad_memory: float32 [32, 1024, 768], P('seq', 'mem')
- grad_norm: float32 [], replicated
- attn_new: float32 [8, 768, 768], P(None, ('seq', 'mem'))
- attn_first_new: float32 [8, 768, 768], P(None, ('seq', 'mem'))
- attn_second_new: float32 [8, 768, 768], P(None, ('seq', 'mem'))
- mlp_new: float32 [3, 768, 2048], P(None, ('seq', 'mem'))
- mlp_first_new: float32 [3, 768, 2048], P(None, ('seq', 'mem'))
- mlp_second_new: float32 [3, 768, 2048], P(None, ('seq', 'mem'))
- gain_new: float32 [3, 768], P(None, ('seq', 'mem'))
- gain_first_new: float32 [3, 768], P(None, ('seq', 'mem'))
- gain_second_new: float32 [3, 768], P(None, ('seq', 'mem'))
The draws below stay inside these ranges and needn't reach their ends.
Inputs may be any that keep to these rules, and one draw needn't show every extreme that they name: The tokens of table i fill its first table_len[i] slots; some table fills all 1024. The live patches of plot i are its first patch_count[i] slots; in each run of 4 plots starting at a multiple of 4, one plot has all 1024 live.
All inputs are finite; a program needn't handle non-finite values.
Results may differ from the reference program's by a relative error of at most 0.02.
The reference program's roundings to bfloat16 on the way count: a program that leaves them out, or rounds other values in their place, can miss the bound.
Values may be sent and summed in bfloat16 or wider, within the bound.
No kernel may reach another device: no remote copies, remote signals or barrier semaphores. Data moves between devices by JAX's collectives and lax.ppermute only.
A program may use at most 384 MiB of HBM per device.

```python
import math
import jax
import jax.numpy as jnp
from jax import lax

D = 768
HEADS = 12
HD = 64
FF = 2048
LEN = 1024
PATCH = 1024
STEP = 10
GROUP = 4
PLOTS = 32
NPARAM = 9439488


ATTN_SCALES = (1.5, 1.5, 1.0, 4.0, 1.5, 0.8, 1.0, 3.0)


def draw_memory(key, part):
    key = jax.random.fold_in(key, 11)
    column = jnp.arange(D, dtype=jnp.float32) / (D - 1)
    scales = 0.7 + 1.4 * column
    noise = jax.random.normal(key, (PLOTS, PATCH, D), jnp.float32)
    return (noise * scales).astype(jnp.bfloat16)


def draw_cotangent(key, part):
    key = jax.random.fold_in(key, 13)
    column = jnp.arange(D, dtype=jnp.float32) / (D - 1)
    scales = 0.6 + 1.2 * column
    noise = jax.random.normal(key, (PLOTS, LEN, D), jnp.float32)
    return (noise * scales).astype(jnp.bfloat16)


def draw_table_len(key, part):
    key = jax.random.fold_in(key, 17)
    first_key, second_key = jax.random.split(key)
    lengths = jax.random.randint(first_key, (PLOTS,), LEN // 2, LEN + 1, dtype=jnp.int32)
    chosen = jax.random.randint(second_key, (), 0, PLOTS, dtype=jnp.int32)
    return jnp.where(jnp.arange(PLOTS, dtype=jnp.int32) == chosen, LEN, lengths).astype(jnp.int32)


def draw_patch_count(key, part):
    key = jax.random.fold_in(key, 19)
    first_key, second_key = jax.random.split(key)
    counts = jax.random.randint(first_key, (PLOTS // GROUP, GROUP), PATCH // 2, PATCH + 1, dtype=jnp.int32)
    chosen = jax.random.randint(second_key, (PLOTS // GROUP, 1), 0, GROUP, dtype=jnp.int32)
    counts = jnp.where(jnp.arange(GROUP, dtype=jnp.int32)[None, :] == chosen, PATCH, counts)
    return counts.reshape(PLOTS).astype(jnp.int32)


def draw_attn_master(key, part):
    key = jax.random.fold_in(key, 23)
    scales = jnp.array(ATTN_SCALES, jnp.float32)[:, None, None] / math.sqrt(D)
    noise = jax.random.normal(key, (8, D, D), jnp.float32)
    return noise * scales


def draw_mlp_master(key, part):
    key = jax.random.fold_in(key, 29)
    scales = jnp.array([1.0 / math.sqrt(D), 1.0 / math.sqrt(D), 2.0 / math.sqrt(FF)], jnp.float32)[:, None, None]
    noise = jax.random.normal(key, (3, D, FF), jnp.float32)
    return noise * scales


def draw_gain_master(key, part):
    key = jax.random.fold_in(key, 31)
    column = jnp.arange(D, dtype=jnp.float32) / (D - 1)
    profile = 0.5 + column
    noise = 1.0 + 0.1 * jax.random.normal(key, (3, D), jnp.float32)
    return profile[None, :] * noise


def shard_levels(rng, shape, cuts, smallest, largest):
    def one(dim, blocks):
        heights = jax.random.uniform(jax.random.fold_in(jax.random.fold_in(rng, 6), dim), (blocks,), jnp.float32, smallest / len(cuts), largest / len(cuts))
        return jnp.repeat(jnp.exp(heights), shape[dim] // blocks).reshape((-1,) + (1,) * (len(shape) - dim - 1))

    loudness = one(*cuts[0])
    for cut in cuts[1:]:
        loudness = loudness * one(*cut)
    return loudness


def normal_values(own_key, shape, scale, most, shards=(), kind=jnp.bfloat16):
    values = scale * jax.random.normal(own_key, shape, jnp.float32)
    if shards:
        values = values * shard_levels(own_key, shape, shards, -0.22, 0.18)
    return jnp.clip(values, -most, most).astype(kind)


def setup_inputs(seed: int = 0) -> dict:
    key_list = jax.random.split(jax.random.key(seed), 15)
    return {
        "tokens": normal_values(key_list[0], (PLOTS, LEN, D), 1.0, 6.0, ((0, 32),)),
        "memory": draw_memory(jax.random.fold_in(key_list[14], 71), 0),
        "cotangent": draw_cotangent(jax.random.fold_in(key_list[14], 71), 0),
        "table_len": draw_table_len(jax.random.fold_in(key_list[14], 71), 0),
        "patch_count": draw_patch_count(jax.random.fold_in(key_list[14], 71), 0),
        "attn_master": draw_attn_master(jax.random.fold_in(key_list[14], 71), 0),
        "attn_first": normal_values(key_list[6], (8, D, D), (0.11 / NPARAM ** 0.5), 0.00048828125, ((1, 32),), jnp.float32),
        "attn_second": jnp.clip(jnp.exp(math.log(8.47503567324992e-10) - 2.7725887 * jax.random.uniform(key_list[7], (8, D, D), jnp.float32) ** shard_levels(key_list[7], (8, D, D), ((1, 32),), -0.2, 0.2)), 5.2968972957812e-11, 8.47503567324992e-10),
        "mlp_master": draw_mlp_master(jax.random.fold_in(key_list[14], 71), 0),
        "mlp_first": normal_values(key_list[9], (3, D, FF), (0.11 / NPARAM ** 0.5), 0.00048828125, ((1, 32),), jnp.float32),
        "mlp_second": jnp.clip(jnp.exp(math.log(8.47503567324992e-10) - 2.7725887 * jax.random.uniform(key_list[10], (3, D, FF), jnp.float32) ** shard_levels(key_list[10], (3, D, FF), ((1, 32),), -0.2, 0.2)), 5.2968972957812e-11, 8.47503567324992e-10),
        "gain_master": draw_gain_master(jax.random.fold_in(key_list[14], 71), 0),
        "gain_first": normal_values(key_list[12], (3, D), (0.33 / NPARAM ** 0.5), 0.0017089844, ((1, 32),), jnp.float32),
        "gain_second": jnp.clip(jnp.exp(math.log(7.627532383480684e-09) - 2.7725887 * jax.random.uniform(key_list[13], (3, D), jnp.float32) ** shard_levels(key_list[13], (3, D), ((1, 32),), -0.2, 0.2)), 4.767207739675428e-10, 7.627532383480684e-09),
    }


NORM_EPSILON = 1e-06
NEG_LARGE = -1e+30
CLIP_NORM = 1.0
BETA_FIRST = 0.9
BETA_SECOND = 0.999
ADAM_EPSILON = 1e-08
RATE_MATRIX = 0.06
RATE_GAIN = 0.6
DECAY_MATRIX = 0.01
HIGHEST = lax.Precision.HIGHEST

@jax.custom_vjp
def low(v):
    return lax.optimization_barrier(v.astype(jnp.bfloat16)).astype(jnp.float32)

@jax.custom_vjp
def low_back(v):
    return v

def low_keep(v):
    return (low(v), None)

def low_pass(kept, grad):
    return (grad,)

def back_keep(v):
    return (v, None)

def back_low(kept, grad):
    return (low(grad),)
low.defvjp(low_keep, low_pass)
low_back.defvjp(back_keep, back_low)

def matmul_high(left, right):
    return jnp.matmul(left, right, precision=HIGHEST)

def rms_scaled(values, gain_row):
    return values * lax.rsqrt(lax.optimization_barrier(jnp.mean(values * values, axis=-1, keepdims=True)) + NORM_EPSILON) * gain_row

def attend_rows(query_block, key_rows, value_rows, allowed):
    scores = low_back(jnp.einsum('qhd,khd->hqk', query_block, key_rows, precision=HIGHEST) * HD ** (-0.5))
    scores = jnp.where(allowed[None], scores, NEG_LARGE)
    weights_soft = low(jax.nn.softmax(scores, axis=-1))
    return jnp.einsum('hqk,khd->qhd', weights_soft, value_rows, precision=HIGHEST)

def attention(queries, key_rows, value_rows, key_live, causal):
    row_count = queries.shape[0]
    block_rows = min(512, row_count)
    key_index = jnp.arange(key_rows.shape[0], dtype=jnp.int32)

    def one_block(offset):
        query_block = lax.dynamic_slice_in_dim(queries, offset, block_rows, 0)
        query_index = offset + jnp.arange(block_rows, dtype=jnp.int32)
        allowed = jnp.broadcast_to(key_live[None, :], (block_rows, key_rows.shape[0]))
        if causal:
            allowed = allowed & (key_index[None, :] <= query_index[:, None])
        return attend_rows(query_block, key_rows, value_rows, allowed)
    offsets = jnp.arange(row_count // block_rows, dtype=jnp.int32) * block_rows
    result = lax.map(jax.checkpoint(one_block), offsets)
    return result.reshape(row_count, HEADS * HD)

def layer_plot(attn_weight, mlp_weight, gain_weight, residual_in, memory_rows, length, patch_total):
    positions = jnp.arange(LEN, dtype=jnp.int32)
    first_normalized = low(rms_scaled(residual_in, gain_weight[0]))
    queries = low(low_back(matmul_high(first_normalized, attn_weight[0]))).reshape(LEN, HEADS, HD)
    key_rows = low(low_back(matmul_high(first_normalized, attn_weight[1]))).reshape(LEN, HEADS, HD)
    value_rows = low(low_back(matmul_high(first_normalized, attn_weight[2]))).reshape(LEN, HEADS, HD)
    mixed_one = low(low_back(attention(queries, key_rows, value_rows, positions < length, True)))
    hidden_one = residual_in + low_back(matmul_high(mixed_one, attn_weight[3].T))
    normed_two = low(rms_scaled(hidden_one, gain_weight[1]))
    cross_queries = low(low_back(matmul_high(normed_two, attn_weight[4]))).reshape(LEN, HEADS, HD)
    memory_keys = low(low_back(matmul_high(memory_rows, attn_weight[5]))).reshape(PATCH, HEADS, HD)
    memory_values = low(low_back(matmul_high(memory_rows, attn_weight[6]))).reshape(PATCH, HEADS, HD)
    patch_live = jnp.arange(PATCH, dtype=jnp.int32) < patch_total
    mixed_two = low(low_back(attention(cross_queries, memory_keys, memory_values, patch_live, False)))
    hidden_two = hidden_one + low_back(matmul_high(mixed_two, attn_weight[7].T))
    third_normalized = low(rms_scaled(hidden_two, gain_weight[2]))
    gate_pre = low_back(matmul_high(third_normalized, mlp_weight[0]))
    up_pre = low_back(matmul_high(third_normalized, mlp_weight[1]))
    inner_act = low(jax.nn.gelu(gate_pre, approximate=True) * up_pre)
    return hidden_two + low_back(matmul_high(inner_act, mlp_weight[2].T))

def adam_step(master, grad, first, second, rate, decay):
    first_new = BETA_FIRST * first + (1.0 - BETA_FIRST) * grad
    second_new = BETA_SECOND * second + (1.0 - BETA_SECOND) * grad * grad
    first_hat = first_new / (1.0 - BETA_FIRST ** STEP)
    second_hat = second_new / (1.0 - BETA_SECOND ** STEP)
    master_new = master - rate * (first_hat / (jnp.sqrt(second_hat) + ADAM_EPSILON) + decay * master)
    return (master_new, first_new, second_new)

def reference(tokens, memory, cotangent, table_len, patch_count, attn_master, attn_first, attn_second, mlp_master, mlp_first, mlp_second, gain_master, gain_first, gain_second):

    def forward(attn_weight, mlp_weight, gain_weight, residual_all, memory_all):
        attn_low = low(attn_weight)
        mlp_low = low(mlp_weight)
        gain_low = low(gain_weight)

        def per_plot(plot_items):
            residual_in, memory_rows, length, patch_total = plot_items
            return layer_plot(attn_low, mlp_low, gain_low, residual_in, memory_rows, length, patch_total)
        return lax.map(per_plot, (residual_all, memory_all, table_len, patch_count))
    output, pullback = jax.vjp(forward, attn_master, mlp_master, gain_master, tokens.astype(jnp.float32), memory.astype(jnp.float32))
    positions = jnp.arange(LEN, dtype=jnp.int32)
    live_rows = (positions[None, :] < table_len[:, None]).astype(jnp.float32)[:, :, None]
    grad_attn, grad_mlp, grad_gain, grad_tokens, grad_memory = pullback(cotangent.astype(jnp.float32) * live_rows)
    grad_norm = jnp.sqrt(jnp.sum(grad_attn * grad_attn) + jnp.sum(grad_mlp * grad_mlp) + jnp.sum(grad_gain * grad_gain))
    factor = CLIP_NORM / jnp.maximum(grad_norm, CLIP_NORM)
    attn_new, attn_first_new, attn_second_new = adam_step(attn_master, grad_attn * factor, attn_first, attn_second, RATE_MATRIX, DECAY_MATRIX)
    mlp_new, mlp_first_new, mlp_second_new = adam_step(mlp_master, grad_mlp * factor, mlp_first, mlp_second, RATE_MATRIX, DECAY_MATRIX)
    gain_new, gain_first_new, gain_second_new = adam_step(gain_master, grad_gain * factor, gain_first, gain_second, RATE_GAIN, 0.0)
    return (output.astype(jnp.bfloat16), grad_tokens, grad_memory, grad_norm, attn_new, attn_first_new, attn_second_new, mlp_new, mlp_first_new, mlp_second_new, gain_new, gain_first_new, gain_second_new)
```

```python
import functools, math
import jax, jax.numpy as jnp
from jax import lax
from jax.sharding import PartitionSpec as P
from jax.experimental import pallas as pl
from jax.experimental.pallas import tpu as pltpu
bf=jnp.bfloat16; f32=jnp.float32
HD=64; HEADS=12
NEG=-1e30
LOG2E=math.log2(math.e)
TN=(((0,),(0,)),((),())); NN=(((1,),(0,)),((),())); NT=(((1,),(1,)),((),()))
def dg(a,b,dims): return lax.dot_general(a,b,dims,preferred_element_type=f32)
def rows16(cols, width, pad=16):
    idx=lax.broadcasted_iota(jnp.int32,(pad,width),0)
    out=jnp.zeros((pad,width),f32)
    for i,c in enumerate(cols): out=jnp.where(idx==i,c,out)
    return out.astype(bf)
def split3(x):
    hi=x.astype(bf).astype(f32); r=x-hi; mid=r.astype(bf).astype(f32); lo=r-mid
    return hi,mid,lo
def scaled_query(qT):
    s=qT.astype(f32)*(0.125*LOG2E)
    hi=s.astype(bf); lo=(s-hi.astype(f32)).astype(bf)
    return hi,lo


def causal_mask(x,q0,bq,fill):
    ki=lax.broadcasted_iota(jnp.int32,(bq,bq),0); qi=lax.broadcasted_iota(jnp.int32,(bq,bq),1)
    d=jnp.where(ki<=qi,x[q0:],fill)
    return jnp.concatenate([x[:q0],d],axis=0) if q0 else d

def fwd_kernel(len_ref,qT_ref,kT_ref,vT_ref,oT_ref,lse_ref,*,causal,bq,hs):
    L=qT_ref.shape[1]; K=kT_ref.shape[1]
    n=len_ref[0]
    kpos=lax.broadcasted_iota(jnp.int32,(1,K),1)
    kx=rows16([jnp.where(kpos<n,0.0,NEG)],K); qx=rows16([jnp.ones((1,L),f32)],L); vx=rows16([jnp.ones((1,K),f32)],K)
    ops=[]
    for h in range(hs):
        r=slice(h*HD,(h+1)*HD)
        kT=kT_ref[r,:]
        hi,lo=scaled_query(qT_ref[r,:])
        ops.append((jnp.concatenate([kT,kT,kx],axis=0),jnp.concatenate([hi,lo,qx],axis=0),jnp.concatenate([vT_ref[r,:],vx],axis=0)))
    jobs=[(h,q0) for h in range(hs) for q0 in range(0,L,bq)]
    def score(j):
        h,q0=j; ke=min(K,q0+bq) if causal else K
        return dg(ops[h][0][:,:ke],ops[h][1][:,q0:q0+bq],TN)
    nxt=score(jobs[0])
    for i,(h,q0) in enumerate(jobs):
        s=nxt
        if i+1<len(jobs): nxt=score(jobs[i+1])
        ke=s.shape[0]
        if causal: s=causal_mask(s,q0,bq,NEG)
        m=jnp.max(s,axis=0,keepdims=True)
        p=jnp.exp2(s-m).astype(bf)
        o=dg(ops[h][2][:,:ke],p,NN)
        l=o[HD:HD+1]
        oT_ref[h*HD:(h+1)*HD,q0:q0+bq]=(o[:HD]*(1.0/l)).astype(bf)
        lse_ref[h,:,q0:q0+bq]=m+jnp.log2(l)

def attn_fwd(n,qT,kT,vT,causal,bq=256,hs=2):
    D,L=qT.shape; K=kT.shape[1]
    hb=lambda w: pl.BlockSpec((hs*HD,w),lambda h:(h,0))
    return pl.pallas_call(functools.partial(fwd_kernel,causal=causal,bq=bq,hs=hs),grid=(D//HD//hs,),
      in_specs=[pl.BlockSpec(memory_space=pltpu.SMEM),hb(L),hb(K),hb(K)],
      out_specs=[hb(L),pl.BlockSpec((hs,1,L),lambda h:(h,0,0))],
      out_shape=[jax.ShapeDtypeStruct((D,L),bf),jax.ShapeDtypeStruct((D//HD,1,L),f32)],
      compiler_params=pltpu.CompilerParams(vmem_limit_bytes=48*2**20),
    )(n,qT,kT,vT)

def bwd_kernel(len_ref,qT_ref,kT_ref,vT_ref,oT_ref,gT_ref,lse_ref,dq_ref,dk_ref,dv_ref,dka,dva,*,causal,bq,hs):
    L=qT_ref.shape[1]; K=kT_ref.shape[1]
    n=len_ref[0]
    kpos=lax.broadcasted_iota(jnp.int32,(1,K),1)
    bias=jnp.where(kpos<n,0.0,NEG)
    one_k=jnp.ones((1,K),f32)
    kx=rows16([bias,one_k,one_k,one_k],K); vx=rows16([one_k,one_k,one_k],K)
    ops=[]
    for h in range(hs):
        r=slice(h*HD,(h+1)*HD)
        kT=kT_ref[r,:]; qT=qT_ref[r,:]; gT=gT_ref[r,:]
        hi,lo=scaled_query(qT)
        delta=jnp.sum(oT_ref[r,:].astype(f32)*gT.astype(f32),axis=0,keepdims=True)
        ops.append(dict(k=kT,q=qT,g=gT,kaug=jnp.concatenate([kT,kT,kx],axis=0),
          qaug=jnp.concatenate([hi,lo,rows16([jnp.ones((1,L),f32),*split3(-lse_ref[h])],L)],axis=0),
          vaug=jnp.concatenate([vT_ref[r,:],vx],axis=0),
          gaug=jnp.concatenate([gT,rows16(list(split3(-delta)),L)],axis=0)))
    jobs=[(h,q0) for h in range(hs) for q0 in reversed(range(0,L,bq))]
    def score(j):
        h,q0=j; ke=min(K,q0+bq) if causal else K; sl=slice(q0,q0+bq); o=ops[h]
        return dg(o["kaug"][:,:ke],o["qaug"][:,sl],TN),dg(o["vaug"][:,:ke],o["gaug"][:,sl],TN)
    nxt=score(jobs[0])
    for i,(h,q0) in enumerate(jobs):
        s,dp=nxt
        if i+1<len(jobs): nxt=score(jobs[i+1])
        ke=s.shape[0]; sl=slice(q0,q0+bq); o=ops[h]; r=slice(h*HD,(h+1)*HD)
        p=jnp.exp2(s)
        if causal: p=causal_mask(p,q0,bq,0.0)
        ds=(p*dp).astype(bf)
        pb=p.astype(bf)
        dq_ref[r,sl]=(dg(o["k"][:,:ke],ds,NN)*0.125).astype(bf)
        dv=dg(o["g"][:,sl],pb,NT)
        dk=dg(o["q"][:,sl],ds,NT)
        if q0==L-bq:
            dka[r]=dk; dva[r]=dv
        else:
            dka[r,:ke]+=dk; dva[r,:ke]+=dv
    dk_ref[...]=(dka[...]*0.125).astype(bf)
    dv_ref[...]=dva[...].astype(bf)

def attn_bwd(n,qT,kT,vT,oT,gT,lse,causal,bq=256,hs=2):
    D,L=qT.shape; K=kT.shape[1]
    hb=lambda w: pl.BlockSpec((hs*HD,w),lambda h:(h,0))
    return pl.pallas_call(functools.partial(bwd_kernel,causal=causal,bq=bq,hs=hs),grid=(D//HD//hs,),
      in_specs=[pl.BlockSpec(memory_space=pltpu.SMEM),hb(L),hb(K),hb(K),hb(L),hb(L),pl.BlockSpec((hs,1,L),lambda h:(h,0,0))],
      out_specs=[hb(L),hb(K),hb(K)],
      out_shape=[jax.ShapeDtypeStruct((D,L),bf),jax.ShapeDtypeStruct((D,K),bf),jax.ShapeDtypeStruct((D,K),bf)],
      scratch_shapes=[pltpu.VMEM((hs*HD,K),f32),pltpu.VMEM((hs*HD,K),f32)],
      compiler_params=pltpu.CompilerParams(vmem_limit_bytes=48*2**20),
    )(n,qT,kT,vT,oT,gT,lse)

TT=(((0,),(1,)),((),()))
EPS=1e-6
VL=60*2**20
def cp(): return pltpu.CompilerParams(vmem_limit_bytes=VL)
def full(shape): return pl.BlockSpec(shape,lambda i:(0,)*len(shape))
GC=0.7978845608028654

def rms_r(v): return lax.rsqrt(jnp.mean(v*v,axis=-1,keepdims=True)+EPS)

def proj_kernel(x_ref,g_ref,w_ref,n_ref,yT_ref):
    @pl.when(pl.program_id(0)==0)
    def _():
        x=x_ref[...].astype(f32)
        n_ref[...]=(x*rms_r(x)*g_ref[0:1,:]).astype(bf)
    yT_ref[...]=dg(w_ref[...],n_ref[...],TT).astype(bf)
def norm_proj(x,g,w,fb=384):
    L,D=x.shape; F=w.shape[1]
    return pl.pallas_call(proj_kernel,grid=(F//fb,),
      in_specs=[full((L,D)),full((1,D)),pl.BlockSpec((D,fb),lambda i:(0,i))],
      out_specs=[full((L,D)),pl.BlockSpec((fb,L),lambda i:(i,0))],
      out_shape=[jax.ShapeDtypeStruct((L,D),bf),jax.ShapeDtypeStruct((F,L),bf)],compiler_params=cp())(x,g,w)
def memproj_kernel(x_ref,w_ref,yT_ref):
    yT_ref[...]=dg(w_ref[...],x_ref[...],TT).astype(bf)
def mem_proj(x,w,fb=384):
    L,D=x.shape; F=w.shape[1]
    return pl.pallas_call(memproj_kernel,grid=(F//fb,),
      in_specs=[full((L,D)),pl.BlockSpec((D,fb),lambda i:(0,i))],
      out_specs=pl.BlockSpec((fb,L),lambda i:(i,0)),
      out_shape=jax.ShapeDtypeStruct((F,L),bf),compiler_params=cp())(x,w)

def post_self_kernel(x_ref,oT_ref,w3_ref,w4_ref,g_ref,h_ref,n_ref,cT_ref):
    h=x_ref[...].astype(f32)+dg(oT_ref[...],w3_ref[...],TT)
    h_ref[...]=h
    n=(h*rms_r(h)*g_ref[0:1,:]).astype(bf)
    n_ref[...]=n
    cT_ref[...]=dg(n,w4_ref[...],NN).astype(bf).T
def post_self(x,oT,w3,w4,g,tb=256):
    L,D=x.shape
    tok=pl.BlockSpec((tb,D),lambda i:(i,0)); tokT=pl.BlockSpec((D,tb),lambda i:(0,i))
    return pl.pallas_call(post_self_kernel,grid=(L//tb,),
      in_specs=[tok,tokT,full((D,D)),full((D,D)),full((1,D))],
      out_specs=[tok,tok,tokT],
      out_shape=[jax.ShapeDtypeStruct((L,D),f32),jax.ShapeDtypeStruct((L,D),bf),jax.ShapeDtypeStruct((D,L),bf)],compiler_params=cp())(x,oT,w3,w4,g)

def mlp_kernel(len_ref,h1_ref,oT_ref,w7_ref,cot_ref,g_ref,wg_ref,wu_ref,wd_ref,
               out_ref,gh_ref,gmT_ref,dw7_ref,dg_ref,dwg_ref,dwu_ref,dwd_ref,
               h2,n3,gb,oacc,nacc,*,tb):
    L,D=h1_ref.shape
    i=pl.program_id(0); last=pl.num_programs(0)-1
    nt=L//tb
    @pl.when(i==0)
    def _():
        n=len_ref[0]
        def body(t,c):
            sl=pl.ds(pl.multiple_of(t*tb,tb),tb)
            h=h1_ref[sl,:]+dg(oT_ref[:,sl],w7_ref[...],TT)
            h2[sl,:]=h
            n3[sl,:]=(h*rms_r(h)*g_ref[0:1,:]).astype(bf)
            row=t*tb+lax.broadcasted_iota(jnp.int32,(tb,1),0)
            gb[sl,:]=jnp.where(row<n,cot_ref[sl,:].astype(f32),0.0).astype(bf)
            return c
        for t in range(nt): body(t,0)
    n3v=n3[...]; gbv=gb[...]
    wg=wg_ref[...]; wu=wu_ref[...]; wd=wd_ref[...]
    g=dg(n3v,wg,NN); u=dg(n3v,wu,NN); di=dg(gbv,wd,NN)
    g2=g*g
    t=jnp.tanh(g*(GC+(GC*0.044715)*g2))
    hp=0.5+0.5*t
    ge=g*hp
    dge=hp+(0.5*g)*(1.0-t*t)*(GC+(3*GC*0.044715)*g2)
    inner=(ge*u).astype(bf)
    dgate=(di*u*dge).astype(bf)
    dup=(di*ge).astype(bf)
    o=dg(inner,wd,NT)
    dn=dg(dgate,wg,NT)+dg(dup,wu,NT)
    dwg_ref[...]=dg(n3v,dgate,TN).astype(bf)
    dwu_ref[...]=dg(n3v,dup,TN).astype(bf)
    dwd_ref[...]=dg(gbv,inner,TN).astype(bf)
    @pl.when(i==0)
    def _():
        oacc[...]=o; nacc[...]=dn
    @pl.when(i>0)
    def _():
        oacc[...]+=o; nacc[...]+=dn
    @pl.when(i==last)
    def _():
        n=len_ref[0]
        acc=jnp.zeros((1,D),f32)
        for t in range(nt):
            sl=slice(t*tb,(t+1)*tb)
            h=h2[sl,:]; uu=nacc[sl,:]
            out_ref[sl,:]=(h+oacc[sl,:]).astype(bf)
            r=rms_r(h); ug=uu*g_ref[0:1,:]
            gh=gb[sl,:].astype(f32)+r*ug-h*((r*r*r)*jnp.mean(ug*h,axis=-1,keepdims=True))
            acc=acc+jnp.sum(uu*h*r,axis=0,keepdims=True)
            gh_ref[sl,:]=gh
            b=gh.astype(bf)
            n3[sl,:]=b
            gmT_ref[:,sl]=dg(b,w7_ref[...],NN).astype(bf).T
        dg_ref[...]=acc
        dw7_ref[...]=dg(n3[...],oT_ref[...],TT).astype(bf)
def mlp(n,h1,oT,w7,cot,g,wm,fc=512,tb=256):
    L,D=h1.shape; F=wm.shape[1]//3; nc=F//fc
    wb=lambda j: pl.BlockSpec((D,fc),lambda i,j=j:(0,j*nc+i))
    gb_=pl.BlockSpec((D,fc),lambda i:(0,i))
    S=jax.ShapeDtypeStruct
    return pl.pallas_call(functools.partial(mlp_kernel,tb=tb),grid=(nc,),
      in_specs=[pl.BlockSpec(memory_space=pltpu.SMEM),full((L,D)),full((D,L)),full((D,D)),full((L,D)),full((1,D)),wb(0),wb(1),wb(2)],
      out_specs=[full((L,D)),full((L,D)),full((D,L)),full((D,D)),full((1,D)),gb_,gb_,gb_],
      out_shape=[S((L,D),bf),S((L,D),f32),S((D,L),bf),S((D,D),bf),S((1,D),f32)]+[S((D,F),bf)]*3,
      scratch_shapes=[pltpu.VMEM((L,D),f32),pltpu.VMEM((L,D),bf),pltpu.VMEM((L,D),bf),pltpu.VMEM((L,D),f32),pltpu.VMEM((L,D),f32)],
      compiler_params=cp())(n,h1,oT,w7,cot,g,wm,wm,wm)

def mid_kernel(h1_ref,gh2_ref,dcT_ref,w4_ref,w3_ref,g_ref,gh1_ref,gmT_ref,gb_ref,dg_ref):
    i=pl.program_id(0)
    u=dg(dcT_ref[...],w4_ref[...],TT)
    h=h1_ref[...]
    r=rms_r(h); ug=u*g_ref[0:1,:]
    gh=gh2_ref[...]+r*ug-h*((r*r*r)*jnp.mean(ug*h,axis=-1,keepdims=True))
    gh1_ref[...]=gh
    b=gh.astype(bf)
    gb_ref[...]=b
    gmT_ref[...]=dg(b,w3_ref[...],NN).astype(bf).T
    s=jnp.sum(u*h*r,axis=0,keepdims=True)
    @pl.when(i==0)
    def _(): dg_ref[...]=s
    @pl.when(i>0)
    def _(): dg_ref[...]+=s
def mid(h1,gh2,dcT,w4,w3,g,tb=256):
    L,D=h1.shape
    tok=pl.BlockSpec((tb,D),lambda i:(i,0)); tokT=pl.BlockSpec((D,tb),lambda i:(0,i))
    S=jax.ShapeDtypeStruct
    return pl.pallas_call(mid_kernel,grid=(L//tb,),
      in_specs=[tok,tok,tokT,full((D,D)),full((D,D)),full((1,D))],
      out_specs=[tok,tokT,tok,full((1,D))],
      out_shape=[S((L,D),f32),S((D,L),bf),S((L,D),bf),S((1,D),f32)],compiler_params=cp())(h1,gh2,dcT,w4,w3,g)

def wgrad_kernel(a_ref,gT_ref,o_ref):
    o_ref[...]=dg(a_ref[...],gT_ref[...],TT).astype(bf)
def wgrad(a,gT,fb=384):
    L,D=a.shape; F=gT.shape[0]
    return pl.pallas_call(wgrad_kernel,grid=(F//fb,),
      in_specs=[full((L,D)),pl.BlockSpec((fb,L),lambda i:(i,0))],
      out_specs=pl.BlockSpec((D,fb),lambda i:(0,i)),
      out_shape=jax.ShapeDtypeStruct((D,F),bf),compiler_params=cp())(a,gT)

def gmem_kernel(kT_ref,vT_ref,w5_ref,w6_ref,o_ref):
    o_ref[...]=(dg(kT_ref[...],w5_ref[...],TT)+dg(vT_ref[...],w6_ref[...],TT)).astype(bf)
def gmem(kT,vT,w56,tb=256):
    D,L=kT.shape
    tokT=pl.BlockSpec((D,tb),lambda i:(0,i))
    return pl.pallas_call(gmem_kernel,grid=(L//tb,),
      in_specs=[tokT,tokT,pl.BlockSpec((D,D),lambda i:(0,0)),pl.BlockSpec((D,D),lambda i:(0,1))],
      out_specs=pl.BlockSpec((tb,D),lambda i:(i,0)),
      out_shape=jax.ShapeDtypeStruct((L,D),bf),compiler_params=cp())(kT,vT,w56,w56)

def first_kernel(x_ref,gh1_ref,qT_ref,kT_ref,vT_ref,w0_ref,w1_ref,w2_ref,g_ref,gt_ref,dg_ref):
    i=pl.program_id(0)
    u=dg(qT_ref[...],w0_ref[...],TT)+dg(kT_ref[...],w1_ref[...],TT)+dg(vT_ref[...],w2_ref[...],TT)
    h=x_ref[...].astype(f32)
    r=rms_r(h); ug=u*g_ref[0:1,:]
    gt_ref[...]=gh1_ref[...]+r*ug-h*((r*r*r)*jnp.mean(ug*h,axis=-1,keepdims=True))
    s=jnp.sum(u*h*r,axis=0,keepdims=True)
    @pl.when(i==0)
    def _(): dg_ref[...]=s
    @pl.when(i>0)
    def _(): dg_ref[...]+=s
def first(x,gh1,qT,kT,vT,w,g,tb=256):
    L,D=x.shape
    tok=pl.BlockSpec((tb,D),lambda i:(i,0)); tokT=pl.BlockSpec((D,tb),lambda i:(0,i))
    S=jax.ShapeDtypeStruct
    wb=lambda j: pl.BlockSpec((D,D),lambda i,j=j:(0,j))
    return pl.pallas_call(first_kernel,grid=(L//tb,),
      in_specs=[tok,tok,tokT,tokT,tokT,wb(0),wb(1),wb(2),full((1,D))],
      out_specs=[tok,full((1,D))],
      out_shape=[S((L,D),f32),S((1,D),f32)],compiler_params=cp())(x,gh1,qT,kT,vT,w,w,w,g)

STEP=10
CLIP_NORM=1.0
BETA_FIRST=0.9
BETA_SECOND=0.999
ADAM_EPSILON=1e-08
RATE_MATRIX=0.06
RATE_GAIN=0.6
DECAY_MATRIX=0.01
AXES=("seq","mem")


def adam_step(master,grad,first_moment,second_moment,rate,decay):
    first_new=BETA_FIRST*first_moment+(1.0-BETA_FIRST)*grad
    second_new=BETA_SECOND*second_moment+(1.0-BETA_SECOND)*grad*grad
    first_hat=first_new/(1.0-BETA_FIRST**STEP)
    second_hat=second_new/(1.0-BETA_SECOND**STEP)
    master_new=master-rate*(first_hat/(jnp.sqrt(second_hat)+ADAM_EPSILON)+decay*master)
    return (master_new,first_new,second_new)


def columns(stack):
    return jnp.concatenate([stack[i] for i in range(stack.shape[0])],axis=1)


def gather(shard):
    return lax.all_gather(shard,AXES,axis=0,tiled=True)


def scatter(parts):
    return lax.psum_scatter(jnp.concatenate(parts,axis=1),AXES,scatter_dimension=0,tiled=True).astype(f32)


def on_device(tokens,memory,cotangent,table_len,patch_count,attn_master,attn_first,attn_second,mlp_master,mlp_first,mlp_second,gain_master,gain_first,gain_second):
    rows=attn_master.shape[1]
    D=attn_master.shape[2]
    aw=attn_master.astype(bf)
    gain_cols=jnp.pad(gain_master.T,((0,0),(0,125))).astype(bf)
    w_first=gather(jnp.concatenate([columns(aw[:3]),gain_cols],axis=1))
    w_second=gather(columns(aw[3:]))
    w_mlp=gather(columns(mlp_master.astype(bf)))
    mem=lax.all_to_all(memory,"mem",split_axis=0,concat_axis=0,tiled=True).reshape(-1,D)
    gains=w_first[:,3*D:3*D+8].astype(f32).T
    g=[gains[i:i+1] for i in range(3)]
    w_qkv=w_first[:,:3*D]
    w3,w4,w56,w7=w_second[:,:D],w_second[:,D:2*D],w_second[:,2*D:4*D],w_second[:,4*D:]
    x=tokens[0]
    n1,qkv=norm_proj(x,g[0],w_qkv)
    q,k,v=qkv[:D],qkv[D:2*D],qkv[2*D:]
    o1,lse1=attn_fwd(table_len,q,k,v,True,512,4)
    h1,n2,cq=post_self(x,o1,w3,w4,g[1])
    mkv=mem_proj(mem,w56)
    mk,mv=mkv[:D],mkv[D:]
    o2,lse2=attn_fwd(patch_count,cq,mk,mv,False,512,2)
    mixed_out,gh2,gm2,dw7,dg3,dwg,dwu,dwd=mlp(table_len,h1,o2,w7,cotangent[0],g[2],w_mlp)
    r_mlp=scatter([dwg,dwu,dwd])
    dcq,dmk,dmv=attn_bwd(patch_count,cq,mk,mv,o2,gm2,lse2,False,256,2)
    gh1,gm1,gb1,dg2=mid(h1,gh2,dcq,w4,w3,g[1])
    gmem_local=gmem(dmk,dmv,w56)
    grad_memory=lax.all_to_all(gmem_local.reshape(memory.shape),"mem",split_axis=0,concat_axis=0,tiled=True).astype(f32)
    dw4=wgrad(n2,dcq)
    dw5=wgrad(mem,dmk)
    dw6=wgrad(mem,dmv)
    dw3=wgrad(gb1,o1)
    r_second=scatter([dw3,dw4,dw5,dw6,dw7])
    dq,dk,dv=attn_bwd(table_len,q,k,v,o1,gm1,lse1,True,256,2)
    dw0=wgrad(n1,dq); dw1=wgrad(n1,dk); dw2=wgrad(n1,dv)
    grad_tokens,dg1=first(x,gh1,dq,dk,dv,w_qkv,g[0])
    dgain=jnp.pad(jnp.concatenate([dg1,dg2,dg3],axis=0).T,((0,0),(0,125))).astype(bf)
    r_first=scatter([dw0,dw1,dw2,dgain])
    split=lambda r,n,w: jnp.stack([r[:,i*w:(i+1)*w] for i in range(n)])
    attn_red=jnp.concatenate([split(r_first,3,D),split(r_second,5,D)],axis=0)
    mlp_red=split(r_mlp,3,mlp_master.shape[2])
    gain_red=r_first[:,3*D:3*D+3].T
    squares=jnp.sum(attn_red*attn_red)+jnp.sum(mlp_red*mlp_red)+jnp.sum(gain_red*gain_red)
    grad_norm=jnp.sqrt(lax.psum(squares,AXES))
    factor=CLIP_NORM/jnp.maximum(grad_norm,CLIP_NORM)
    a=adam_step(attn_master,attn_red*factor,attn_first,attn_second,RATE_MATRIX,DECAY_MATRIX)
    m=adam_step(mlp_master,mlp_red*factor,mlp_first,mlp_second,RATE_MATRIX,DECAY_MATRIX)
    gn=adam_step(gain_master,gain_red*factor,gain_first,gain_second,RATE_GAIN,0.0)
    return (mixed_out[None],grad_tokens[None],grad_memory,grad_norm)+a+m+gn


def solution(mesh):
    both=P(("seq","mem"),None,None)
    mid_split=P(None,("seq","mem"),None)
    gain_split=P(None,("seq","mem"))
    return jax.shard_map(on_device,mesh=mesh,
        in_specs=(both,P("seq","mem",None),both,P(("seq","mem")),P(("seq","mem")))+(mid_split,)*6+(gain_split,)*3,
        out_specs=(both,both,P("seq","mem",None),P())+(mid_split,)*6+(gain_split,)*3,
        check_vma=False)
```

```python
import functools, math
import jax, jax.numpy as jnp
from jax import lax
from jax.sharding import PartitionSpec as P
from jax.experimental import pallas as pl
from jax.experimental.pallas import tpu as pltpu
bf=jnp.bfloat16; f32=jnp.float32
HD=64; HEADS=12
NEG=-1e30
VA=24*2**20
LOG2E=math.log2(math.e)
TN=(((0,),(0,)),((),())); NN=(((1,),(0,)),((),())); NT=(((1,),(1,)),((),()))
def dg(a,b,dims): return lax.dot_general(a,b,dims,preferred_element_type=f32)
def rows16(cols, width, pad=16):
    idx=lax.broadcasted_iota(jnp.int32,(pad,width),0)
    out=jnp.zeros((pad,width),f32)
    for i,c in enumerate(cols): out=jnp.where(idx==i,c,out)
    return out.astype(bf)
def split3(x):
    hi=x.astype(bf).astype(f32); r=x-hi; mid=r.astype(bf).astype(f32); lo=r-mid
    return hi,mid,lo
def scaled_query(qT):
    s=qT.astype(f32)*(0.125*LOG2E)
    hi=s.astype(bf); lo=(s-hi.astype(f32)).astype(bf)
    return hi,lo


def causal_mask(x,q0,bq,fill):
    ki=lax.broadcasted_iota(jnp.int32,(bq,bq),0); qi=lax.broadcasted_iota(jnp.int32,(bq,bq),1)
    d=jnp.where(ki<=qi,x[q0:],fill)
    return jnp.concatenate([x[:q0],d],axis=0) if q0 else d

def fwd_kernel(len_ref,qT_ref,kT_ref,vT_ref,oT_ref,lse_ref,*,causal,bq,hs):
    L=qT_ref.shape[1]; K=kT_ref.shape[1]
    n=len_ref[0]
    kpos=lax.broadcasted_iota(jnp.int32,(1,K),1)
    kx=rows16([jnp.where(kpos<n,0.0,NEG)],K); qx=rows16([jnp.ones((1,L),f32)],L); vx=rows16([jnp.ones((1,K),f32)],K)
    ops=[]
    for h in range(hs):
        r=slice(h*HD,(h+1)*HD)
        kT=kT_ref[r,:]
        hi,lo=scaled_query(qT_ref[r,:])
        ops.append((jnp.concatenate([kT,kT,kx],axis=0),jnp.concatenate([hi,lo,qx],axis=0),jnp.concatenate([vT_ref[r,:],vx],axis=0)))
    jobs=[(h,q0) for h in range(hs) for q0 in range(0,L,bq)]
    def score(j):
        h,q0=j; ke=min(K,q0+bq) if causal else K
        return dg(ops[h][0][:,:ke],ops[h][1][:,q0:q0+bq],TN)
    nxt=score(jobs[0])
    for i,(h,q0) in enumerate(jobs):
        s=nxt
        if i+1<len(jobs): nxt=score(jobs[i+1])
        ke=s.shape[0]
        if causal: s=causal_mask(s,q0,bq,NEG)
        m=jnp.max(s,axis=0,keepdims=True)
        p=jnp.exp2(s-m).astype(bf)
        o=dg(ops[h][2][:,:ke],p,NN)
        l=o[HD:HD+1]
        oT_ref[h*HD:(h+1)*HD,q0:q0+bq]=(o[:HD]*(1.0/l)).astype(bf)
        lse_ref[h,:,q0:q0+bq]=m+jnp.log2(l)

def head_block(hs,w,offset=0):
    return pl.BlockSpec((hs*HD,w),lambda h:(h+offset//hs,0))
def attn_fwd(n,q,k,v,causal,bq=256,hs=2):
    L=q[0].shape[1]; K=k[0].shape[1]; D=HEADS*HD
    return pl.pallas_call(functools.partial(fwd_kernel,causal=causal,bq=bq,hs=hs),grid=(HEADS//hs,),
      in_specs=[pl.BlockSpec(memory_space=pltpu.SMEM),head_block(hs,L,q[1]),head_block(hs,K,k[1]),head_block(hs,K,v[1])],
      out_specs=[head_block(hs,L),pl.BlockSpec((hs,1,L),lambda h:(h,0,0))],
      out_shape=[jax.ShapeDtypeStruct((D,L),bf),jax.ShapeDtypeStruct((HEADS,1,L),f32)],
      compiler_params=pltpu.CompilerParams(vmem_limit_bytes=VA),
    )(n,q[0],k[0],v[0])

def bwd_kernel(len_ref,qT_ref,kT_ref,vT_ref,oT_ref,gT_ref,lse_ref,dq_ref,dk_ref,dv_ref,dka,dva,*,causal,bq,hs):
    L=qT_ref.shape[1]; K=kT_ref.shape[1]
    n=len_ref[0]
    kpos=lax.broadcasted_iota(jnp.int32,(1,K),1)
    bias=jnp.where(kpos<n,0.0,NEG)
    one_k=jnp.ones((1,K),f32)
    kx=rows16([bias,one_k,one_k,one_k],K); vx=rows16([one_k,one_k,one_k],K)
    ops=[]
    for h in range(hs):
        r=slice(h*HD,(h+1)*HD)
        kT=kT_ref[r,:]; qT=qT_ref[r,:]; gT=gT_ref[r,:]
        hi,lo=scaled_query(qT)
        delta=jnp.sum(oT_ref[r,:].astype(f32)*gT.astype(f32),axis=0,keepdims=True)
        ops.append(dict(k=kT,q=qT,g=gT,kaug=jnp.concatenate([kT,kT,kx],axis=0),
          qaug=jnp.concatenate([hi,lo,rows16([jnp.ones((1,L),f32),*split3(-lse_ref[h])],L)],axis=0),
          vaug=jnp.concatenate([vT_ref[r,:],vx],axis=0),
          gaug=jnp.concatenate([gT,rows16(list(split3(-delta)),L)],axis=0)))
    jobs=[(h,q0) for h in range(hs) for q0 in reversed(range(0,L,bq))]
    def score(j):
        h,q0=j; ke=min(K,q0+bq) if causal else K; sl=slice(q0,q0+bq); o=ops[h]
        return dg(o["kaug"][:,:ke],o["qaug"][:,sl],TN),dg(o["vaug"][:,:ke],o["gaug"][:,sl],TN)
    nxt=score(jobs[0])
    for i,(h,q0) in enumerate(jobs):
        s,dp=nxt
        if i+1<len(jobs): nxt=score(jobs[i+1])
        ke=s.shape[0]; sl=slice(q0,q0+bq); o=ops[h]; r=slice(h*HD,(h+1)*HD)
        p=jnp.exp2(s)
        if causal: p=causal_mask(p,q0,bq,0.0)
        ds=(p*dp).astype(bf)
        pb=p.astype(bf)
        dq_ref[r,sl]=(dg(o["k"][:,:ke],ds,NN)*0.125).astype(bf)
        dv=dg(o["g"][:,sl],pb,NT)
        dk=dg(o["q"][:,sl],ds,NT)
        if q0==L-bq:
            dka[r]=dk; dva[r]=dv
        else:
            dka[r,:ke]+=dk; dva[r,:ke]+=dv
    dk_ref[...]=(dka[...]*0.125).astype(bf)
    dv_ref[...]=dva[...].astype(bf)

def bwd_part_kernel(*refs,**kw):
    bwd_kernel(*refs[:7],*refs[10:],**kw)
def attn_bwd(n,q,k,v,oT,gT,lse,causal,bq=256,hs=2,part=None,into=None):
    L=q[0].shape[1]; K=k[0].shape[1]; D=HEADS*HD
    h0,hn=part or (0,HEADS)
    hb=lambda w,o=0: head_block(hs,w,o+h0)
    S=jax.ShapeDtypeStruct
    specs=[pl.BlockSpec(memory_space=pltpu.SMEM),hb(L,q[1]),hb(K,k[1]),hb(K,v[1]),hb(L),hb(L),pl.BlockSpec((hs,1,L),lambda h:(h+h0//hs,0,0))]
    args=(n,q[0],k[0],v[0],oT,gT,lse)
    if into is not None:
        specs+=[pl.BlockSpec(memory_space=pl.ANY)]*3
        args+=tuple(into)
    return pl.pallas_call(functools.partial(bwd_kernel if into is None else bwd_part_kernel,causal=causal,bq=bq,hs=hs),grid=(hn//hs,),
      in_specs=specs,out_specs=[hb(L),hb(K),hb(K)],
      out_shape=[S((D,L),bf),S((D,K),bf),S((D,K),bf)],
      input_output_aliases={} if into is None else {7:0,8:1,9:2},
      scratch_shapes=[pltpu.VMEM((hs*HD,K),f32),pltpu.VMEM((hs*HD,K),f32)],
      compiler_params=pltpu.CompilerParams(vmem_limit_bytes=VA),
    )(*args)

TT=(((0,),(1,)),((),()))
EPS=1e-6
VL=60*2**20
def cp(mb=24): return pltpu.CompilerParams(vmem_limit_bytes=mb*2**20)
def full(shape): return pl.BlockSpec(shape,lambda i:(0,)*len(shape))
GC=0.7978845608028654

def rms_r(v): return lax.rsqrt(jnp.mean(v*v,axis=-1,keepdims=True)+EPS)

def wcol(D,j): return pl.BlockSpec((D,D),lambda i:(0,j))
def gain_spec(D): return pl.BlockSpec((8,D),lambda i:(0,0))

def proj_kernel(x_ref,e_ref,w_ref,n_ref,yT_ref,g_ref):
    @pl.when(pl.program_id(0)==0)
    def _():
        g=e_ref[...].astype(f32).T[0:8,:]
        g_ref[...]=g
        x=x_ref[...].astype(f32)
        n_ref[...]=(x*rms_r(x)*g[0:1,:]).astype(bf)
    yT_ref[...]=dg(w_ref[...],n_ref[...],TT).astype(bf)
def norm_proj(x,w,fb=384):
    L,D=x.shape; F=3*D
    return pl.pallas_call(proj_kernel,grid=(F//fb,),
      in_specs=[full((L,D)),pl.BlockSpec((D,128),lambda i:(0,F//128)),pl.BlockSpec((D,fb),lambda i:(0,i))],
      out_specs=[full((L,D)),pl.BlockSpec((fb,L),lambda i:(i,0)),gain_spec(D)],
      out_shape=[jax.ShapeDtypeStruct((L,D),bf),jax.ShapeDtypeStruct((F,L),bf),jax.ShapeDtypeStruct((8,D),f32)],compiler_params=cp())(x,w,w)
def memproj_kernel(x_ref,w_ref,yT_ref):
    yT_ref[...]=dg(w_ref[...],x_ref[...],TT).astype(bf)
def mem_proj(x,w,first_col,fb=384):
    L,D=x.shape; F=2*D
    return pl.pallas_call(memproj_kernel,grid=(F//fb,),
      in_specs=[full((L,D)),pl.BlockSpec((D,fb),lambda i:(0,first_col//fb+i))],
      out_specs=pl.BlockSpec((fb,L),lambda i:(i,0)),
      out_shape=jax.ShapeDtypeStruct((F,L),bf),compiler_params=cp())(x,w)

def post_self_kernel(x_ref,oT_ref,w3_ref,w4_ref,g_ref,h_ref,n_ref,cT_ref):
    h=x_ref[...].astype(f32)+dg(oT_ref[...],w3_ref[...],TT)
    h_ref[...]=h
    n=(h*rms_r(h)*g_ref[1:2,:]).astype(bf)
    n_ref[...]=n
    cT_ref[...]=dg(n,w4_ref[...],NN).astype(bf).T
def post_self(x,oT,w,g,tb=256):
    L,D=x.shape
    tok=pl.BlockSpec((tb,D),lambda i:(i,0)); tokT=pl.BlockSpec((D,tb),lambda i:(0,i))
    return pl.pallas_call(post_self_kernel,grid=(L//tb,),
      in_specs=[tok,tokT,wcol(D,0),wcol(D,1),gain_spec(D)],
      out_specs=[tok,tok,tokT],
      out_shape=[jax.ShapeDtypeStruct((L,D),f32),jax.ShapeDtypeStruct((L,D),bf),jax.ShapeDtypeStruct((D,L),bf)],compiler_params=cp())(x,oT,w,w,g)

def mlp_chunk(n3,gb,wg,wu,wd,dw_ref,inner_s,dgate_s,dup_s,oacc,nacc,tb):
    L=n3.shape[0]; nt=L//tb
    def pre(t):
        sl=slice(t*tb,(t+1)*tb)
        a=n3[sl,:]
        return dg(a,wg[...],NN),dg(a,wu[...],NN),dg(gb[sl,:],wd[...],NN)
    nxt=pre(0)
    for t in range(nt):
        sl=slice(t*tb,(t+1)*tb)
        g,u,di=nxt
        if t+1<nt: nxt=pre(t+1)
        g2=g*g
        th=jnp.tanh(g*(GC+(GC*0.044715)*g2))
        hp=0.5+0.5*th
        ge=g*hp
        dge=hp+(0.5*g)*(1.0-th*th)*(GC+(3*GC*0.044715)*g2)
        inner=(ge*u).astype(bf)
        dgate=(di*u*dge).astype(bf)
        dup=(di*ge).astype(bf)
        inner_s[sl,:]=inner; dgate_s[sl,:]=dgate; dup_s[sl,:]=dup
        oacc[sl,:]+=dg(inner,wd[...],NT)
        nacc[sl,:]+=dg(dgate,wg[...],NT)+dg(dup,wu[...],NT)
    dw_ref[0]=dg(n3[...],dgate_s[...],TN).astype(bf)
    dw_ref[1]=dg(n3[...],dup_s[...],TN).astype(bf)
    dw_ref[2]=dg(gb[...],inner_s[...],TN).astype(bf)

def mlp_kernel(core_ref,len_ref,h1_ref,oT_ref,w7_ref,cot_ref,g_ref,wg_ref,wu_ref,wd_ref,
               out_ref,gh_ref,gmT_ref,gb2_ref,dg_ref,send_ref,keep_ref,
               h2,n3,gb,oacc,nacc,dw,inner_s,dgate_s,dup_s,sems,*,tb):
    L,D=h1_ref.shape
    fc=dw.shape[3]
    i=pl.program_id(0); count=pl.num_programs(0); half=count//2
    slot=lax.rem(i,2)
    def copy(step,to):
        col=pl.multiple_of(lax.rem(step,half)*fc,fc)
        return pltpu.make_async_copy(dw.at[lax.rem(step,2)],to.at[:,:,pl.ds(col,fc)],sems.at[lax.rem(step,2)])
    @pl.when(i==0)
    def _():
        n=len_ref[0]
        for t in range(L//tb):
            sl=slice(t*tb,(t+1)*tb)
            h=h1_ref[sl,:]+dg(oT_ref[:,sl],w7_ref[...],TT)
            h2[sl,:]=h
            oacc[sl,:]=h
            nacc[sl,:]=jnp.zeros((tb,D),f32)
            n3[sl,:]=(h*rms_r(h)*g_ref[2:3,:]).astype(bf)
            row=t*tb+lax.broadcasted_iota(jnp.int32,(tb,1),0)
            gb[sl,:]=jnp.where(row<n,cot_ref[sl,:].astype(f32),0.0).astype(bf)
    @pl.when(i>=2)
    def _():
        copy(i-2,send_ref).wait()
    mlp_chunk(n3,gb,wg_ref,wu_ref,wd_ref,dw.at[slot],inner_s,dgate_s,dup_s,oacc,nacc,tb)
    @pl.when(i<half)
    def _():
        copy(i,send_ref).start()
    @pl.when(i>=half)
    def _():
        copy(i,keep_ref).start()
    @pl.when(i==count-1)
    def _():
        acc=jnp.zeros((1,D),f32)
        for t in range(L//tb):
            sl=slice(t*tb,(t+1)*tb)
            h=h2[sl,:]; uu=nacc[sl,:]
            out_ref[sl,:]=oacc[sl,:].astype(bf)
            r=rms_r(h); ug=uu*g_ref[2:3,:]
            gh=gb[sl,:].astype(f32)+r*ug-h*((r*r*r)*jnp.mean(ug*h,axis=-1,keepdims=True))
            acc=acc+jnp.sum(uu*h*r,axis=0,keepdims=True)
            gh_ref[sl,:]=gh
            b=gh.astype(bf)
            gb2_ref[sl,:]=b
            gmT_ref[:,sl]=dg(b,w7_ref[...],NN).astype(bf).T
        dg_ref[...]=acc
        copy(i-1,keep_ref).wait()
        copy(i,keep_ref).wait()
def mlp(core,n,h1,oT,w_second,cot,g,wm,fc=512,tb=256):
    L,D=h1.shape; F=wm.shape[1]//3; nc=F//fc; hc=nc//2
    whole=lambda shape: pl.BlockSpec(shape,lambda i,c:(0,)*len(shape),pipeline_mode=pl.Buffered(1))
    wb=lambda j: pl.BlockSpec((D,fc),lambda i,c,j=j:(0,j*nc+lax.rem(i+(1-c[0])*hc,nc)))
    S=jax.ShapeDtypeStruct
    hbm=pl.BlockSpec(memory_space=pl.ANY)
    return pl.pallas_call(functools.partial(mlp_kernel,tb=tb),
      grid_spec=pltpu.PrefetchScalarGridSpec(num_scalar_prefetch=1,grid=(nc,),
      in_specs=[pl.BlockSpec(memory_space=pltpu.SMEM),whole((L,D)),whole((D,L)),pl.BlockSpec((D,D),lambda i,c:(0,4),pipeline_mode=pl.Buffered(1)),whole((L,D)),whole((8,D)),wb(0),wb(1),wb(2)],
      out_specs=[whole((L,D)),whole((L,D)),whole((D,L)),whole((L,D)),whole((1,D)),hbm,hbm],
      scratch_shapes=[pltpu.VMEM((L,D),f32),pltpu.VMEM((L,D),bf),pltpu.VMEM((L,D),bf),pltpu.VMEM((L,D),f32),pltpu.VMEM((L,D),f32),
        pltpu.VMEM((2,3,D,fc),bf),pltpu.VMEM((L,fc),bf),pltpu.VMEM((L,fc),bf),pltpu.VMEM((L,fc),bf),pltpu.SemaphoreType.DMA((2,))]),
      out_shape=[S((L,D),bf),S((L,D),f32),S((D,L),bf),S((L,D),bf),S((1,D),f32),S((3,D,F//2),bf),S((3,D,F//2),bf)],
      compiler_params=cp(48))(core,n,h1,oT,w_second,cot,g,wm,wm,wm)

def mid_kernel(h1_ref,gh2_ref,dcT_ref,w4_ref,w3_ref,g_ref,gh1_ref,gmT_ref,gb_ref,dg_ref):
    i=pl.program_id(0)
    u=dg(dcT_ref[...],w4_ref[...],TT)
    h=h1_ref[...]
    r=rms_r(h); ug=u*g_ref[1:2,:]
    gh=gh2_ref[...]+r*ug-h*((r*r*r)*jnp.mean(ug*h,axis=-1,keepdims=True))
    gh1_ref[...]=gh
    b=gh.astype(bf)
    gb_ref[...]=b
    gmT_ref[...]=dg(b,w3_ref[...],NN).astype(bf).T
    s=jnp.sum(u*h*r,axis=0,keepdims=True)
    @pl.when(i==0)
    def _(): dg_ref[...]=s
    @pl.when(i>0)
    def _(): dg_ref[...]+=s
def mid(h1,gh2,dcT,w,g,tb=256):
    L,D=h1.shape
    tok=pl.BlockSpec((tb,D),lambda i:(i,0)); tokT=pl.BlockSpec((D,tb),lambda i:(0,i))
    S=jax.ShapeDtypeStruct
    return pl.pallas_call(mid_kernel,grid=(L//tb,),
      in_specs=[tok,tok,tokT,wcol(D,1),wcol(D,0),gain_spec(D)],
      out_specs=[tok,tokT,tok,full((1,D))],
      out_shape=[S((L,D),f32),S((D,L),bf),S((L,D),bf),S((1,D),f32)],compiler_params=cp())(h1,gh2,dcT,w,w,g)

def wgrads_kernel(core_ref,*refs,pairs,na,ng):
    a_refs=refs[:na]; g_refs=refs[na:na+ng]; send_ref,keep_ref=refs[na+ng:]
    k=core_ref[0]
    W=send_ref.shape[2]
    for out,half in ((send_ref,1-k),(keep_ref,k)):
        start=pl.multiple_of(half*W,W)
        for m,(ia,ig) in enumerate(pairs):
            out[m]=dg(a_refs[ia][...],g_refs[ig][pl.ds(start,W),:],TT).astype(bf)
def wgrads(core,a,g,pairs):
    D=a[0].shape[1]; F=g[0].shape[0]
    v=pl.BlockSpec(memory_space=pltpu.VMEM)
    S=jax.ShapeDtypeStruct((len(pairs),D,F//2),bf)
    return pl.pallas_call(functools.partial(wgrads_kernel,pairs=tuple(pairs),na=len(a),ng=len(g)),
      in_specs=[pl.BlockSpec(memory_space=pltpu.SMEM)]+[v]*(len(a)+len(g)),out_specs=[v,v],
      out_shape=[S,S],compiler_params=cp(40))(core,*a,*g)

def gmem_kernel(kT_ref,vT_ref,w5_ref,w6_ref,o_ref):
    o_ref[...]=(dg(kT_ref[...],w5_ref[...],TT)+dg(vT_ref[...],w6_ref[...],TT)).astype(bf)
def gmem(kT,vT,w56,tb=256):
    D,L=kT.shape
    tokT=pl.BlockSpec((D,tb),lambda i:(0,i))
    return pl.pallas_call(gmem_kernel,grid=(L//tb,),
      in_specs=[tokT,tokT,wcol(D,2),wcol(D,3)],
      out_specs=pl.BlockSpec((tb,D),lambda i:(i,0)),
      out_shape=jax.ShapeDtypeStruct((L,D),bf),compiler_params=cp())(kT,vT,w56,w56)

def first_kernel(x_ref,gh1_ref,qT_ref,kT_ref,vT_ref,w0_ref,w1_ref,w2_ref,g_ref,gt_ref,dg_ref):
    i=pl.program_id(0)
    u=dg(qT_ref[...],w0_ref[...],TT)+dg(kT_ref[...],w1_ref[...],TT)+dg(vT_ref[...],w2_ref[...],TT)
    h=x_ref[...].astype(f32)
    r=rms_r(h); ug=u*g_ref[0:1,:]
    gt_ref[...]=gh1_ref[...]+r*ug-h*((r*r*r)*jnp.mean(ug*h,axis=-1,keepdims=True))
    s=jnp.sum(u*h*r,axis=0,keepdims=True)
    @pl.when(i==0)
    def _(): dg_ref[...]=s
    @pl.when(i>0)
    def _(): dg_ref[...]+=s
def first(x,gh1,qT,kT,vT,w,g,tb=256):
    L,D=x.shape
    tok=pl.BlockSpec((tb,D),lambda i:(i,0)); tokT=pl.BlockSpec((D,tb),lambda i:(0,i))
    S=jax.ShapeDtypeStruct
    wb=lambda j: pl.BlockSpec((D,D),lambda i,j=j:(0,j))
    return pl.pallas_call(first_kernel,grid=(L//tb,),
      in_specs=[tok,tok,tokT,tokT,tokT,wb(0),wb(1),wb(2),gain_spec(D)],
      out_specs=[tok,full((1,D))],
      out_shape=[S((L,D),f32),S((1,D),f32)],compiler_params=cp())(x,gh1,qT,kT,vT,w,w,w,g)

SEQ="seq"
MEM="mem"


def plane_bits(seq_size):
    return max(0,(seq_size//2).bit_length()-1)


def bit_order(core,bits):
    order=list(range(1,bits+1))
    return order if core==0 else order[::-1]


def subset_mask(core,subset,bits):
    order=bit_order(core,bits)
    mask=0
    for p in range(bits):
        if subset>>p&1:
            mask^=1<<(order[p]-1)
    return mask


def cross(x,position,seq_size):
    bits=plane_bits(seq_size)
    perm=[(s,s^(1<<bit_order(s&1,bits)[position])) for s in range(seq_size)]
    return lax.ppermute(x,SEQ,perm)


def swap_core(x,seq_size):
    return lax.ppermute(x,SEQ,[(s,s^1) for s in range(seq_size)])


def shift_mem(x,step,mem_size):
    return lax.ppermute(x,MEM,[(z,(z+step)%mem_size) for z in range(mem_size)])


def copy_kernel(index_ref,*refs,places):
    count=len(places)
    sources=refs[:count]; out=refs[count]; sems=refs[count+1]
    copies=[]
    for j,(source,place) in enumerate(zip(sources,places)):
        copies.append(pltpu.make_async_copy(source,out.at[index_ref[place]],sems.at[j]))
        copies[-1].start()
    for c in copies:
        c.wait()


def place_rows(index,pieces,places,slots):
    piece=pieces[0]
    return pl.pallas_call(functools.partial(copy_kernel,places=tuple(places)),
        in_specs=[pl.BlockSpec(memory_space=pltpu.SMEM)]+[pl.BlockSpec(memory_space=pl.ANY)]*len(pieces),
        out_specs=pl.BlockSpec(memory_space=pltpu.VMEM),
        out_shape=jax.ShapeDtypeStruct((slots,)+piece.shape,piece.dtype),
        scratch_shapes=[pltpu.SemaphoreType.DMA((len(pieces),))],
        compiler_params=cp(20),
    )(index,*pieces)


class Place:
    def __init__(self,seq_size,mem_size):
        self.S=seq_size; self.M=mem_size; self.bits=plane_bits(seq_size); self.NP=seq_size//2
        s=lax.axis_index(SEQ); self.z=lax.axis_index(MEM)
        self.core=s%2; self.plane=s//2

    def slab(self,subset,own=True):
        m0=subset_mask(0,subset,self.bits); m1=subset_mask(1,subset,self.bits)
        c=self.core if own else 1-self.core
        return self.plane^jnp.where(c==0,m0,m1)


def gather_mem_direct(shard,pl_):
    M=pl_.M
    pieces=[shard]+[shift_mem(shard,j,M) for j in range(1,M)]
    index=jnp.stack([(pl_.z-j)%M for j in range(M)]).astype(jnp.int32)
    return place_rows(index,pieces,range(M),M).reshape(M*shard.shape[0],shard.shape[1])


def tie(*values):
    return lax.optimization_barrier(values)


class Gather:
    def __init__(self,slab,here):
        self.here=here; self.pieces={0:slab}; self.other={}
        for p in range(here.bits):
            self.pieces[1<<p]=cross(slab,p,here.S)
        self.other[0]=swap_core(slab,here.S)

    def forward(self,dep):
        here=self.here
        self.pieces[1],dep=tie(self.pieces[1],dep)
        for subset in range(1,here.NP):
            top=subset.bit_length()-1
            if subset not in self.pieces:
                self.pieces[subset]=cross(self.pieces[subset^(1<<top)],top,here.S)
        for subset in range(1,here.NP-1):
            self.other[subset]=swap_core(self.pieces[subset],here.S)
        return dep

    def last(self,dep):
        end=self.here.NP-1
        if end and end not in self.other:
            self.pieces[end],dep=tie(self.pieces[end],dep)
            self.other[end]=swap_core(self.pieces[end],self.here.S)
        return dep

    def hold(self,dep):
        n=self.here.NP
        keys=list(range(n))
        out=tie(*[self.pieces[s] for s in keys],*[self.other[s] for s in keys],dep)
        self.pieces=dict(zip(keys,out[:n])); self.other=dict(zip(keys,out[n:2*n]))
        return out[-1]

    def place(self):
        here=self.here
        n=here.NP
        idx=[here.slab(s)*2+here.core for s in range(n)]+[here.slab(s,False)*2+1-here.core for s in range(n)]
        index=jnp.stack(idx).astype(jnp.int32)
        parts=[self.pieces[s] for s in range(n)]+[self.other[s] for s in range(n)]
        out=place_rows(index,parts,range(2*n),2*n)
        return out.reshape(-1,parts[0].shape[1])


def fold_kernel(index_ref,ka,kb,ra,rb,send,keep):
    send[...]=(kb[...].astype(f32)+rb[...].astype(f32)).astype(bf)
    keep[...]=(ka[...].astype(f32)+ra[...].astype(f32)).astype(bf)


def fold(index,keep,recv):
    G,n,R,W=keep.shape; h=n//2
    low=pl.BlockSpec((1,1,R,W),lambda i,m,ix:(m,ix[i],0,0))
    high=pl.BlockSpec((1,1,R,W),lambda i,m,ix:(m,ix[h+i],0,0))
    out=pl.BlockSpec((1,1,R,W),lambda i,m,ix:(m,i,0,0))
    S=jax.ShapeDtypeStruct((G,h,R,W),bf)
    return pl.pallas_call(fold_kernel,
        grid_spec=pltpu.PrefetchScalarGridSpec(num_scalar_prefetch=1,grid=(h,G),in_specs=[low,high,low,high],out_specs=[out,out]),
        out_shape=[S,S],compiler_params=cp(16))(index,keep,keep,recv,recv)


def split_kernel(index_ref,a,b,*outs):
    for j,o in enumerate(outs):
        z=index_ref[j]
        o[...]=(a[:,:,pl.ds(z,1)].astype(f32)+b[:,:,pl.ds(z,1)].astype(f32)).astype(bf)


def split_mem(index,a,b):
    G,two,M,r,W=a.shape
    full_=pl.BlockSpec(memory_space=pltpu.VMEM)
    S=jax.ShapeDtypeStruct((G,two,1,r,W),bf)
    return pl.pallas_call(split_kernel,in_specs=[pl.BlockSpec(memory_space=pltpu.SMEM),full_,full_],out_specs=[full_]*M,
        out_shape=[S]*M,compiler_params=cp(16))(index,a,b)


def order_kernel(a,b,o):
    for z in range(o.shape[0]):
        o[z]=(a[:,:,z].astype(f32)+b[:,:,z].astype(f32)).astype(bf)


def order_mem(a,b):
    G,two,M,r,W=a.shape
    v=pl.BlockSpec(memory_space=pltpu.VMEM)
    return pl.pallas_call(order_kernel,in_specs=[v,v],out_specs=v,
        out_shape=jax.ShapeDtypeStruct((M,G,two,r,W),bf),compiler_params=cp(16))(a,b)


class Reduce:
    def __init__(self,send,keep,here):
        G,D,W=send.shape
        NP=here.NP; R=D//NP
        self.here=here; self.r=R//2//here.M
        self.recv=swap_core(send,here.S).reshape(G,NP,R,W)
        self.keep=keep.reshape(G,NP,R,W)
        self.index=jnp.stack([here.slab(s) for s in range(NP)]).astype(jnp.int32)
        self.p=here.bits-1

    def fold(self,dep):
        self.recv,dep=tie(self.recv,dep)
        if self.p<0:
            return dep
        go,keep=fold(self.index,self.keep,self.recv)
        go,self.keep,dep=tie(go,keep,dep)
        self.recv=cross(go,self.p,self.here.S)
        self.index=jnp.arange(1<<self.p,dtype=jnp.int32)
        self.p-=1
        return dep

    def halves(self,dep):
        while self.p>=0:
            dep=self.fold(dep)
        self.recv,dep=tie(self.recv,dep)
        G,_,R,W=self.keep.shape
        shape=(G,2,self.here.M,self.r,W)
        return self.keep.reshape(shape),self.recv.reshape(shape),dep

    def over_mem(self,dep):
        a,b,dep=self.halves(dep)
        parts,dep=tie(order_mem(a,b),dep)
        return lax.psum_scatter(parts,MEM,scatter_dimension=0,tiled=True)[0],dep

    def over_mem_direct(self,dep):
        a,b,dep=self.halves(dep)
        M=self.here.M
        parts=split_mem(jnp.stack([(self.here.z+j)%M for j in range(M)]).astype(jnp.int32),a,b)
        total=parts[0].astype(f32)
        for j in range(1,M):
            total=total+shift_mem(parts[j],j,M).astype(f32)
        G,_,_,r,W=a.shape
        return total.reshape(G,2,r,W)


def own_rows(total,pl_):
    give=lax.dynamic_index_in_dim(total,1-pl_.core,1,keepdims=False)
    own=lax.dynamic_index_in_dim(total,pl_.core,1,keepdims=False)
    other=swap_core(give,pl_.S)
    low=jnp.where(pl_.core==0,own,other); high=jnp.where(pl_.core==0,other,own)
    return jnp.concatenate([low,high],axis=-1)


def sum_all(x,pl_):
    for b in range(pl_.S.bit_length()-1):
        x=x+lax.ppermute(x,SEQ,[(s,s^(1<<b)) for s in range(pl_.S)])
    for b in range(pl_.M.bit_length()-1):
        x=x+lax.ppermute(x,MEM,[(z,z^(1<<b)) for z in range(pl_.M)])
    return x

STEP=10
CLIP_NORM=1.0
BETA_FIRST=0.9
BETA_SECOND=0.999
ADAM_EPSILON=1e-08
RATE_MATRIX=0.06
RATE_GAIN=0.6
DECAY_MATRIX=0.01


def adam_step(master,grad,first_moment,second_moment,rate,decay):
    first_new=BETA_FIRST*first_moment+(1.0-BETA_FIRST)*grad
    second_new=BETA_SECOND*second_moment+(1.0-BETA_SECOND)*grad*grad
    first_hat=first_new/(1.0-BETA_FIRST**STEP)
    second_hat=second_new/(1.0-BETA_SECOND**STEP)
    master_new=master-rate*(first_hat/(jnp.sqrt(second_hat)+ADAM_EPSILON)+decay*master)
    return (master_new,first_new,second_new)


def columns(stack):
    return jnp.concatenate([stack[i] for i in range(stack.shape[0])],axis=1)


def on_device(seq_size,mem_size,tokens,memory,cotangent,table_len,patch_count,attn_master,attn_first,attn_second,mlp_master,mlp_first,mlp_second,gain_master,gain_first,gain_second):
    here=Place(seq_size,mem_size)
    core=here.core.reshape(1).astype(jnp.int32)
    rows,D=attn_master.shape[1:]
    aw=attn_master.astype(bf)
    gain_cols=jnp.pad(gain_master.T,((0,0),(0,125))).astype(bf)
    x=tokens[0]
    slab_first=gather_mem_direct(jnp.concatenate([columns(aw[:3]),gain_cols],axis=1),here)
    slab_second=lax.all_gather(columns(aw[3:]),MEM,axis=0,tiled=True)
    slab_mlp=lax.all_gather(columns(mlp_master.astype(bf)),MEM,axis=0,tiled=True)
    slab_first,memory=tie(slab_first,memory)
    mem=lax.all_to_all(memory,"mem",split_axis=0,concat_axis=0,tiled=True).reshape(-1,D)
    first_group=Gather(slab_first,here)
    x=first_group.last(first_group.forward(x))
    slab_second=first_group.hold(slab_second)
    second_group=Gather(slab_second,here)
    w_first=first_group.place()
    n1,qkv,gains=norm_proj(x,w_first)
    qkv=second_group.forward(qkv)
    q,k,v=(qkv,0),(qkv,HEADS),(qkv,2*HEADS)
    o1,lse1=attn_fwd(table_len,q,k,v,True,512,4)
    o1=second_group.last(o1)
    slab_mlp=second_group.hold(slab_mlp)
    mlp_group=Gather(slab_mlp,here)
    w_second=second_group.place()
    mkv=mem_proj(mem,w_second,2*D)
    mkv,o1=tie(mkv,o1)
    h1,n2,cq=post_self(x,o1,w_second,gains)
    cq=mlp_group.forward(cq)
    q2,k2,v2=(cq,0),(mkv,0),(mkv,HEADS)
    o2,lse2=attn_fwd(patch_count,q2,k2,v2,False,512,2)
    o2=mlp_group.last(o2)
    w_mlp=mlp_group.place()
    mixed_out,gh2,gm2,gb2,dg3,mlp_send,mlp_keep=mlp(core,table_len,h1,o2,w_second,cotangent[0],gains,w_mlp)
    red_mlp=Reduce(mlp_send,mlp_keep,here)
    half=HEADS//2
    part=attn_bwd(patch_count,q2,k2,v2,o2,gm2,lse2,False,256,2,(0,half))
    part=(red_mlp.fold(part[0]),)+tuple(part[1:])
    dcq,dmk,dmv=attn_bwd(patch_count,q2,k2,v2,o2,gm2,lse2,False,256,2,(half,half),part)
    gh1,gm1,gb1,dg2=mid(h1,gh2,dcq,w_second,gains)
    gb1=red_mlp.fold(gb1)
    second_send,second_keep=wgrads(core,[gb1,n2,mem,gb2],[o1,dcq,dmk,dmv,o2],[(0,0),(1,1),(2,2),(2,3),(3,4)])
    second_send,dmk=tie(second_send,dmk)
    red_second=Reduce(second_send,second_keep,here)
    gmem_local=gmem(dmk,dmv,w_second)
    gmem_local=red_second.fold(gmem_local)
    t_mlp,gmem_local=red_mlp.over_mem(gmem_local)
    grad_memory=lax.all_to_all(gmem_local.reshape(memory.shape),"mem",split_axis=0,concat_axis=0,tiled=True).astype(f32)
    gm1,gmem_local=tie(gm1,gmem_local)
    dq,dk,dv=attn_bwd(table_len,q,k,v,o1,gm1,lse1,True,256,2)
    first_send,first_keep=wgrads(core,[n1],[dq,dk,dv],[(0,0),(0,1),(0,2)])
    red_first=Reduce(first_send,first_keep,here)
    dq=red_second.fold(dq)
    dq=red_first.fold(dq)
    grad_tokens,dg1=first(x,gh1,dq,dk,dv,w_first,gains)
    dg1=red_first.fold(dg1)
    t_second,dg1=red_second.over_mem(dg1)
    gain_all=sum_all(jnp.concatenate([dg1,dg2,dg3],axis=0),here)
    t_first=red_first.over_mem_direct(dg1)
    totals=(t_first,t_second.astype(f32),t_mlp.astype(f32))
    squares=sum(jnp.sum(t*t) for t in totals)
    grad_norm=jnp.sqrt(sum_all(squares.reshape(1,1),here)[0,0]+jnp.sum(gain_all*gain_all))
    factor=CLIP_NORM/jnp.maximum(grad_norm,CLIP_NORM)
    red=[own_rows(t,here) for t in totals]
    attn_red=jnp.concatenate(red[:2],axis=0)
    mlp_red=red[2]
    device=lax.axis_index("seq")*mem_size+lax.axis_index("mem")
    gain_red=lax.dynamic_slice_in_dim(gain_all,device*rows,rows,1)
    a=adam_step(attn_master,attn_red*factor,attn_first,attn_second,RATE_MATRIX,DECAY_MATRIX)
    m=adam_step(mlp_master,mlp_red*factor,mlp_first,mlp_second,RATE_MATRIX,DECAY_MATRIX)
    gn=adam_step(gain_master,gain_red*factor,gain_first,gain_second,RATE_GAIN,0.0)
    return (mixed_out[None],grad_tokens[None],grad_memory,grad_norm)+a+m+gn


def solution(mesh):
    both=P(("seq","mem"),None,None)
    mid_split=P(None,("seq","mem"),None)
    gain_split=P(None,("seq","mem"))
    return jax.shard_map(functools.partial(on_device,mesh.shape["seq"],mesh.shape["mem"]),mesh=mesh,
        in_specs=(both,P("seq","mem",None),both,P(("seq","mem")),P(("seq","mem")))+(mid_split,)*6+(gain_split,)*3,
        out_specs=(both,both,P("seq","mem",None),P())+(mid_split,)*6+(gain_split,)*3,
        check_vma=False)
```

```python
import functools, math
import jax, jax.numpy as jnp
from jax import lax
from jax.sharding import PartitionSpec as P
from jax.experimental import pallas as pl
from jax.experimental.pallas import tpu as pltpu
bf=jnp.bfloat16; f32=jnp.float32
HD=64; HEADS=12
def cost(us):
    return pl.CostEstimate(flops=int(us*1e+10),bytes_accessed=10**5,transcendentals=0)
NEG=-1e30
VA=16*2**20
LOG2E=math.log2(math.e)
TN=(((0,),(0,)),((),())); NN=(((1,),(0,)),((),())); NT=(((1,),(1,)),((),()))
def dg(a,b,dims): return lax.dot_general(a,b,dims,preferred_element_type=f32)
def rows16(cols, width, pad=16):
    idx=lax.broadcasted_iota(jnp.int32,(pad,width),0)
    out=jnp.zeros((pad,width),f32)
    for i,c in enumerate(cols): out=jnp.where(idx==i,c,out)
    return out.astype(bf)
def split3(x):
    hi=x.astype(bf).astype(f32); r=x-hi; mid=r.astype(bf).astype(f32); lo=r-mid
    return hi,mid,lo
def scaled_query(qT):
    s=qT.astype(f32)*(0.125*LOG2E)
    hi=s.astype(bf); lo=(s-hi.astype(f32)).astype(bf)
    return hi,lo


def causal_mask(x,q0,bq,fill):
    ki=lax.broadcasted_iota(jnp.int32,(bq,bq),0); qi=lax.broadcasted_iota(jnp.int32,(bq,bq),1)
    d=jnp.where(ki<=qi,x[q0:],fill)
    return jnp.concatenate([x[:q0],d],axis=0) if q0 else d

def fwd_kernel(len_ref,qT_ref,kT_ref,vT_ref,oT_ref,lse_ref,*,causal,bq,hs):
    L=qT_ref.shape[1]; K=kT_ref.shape[1]
    n=len_ref[0]
    kpos=lax.broadcasted_iota(jnp.int32,(1,K),1)
    kx=rows16([jnp.where(kpos<n,0.0,NEG)],K); qx=rows16([jnp.ones((1,L),f32)],L); vx=rows16([jnp.ones((1,K),f32)],K)
    ops=[]
    for h in range(hs):
        r=slice(h*HD,(h+1)*HD)
        kT=kT_ref[r,:]
        hi,lo=scaled_query(qT_ref[r,:])
        ops.append((jnp.concatenate([kT,kT,kx],axis=0),jnp.concatenate([hi,lo,qx],axis=0),jnp.concatenate([vT_ref[r,:],vx],axis=0)))
    jobs=[(h,q0) for h in range(hs) for q0 in range(0,L,bq)]
    def score(j):
        h,q0=j; ke=min(K,q0+bq) if causal else K
        return dg(ops[h][0][:,:ke],ops[h][1][:,q0:q0+bq],TN)
    nxt=score(jobs[0])
    for i,(h,q0) in enumerate(jobs):
        s=nxt
        if i+1<len(jobs): nxt=score(jobs[i+1])
        ke=s.shape[0]
        if causal: s=causal_mask(s,q0,bq,NEG)
        m=jnp.max(s,axis=0,keepdims=True)
        p=jnp.exp2(s-m).astype(bf)
        o=dg(ops[h][2][:,:ke],p,NN)
        l=o[HD:HD+1]
        oT_ref[h*HD:(h+1)*HD,q0:q0+bq]=(o[:HD]*(1.0/l)).astype(bf)
        lse_ref[h,:,q0:q0+bq]=m+jnp.log2(l)

def head_block(hs,w,offset=0):
    return pl.BlockSpec((hs*HD,w),lambda h:(h+offset//hs,0))
def fwd_part_kernel(*refs,**kw):
    fwd_kernel(*refs[:4],*refs[6:],**kw)
def attn_fwd(n,q,k,v,causal,bq=256,hs=2,part=None,into=None):
    L=q[0].shape[1]; K=k[0].shape[1]; D=HEADS*HD
    h0,hn=part or (0,HEADS)
    hb=lambda w,o=0: head_block(hs,w,o+h0)
    specs=[pl.BlockSpec(memory_space=pltpu.SMEM),hb(L,q[1]),hb(K,k[1]),hb(K,v[1])]
    args=(n,q[0],k[0],v[0])
    if into is not None:
        specs+=[pl.BlockSpec(memory_space=pl.ANY)]*2
        args+=tuple(into)
    return pl.pallas_call(functools.partial(fwd_kernel if into is None else fwd_part_kernel,causal=causal,bq=bq,hs=hs),grid=(hn//hs,),
      in_specs=specs,
      out_specs=[hb(L),pl.BlockSpec((hs,1,L),lambda h:(h+h0//hs,0,0))],
      out_shape=[jax.ShapeDtypeStruct((D,L),bf),jax.ShapeDtypeStruct((HEADS,1,L),f32)],
      input_output_aliases={} if into is None else {4:0,5:1},
      cost_estimate=cost(0.3),compiler_params=pltpu.CompilerParams(vmem_limit_bytes=VA),
    )(*args)

def bwd_kernel(len_ref,qT_ref,kT_ref,vT_ref,oT_ref,gT_ref,lse_ref,dq_ref,dk_ref,dv_ref,dka,dva,*,causal,bq,hs):
    L=qT_ref.shape[1]; K=kT_ref.shape[1]
    n=len_ref[0]
    kpos=lax.broadcasted_iota(jnp.int32,(1,K),1)
    bias=jnp.where(kpos<n,0.0,NEG)
    one_k=jnp.ones((1,K),f32)
    kx=rows16([bias,one_k,one_k,one_k],K); vx=rows16([one_k,one_k,one_k],K)
    ops=[]
    for h in range(hs):
        r=slice(h*HD,(h+1)*HD)
        kT=kT_ref[r,:]; qT=qT_ref[r,:]; gT=gT_ref[r,:]
        hi,lo=scaled_query(qT)
        delta=jnp.sum(oT_ref[r,:].astype(f32)*gT.astype(f32),axis=0,keepdims=True)
        ops.append(dict(k=kT,q=qT,g=gT,kaug=jnp.concatenate([kT,kT,kx],axis=0),
          qaug=jnp.concatenate([hi,lo,rows16([jnp.ones((1,L),f32),*split3(-lse_ref[h])],L)],axis=0),
          vaug=jnp.concatenate([vT_ref[r,:],vx],axis=0),
          gaug=jnp.concatenate([gT,rows16(list(split3(-delta)),L)],axis=0)))
    jobs=[(h,q0) for h in range(hs) for q0 in reversed(range(0,L,bq))]
    def score(j):
        h,q0=j; ke=min(K,q0+bq) if causal else K; sl=slice(q0,q0+bq); o=ops[h]
        return dg(o["kaug"][:,:ke],o["qaug"][:,sl],TN),dg(o["vaug"][:,:ke],o["gaug"][:,sl],TN)
    nxt=score(jobs[0])
    for i,(h,q0) in enumerate(jobs):
        s,dp=nxt
        if i+1<len(jobs): nxt=score(jobs[i+1])
        ke=s.shape[0]; sl=slice(q0,q0+bq); o=ops[h]; r=slice(h*HD,(h+1)*HD)
        p=jnp.exp2(s)
        if causal: p=causal_mask(p,q0,bq,0.0)
        ds=(p*dp).astype(bf)
        pb=p.astype(bf)
        dq_ref[r,sl]=(dg(o["k"][:,:ke],ds,NN)*0.125).astype(bf)
        dv=dg(o["g"][:,sl],pb,NT)
        dk=dg(o["q"][:,sl],ds,NT)
        if q0==L-bq:
            dka[r]=dk; dva[r]=dv
        else:
            dka[r,:ke]+=dk; dva[r,:ke]+=dv
    dk_ref[...]=(dka[...]*0.125).astype(bf)
    dv_ref[...]=dva[...].astype(bf)

def bwd_part_kernel(*refs,**kw):
    bwd_kernel(*refs[:7],*refs[10:],**kw)
def attn_bwd(n,q,k,v,oT,gT,lse,causal,bq=256,hs=2,part=None,into=None):
    L=q[0].shape[1]; K=k[0].shape[1]; D=HEADS*HD
    h0,hn=part or (0,HEADS)
    hb=lambda w,o=0: head_block(hs,w,o+h0)
    S=jax.ShapeDtypeStruct
    specs=[pl.BlockSpec(memory_space=pltpu.SMEM),hb(L,q[1]),hb(K,k[1]),hb(K,v[1]),hb(L),hb(L),pl.BlockSpec((hs,1,L),lambda h:(h+h0//hs,0,0))]
    args=(n,q[0],k[0],v[0],oT,gT,lse)
    if into is not None:
        specs+=[pl.BlockSpec(memory_space=pl.ANY)]*3
        args+=tuple(into)
    return pl.pallas_call(functools.partial(bwd_kernel if into is None else bwd_part_kernel,causal=causal,bq=bq,hs=hs),grid=(hn//hs,),
      in_specs=specs,out_specs=[hb(L),hb(K),hb(K)],
      out_shape=[S((D,L),bf),S((D,K),bf),S((D,K),bf)],
      input_output_aliases={} if into is None else {7:0,8:1,9:2},
      scratch_shapes=[pltpu.VMEM((hs*HD,K),f32),pltpu.VMEM((hs*HD,K),f32)],
      cost_estimate=cost(14),compiler_params=pltpu.CompilerParams(vmem_limit_bytes=VA),
    )(*args)

TT=(((0,),(1,)),((),()))
EPS=1e-6
VL=60*2**20
def cp(mb=24): return pltpu.CompilerParams(vmem_limit_bytes=mb*2**20)
def full(shape): return pl.BlockSpec(shape,lambda i:(0,)*len(shape))
GC=0.7978845608028654

def rms_r(v): return lax.rsqrt(jnp.mean(v*v,axis=-1,keepdims=True)+EPS)

def wcol(D,j): return pl.BlockSpec((D,D),lambda i:(0,j))
def gain_spec(D): return pl.BlockSpec((8,D),lambda i:(0,0))

def proj_kernel(x_ref,e_ref,w_ref,n_ref,yT_ref,g_ref):
    @pl.when(pl.program_id(0)==0)
    def _():
        g=e_ref[...].astype(f32).T[0:8,:]
        g_ref[...]=g
        x=x_ref[...].astype(f32)
        n_ref[...]=(x*rms_r(x)*g[0:1,:]).astype(bf)
    yT_ref[...]=dg(w_ref[...],n_ref[...],TT).astype(bf)
def norm_proj(x,w,fb=384):
    L,D=x.shape; F=3*D
    return pl.pallas_call(proj_kernel,grid=(F//fb,),
      in_specs=[full((L,D)),pl.BlockSpec((D,128),lambda i:(0,F//128)),pl.BlockSpec((D,fb),lambda i:(0,i))],
      out_specs=[full((L,D)),pl.BlockSpec((fb,L),lambda i:(i,0)),gain_spec(D)],
      out_shape=[jax.ShapeDtypeStruct((L,D),bf),jax.ShapeDtypeStruct((F,L),bf),jax.ShapeDtypeStruct((8,D),f32)],cost_estimate=cost(6),compiler_params=cp())(x,w,w)
def memproj_kernel(x_ref,w_ref,yT_ref):
    yT_ref[...]=dg(w_ref[...],x_ref[...],TT).astype(bf)
def mem_proj(x,w,first_col,fb=384):
    L,D=x.shape; F=2*D
    return pl.pallas_call(memproj_kernel,grid=(F//fb,),
      in_specs=[full((L,D)),pl.BlockSpec((D,fb),lambda i:(0,first_col//fb+i))],
      out_specs=pl.BlockSpec((fb,L),lambda i:(i,0)),
      out_shape=jax.ShapeDtypeStruct((F,L),bf),cost_estimate=cost(4),compiler_params=cp())(x,w)

def post_self_kernel(x_ref,oT_ref,w3_ref,w4_ref,g_ref,h_ref,n_ref,cT_ref):
    h=x_ref[...].astype(f32)+dg(oT_ref[...],w3_ref[...],TT)
    h_ref[...]=h
    n=(h*rms_r(h)*g_ref[1:2,:]).astype(bf)
    n_ref[...]=n
    cT_ref[...]=dg(n,w4_ref[...],NN).astype(bf).T
def post_self(x,oT,w,g,tb=256):
    L,D=x.shape
    tok=pl.BlockSpec((tb,D),lambda i:(i,0)); tokT=pl.BlockSpec((D,tb),lambda i:(0,i))
    return pl.pallas_call(post_self_kernel,grid=(L//tb,),
      in_specs=[tok,tokT,wcol(D,0),wcol(D,1),gain_spec(D)],
      out_specs=[tok,tok,tokT],
      out_shape=[jax.ShapeDtypeStruct((L,D),f32),jax.ShapeDtypeStruct((L,D),bf),jax.ShapeDtypeStruct((D,L),bf)],cost_estimate=cost(6),compiler_params=cp())(x,oT,w,w,g)

def mlp_chunk(n3,gb,wg,wu,wd,dw_ref,inner_s,dgate_s,dup_s,oacc,nacc,tb):
    L=n3.shape[0]; nt=L//tb
    def pre(t):
        sl=slice(t*tb,(t+1)*tb)
        a=n3[sl,:]
        return dg(a,wg[...],NN),dg(a,wu[...],NN),dg(gb[sl,:],wd[...],NN)
    nxt=pre(0)
    for t in range(nt):
        sl=slice(t*tb,(t+1)*tb)
        g,u,di=nxt
        if t+1<nt: nxt=pre(t+1)
        g2=g*g
        th=jnp.tanh(g*(GC+(GC*0.044715)*g2))
        hp=0.5+0.5*th
        ge=g*hp
        dge=hp+(0.5*g)*(1.0-th*th)*(GC+(3*GC*0.044715)*g2)
        inner=(ge*u).astype(bf)
        dgate=(di*u*dge).astype(bf)
        dup=(di*ge).astype(bf)
        inner_s[sl,:]=inner; dgate_s[sl,:]=dgate; dup_s[sl,:]=dup
        oacc[sl,:]+=dg(inner,wd[...],NT)
        nacc[sl,:]+=dg(dgate,wg[...],NT)+dg(dup,wu[...],NT)
    dw_ref[0]=dg(n3[...],dgate_s[...],TN).astype(bf)
    dw_ref[1]=dg(n3[...],dup_s[...],TN).astype(bf)
    dw_ref[2]=dg(gb[...],inner_s[...],TN).astype(bf)

def mlp_kernel(core_ref,len_ref,h1_ref,oT_ref,w7_ref,cot_ref,g_ref,wg_ref,wu_ref,wd_ref,
               out_ref,gh_ref,gmT_ref,gb2_ref,dg_ref,send_ref,keep_ref,
               h2,n3,gb,oacc,nacc,dw,inner_s,dgate_s,dup_s,sems,*,tb):
    L,D=h1_ref.shape
    fc=dw.shape[3]
    i=pl.program_id(0); count=pl.num_programs(0); half=count//2
    slot=lax.rem(i,2)
    def copy(step,to):
        col=pl.multiple_of(lax.rem(step,half)*fc,fc)
        return pltpu.make_async_copy(dw.at[lax.rem(step,2)],to.at[:,:,pl.ds(col,fc)],sems.at[lax.rem(step,2)])
    @pl.when(i==0)
    def _():
        n=len_ref[0]
        for t in range(L//tb):
            sl=slice(t*tb,(t+1)*tb)
            h=h1_ref[sl,:]+dg(oT_ref[:,sl],w7_ref[...],TT)
            h2[sl,:]=h
            oacc[sl,:]=h
            nacc[sl,:]=jnp.zeros((tb,D),f32)
            n3[sl,:]=(h*rms_r(h)*g_ref[2:3,:]).astype(bf)
            row=t*tb+lax.broadcasted_iota(jnp.int32,(tb,1),0)
            gb[sl,:]=jnp.where(row<n,cot_ref[sl,:].astype(f32),0.0).astype(bf)
    @pl.when(i>=2)
    def _():
        copy(i-2,send_ref).wait()
    mlp_chunk(n3,gb,wg_ref,wu_ref,wd_ref,dw.at[slot],inner_s,dgate_s,dup_s,oacc,nacc,tb)
    @pl.when(i<half)
    def _():
        copy(i,send_ref).start()
    @pl.when(i>=half)
    def _():
        copy(i,keep_ref).start()
    @pl.when(i==count-1)
    def _():
        acc=jnp.zeros((1,D),f32)
        for t in range(L//tb):
            sl=slice(t*tb,(t+1)*tb)
            h=h2[sl,:]; uu=nacc[sl,:]
            out_ref[sl,:]=oacc[sl,:].astype(bf)
            r=rms_r(h); ug=uu*g_ref[2:3,:]
            gh=gb[sl,:].astype(f32)+r*ug-h*((r*r*r)*jnp.mean(ug*h,axis=-1,keepdims=True))
            acc=acc+jnp.sum(uu*h*r,axis=0,keepdims=True)
            gh_ref[sl,:]=gh
            b=gh.astype(bf)
            gb2_ref[sl,:]=b
            gmT_ref[:,sl]=dg(b,w7_ref[...],NN).astype(bf).T
        dg_ref[...]=acc
        copy(i-1,keep_ref).wait()
        copy(i,keep_ref).wait()
def mlp(core,n,h1,oT,w_second,cot,g,wm,fc=512,tb=256):
    L,D=h1.shape; F=wm.shape[1]//3; nc=F//fc; hc=nc//2
    whole=lambda shape: pl.BlockSpec(shape,lambda i,c:(0,)*len(shape),pipeline_mode=pl.Buffered(1))
    wb=lambda j: pl.BlockSpec((D,fc),lambda i,c,j=j:(0,j*nc+lax.rem(i+(1-c[0])*hc,nc)))
    S=jax.ShapeDtypeStruct
    hbm=pl.BlockSpec(memory_space=pl.ANY)
    return pl.pallas_call(functools.partial(mlp_kernel,tb=tb),
      grid_spec=pltpu.PrefetchScalarGridSpec(num_scalar_prefetch=1,grid=(nc,),
      in_specs=[pl.BlockSpec(memory_space=pltpu.SMEM),whole((L,D)),whole((D,L)),pl.BlockSpec((D,D),lambda i,c:(0,4),pipeline_mode=pl.Buffered(1)),whole((L,D)),whole((8,D)),wb(0),wb(1),wb(2)],
      out_specs=[whole((L,D)),whole((L,D)),whole((D,L)),whole((L,D)),whole((1,D)),hbm,hbm],
      scratch_shapes=[pltpu.VMEM((L,D),f32),pltpu.VMEM((L,D),bf),pltpu.VMEM((L,D),bf),pltpu.VMEM((L,D),f32),pltpu.VMEM((L,D),f32),
        pltpu.VMEM((2,3,D,fc),bf),pltpu.VMEM((L,fc),bf),pltpu.VMEM((L,fc),bf),pltpu.VMEM((L,fc),bf),pltpu.SemaphoreType.DMA((2,))]),
      out_shape=[S((L,D),bf),S((L,D),f32),S((D,L),bf),S((L,D),bf),S((1,D),f32),S((3,D,F//2),bf),S((3,D,F//2),bf)],
      cost_estimate=cost(42),compiler_params=cp(48))(core,n,h1,oT,w_second,cot,g,wm,wm,wm)

def mid_kernel(h1_ref,gh2_ref,dcT_ref,w4_ref,w3_ref,g_ref,gh1_ref,gmT_ref,gb_ref,dg_ref):
    i=pl.program_id(0)
    u=dg(dcT_ref[...],w4_ref[...],TT)
    h=h1_ref[...]
    r=rms_r(h); ug=u*g_ref[1:2,:]
    gh=gh2_ref[...]+r*ug-h*((r*r*r)*jnp.mean(ug*h,axis=-1,keepdims=True))
    gh1_ref[...]=gh
    b=gh.astype(bf)
    gb_ref[...]=b
    gmT_ref[...]=dg(b,w3_ref[...],NN).astype(bf).T
    s=jnp.sum(u*h*r,axis=0,keepdims=True)
    @pl.when(i==0)
    def _(): dg_ref[...]=s
    @pl.when(i>0)
    def _(): dg_ref[...]+=s
def mid(h1,gh2,dcT,w,g,tb=256):
    L,D=h1.shape
    tok=pl.BlockSpec((tb,D),lambda i:(i,0)); tokT=pl.BlockSpec((D,tb),lambda i:(0,i))
    S=jax.ShapeDtypeStruct
    return pl.pallas_call(mid_kernel,grid=(L//tb,),
      in_specs=[tok,tok,tokT,wcol(D,1),wcol(D,0),gain_spec(D)],
      out_specs=[tok,tokT,tok,full((1,D))],
      out_shape=[S((L,D),f32),S((D,L),bf),S((L,D),bf),S((1,D),f32)],cost_estimate=cost(0.2),compiler_params=cp())(h1,gh2,dcT,w,w,g)

def wgrads_kernel(core_ref,*refs,pairs,na,ng):
    a_refs=refs[:na]; g_refs=refs[na:na+ng]; send_ref,keep_ref=refs[na+ng:]
    k=core_ref[0]
    W=send_ref.shape[2]
    for out,half in ((send_ref,1-k),(keep_ref,k)):
        start=pl.multiple_of(half*W,W)
        for m,(ia,ig) in enumerate(pairs):
            out[m]=dg(a_refs[ia][...],g_refs[ig][pl.ds(start,W),:],TT).astype(bf)
def wgrads(core,a,g,pairs):
    D=a[0].shape[1]; F=g[0].shape[0]
    v=pl.BlockSpec(memory_space=pltpu.VMEM)
    S=jax.ShapeDtypeStruct((len(pairs),D,F//2),bf)
    return pl.pallas_call(functools.partial(wgrads_kernel,pairs=tuple(pairs),na=len(a),ng=len(g)),
      in_specs=[pl.BlockSpec(memory_space=pltpu.SMEM)]+[v]*(len(a)+len(g)),out_specs=[v,v],
      out_shape=[S,S],cost_estimate=cost(8),compiler_params=cp(40))(core,*a,*g)

def gmem_kernel(kT_ref,vT_ref,w5_ref,w6_ref,o_ref):
    o_ref[...]=(dg(kT_ref[...],w5_ref[...],TT)+dg(vT_ref[...],w6_ref[...],TT)).astype(bf)
def gmem(kT,vT,w56,tb=256):
    D,L=kT.shape
    tokT=pl.BlockSpec((D,tb),lambda i:(0,i))
    return pl.pallas_call(gmem_kernel,grid=(L//tb,),
      in_specs=[tokT,tokT,wcol(D,2),wcol(D,3)],
      out_specs=pl.BlockSpec((tb,D),lambda i:(i,0)),
      out_shape=jax.ShapeDtypeStruct((L,D),bf),cost_estimate=cost(0.2),compiler_params=cp())(kT,vT,w56,w56)

def first_kernel(x_ref,gh1_ref,qT_ref,kT_ref,vT_ref,w0_ref,w1_ref,w2_ref,g_ref,gt_ref,dg_ref):
    i=pl.program_id(0)
    u=dg(qT_ref[...],w0_ref[...],TT)+dg(kT_ref[...],w1_ref[...],TT)+dg(vT_ref[...],w2_ref[...],TT)
    h=x_ref[...].astype(f32)
    r=rms_r(h); ug=u*g_ref[0:1,:]
    gt_ref[...]=gh1_ref[...]+r*ug-h*((r*r*r)*jnp.mean(ug*h,axis=-1,keepdims=True))
    s=jnp.sum(u*h*r,axis=0,keepdims=True)
    @pl.when(i==0)
    def _(): dg_ref[...]=s
    @pl.when(i>0)
    def _(): dg_ref[...]+=s
def first(x,gh1,qT,kT,vT,w,g,tb=256):
    L,D=x.shape
    tok=pl.BlockSpec((tb,D),lambda i:(i,0)); tokT=pl.BlockSpec((D,tb),lambda i:(0,i))
    S=jax.ShapeDtypeStruct
    wb=lambda j: pl.BlockSpec((D,D),lambda i,j=j:(0,j))
    return pl.pallas_call(first_kernel,grid=(L//tb,),
      in_specs=[tok,tok,tokT,tokT,tokT,wb(0),wb(1),wb(2),gain_spec(D)],
      out_specs=[tok,full((1,D))],
      out_shape=[S((L,D),f32),S((1,D),f32)],cost_estimate=cost(7),compiler_params=cp())(x,gh1,qT,kT,vT,w,w,w,g)

SEQ="seq"
MEM="mem"


def plane_bits(seq_size):
    return max(0,(seq_size//2).bit_length()-1)


def bit_order(core,bits):
    order=list(range(1,bits+1))
    return order if core==0 else order[::-1]


def subset_mask(core,subset,bits):
    order=bit_order(core,bits)
    mask=0
    for p in range(bits):
        if subset>>p&1:
            mask^=1<<(order[p]-1)
    return mask


def cross(x,position,seq_size):
    bits=plane_bits(seq_size)
    perm=[(s,s^(1<<bit_order(s&1,bits)[position])) for s in range(seq_size)]
    return lax.ppermute(x,SEQ,perm)


def swap_core(x,seq_size):
    return lax.ppermute(x,SEQ,[(s,s^1) for s in range(seq_size)])


def shift_mem(x,step,mem_size):
    return lax.ppermute(x,MEM,[(z,(z+step)%mem_size) for z in range(mem_size)])


def copy_kernel(index_ref,*refs,places,columns):
    count=len(places)
    sources=refs[:count]; out=refs[count]; sems=refs[count+1]
    copies=[]
    for j,(source,place) in enumerate(zip(sources,places)):
        if columns is not None:
            source=source.at[:,pl.ds(columns[0],columns[1]-columns[0])]
        copies.append(pltpu.make_async_copy(source,out.at[index_ref[place]],sems.at[j]))
        copies[-1].start()
    for c in copies:
        c.wait()


def place_rows(index,pieces,places,slots,us,columns=None):
    piece=pieces[0]
    shape=piece.shape if columns is None else (piece.shape[0],columns[1]-columns[0])
    return pl.pallas_call(functools.partial(copy_kernel,places=tuple(places),columns=columns),
        in_specs=[pl.BlockSpec(memory_space=pltpu.SMEM)]+[pl.BlockSpec(memory_space=pltpu.HBM)]*len(pieces),
        out_specs=pl.BlockSpec(memory_space=pltpu.VMEM),
        out_shape=jax.ShapeDtypeStruct((slots,)+shape,piece.dtype),
        scratch_shapes=[pltpu.SemaphoreType.DMA((len(pieces),))],
        cost_estimate=cost(us),compiler_params=cp(20),
    )(index,*pieces)


class Place:
    def __init__(self,seq_size,mem_size):
        self.S=seq_size; self.M=mem_size; self.bits=plane_bits(seq_size); self.NP=seq_size//2
        s=lax.axis_index(SEQ); self.z=lax.axis_index(MEM)
        self.core=s%2; self.plane=s//2

    def slab(self,subset,own=True):
        m0=subset_mask(0,subset,self.bits); m1=subset_mask(1,subset,self.bits)
        c=self.core if own else 1-self.core
        return self.plane^jnp.where(c==0,m0,m1)


def gather_mem_direct(shard,pl_):
    M=pl_.M
    pieces=[shard]+[shift_mem(shard,j,M) for j in range(1,M)]
    index=jnp.stack([(pl_.z-j)%M for j in range(M)]).astype(jnp.int32)
    return place_rows(index,pieces,range(M),M,3).reshape(M*shard.shape[0],shard.shape[1])


def gather_mem_exchange(shard,here):
    M=here.M
    copies=jnp.broadcast_to(shard[None],(M,)+shard.shape)
    return lax.all_to_all(copies,MEM,split_axis=0,concat_axis=0,tiled=True).reshape(M*shard.shape[0],shard.shape[1])


def tie(*values):
    return lax.optimization_barrier(values)


class Ring:
    def __init__(self,shard,here):
        self.here=here; self.got=[shard]
        self.next()

    def next(self):
        if len(self.got)<self.here.M:
            self.got.append(shift_mem(self.got[-1],1,self.here.M))

    def step(self,dep):
        self.got[-1],dep=tie(self.got[-1],dep)
        self.next()
        return dep

    def finish(self,dep):
        while len(self.got)<self.here.M:
            self.next()
        self.got[-1],dep=tie(self.got[-1],dep)
        return dep

    def place(self,first,end):
        M=self.here.M
        index=jnp.stack([(self.here.z-j)%M for j in range(M)]).astype(jnp.int32)
        rows=self.got[0].shape[0]
        return place_rows(index,self.got,range(M),M,3,(first,end)).reshape(M*rows,end-first)


class Gather:
    def __init__(self,slab,here):
        self.here=here; self.pieces={0:slab}; self.other={}
        for p in range(here.bits):
            self.pieces[1<<p]=cross(slab,p,here.S)

    def arrived(self,dep,keys=None):
        keys=sorted(self.pieces) if keys is None else keys
        others=sorted(self.other)
        out=tie(*[self.pieces[s] for s in keys],*[self.other[s] for s in others],dep)
        self.pieces.update(zip(keys,out)); self.other.update(zip(others,out[len(keys):]))
        return out[-1]

    def forward(self):
        here=self.here
        for subset in range(1,here.NP):
            top=subset.bit_length()-1
            if subset not in self.pieces:
                self.pieces[subset]=cross(self.pieces[subset^(1<<top)],top,here.S)

    def swap(self):
        for subset in sorted(self.pieces):
            if subset not in self.other and subset!=self.here.NP-1:
                self.other[subset]=swap_core(self.pieces[subset],self.here.S)

    def swap_last(self):
        end=self.here.NP-1
        if end not in self.other:
            self.other[end]=swap_core(self.pieces[end],self.here.S)

    def place(self):
        here=self.here
        n=here.NP
        idx=[here.slab(s)*2+here.core for s in range(n)]+[here.slab(s,False)*2+1-here.core for s in range(n)]
        index=jnp.stack(idx).astype(jnp.int32)
        parts=[self.pieces[s] for s in range(n)]+[self.other[s] for s in range(n)]
        out=place_rows(index,parts,range(2*n),2*n,0.05)
        return out.reshape(-1,parts[0].shape[1])


def fold_kernel(index_ref,ka,kb,ra,rb,send,keep):
    send[...]=(kb[...].astype(f32)+rb[...].astype(f32)).astype(bf)
    keep[...]=(ka[...].astype(f32)+ra[...].astype(f32)).astype(bf)


def fold(index,keep,recv):
    G,n,R,W=keep.shape; h=n//2
    low=pl.BlockSpec((1,1,R,W),lambda i,m,ix:(m,ix[i],0,0))
    high=pl.BlockSpec((1,1,R,W),lambda i,m,ix:(m,ix[h+i],0,0))
    out=pl.BlockSpec((1,1,R,W),lambda i,m,ix:(m,i,0,0))
    S=jax.ShapeDtypeStruct((G,h,R,W),bf)
    return pl.pallas_call(fold_kernel,
        grid_spec=pltpu.PrefetchScalarGridSpec(num_scalar_prefetch=1,grid=(h,G),in_specs=[low,high,low,high],out_specs=[out,out]),
        out_shape=[S,S],cost_estimate=cost(3),compiler_params=cp(16))(index,keep,keep,recv,recv)


def split_kernel(index_ref,a,b,*outs):
    for j,o in enumerate(outs):
        z=index_ref[j]
        o[...]=(a[:,:,pl.ds(z,1)].astype(f32)+b[:,:,pl.ds(z,1)].astype(f32)).astype(bf)


def split_mem(index,a,b):
    G,two,M,r,W=a.shape
    full_=pl.BlockSpec(memory_space=pltpu.VMEM)
    S=jax.ShapeDtypeStruct((G,two,1,r,W),bf)
    return pl.pallas_call(split_kernel,in_specs=[pl.BlockSpec(memory_space=pltpu.SMEM),full_,full_],out_specs=[full_]*M,
        out_shape=[S]*M,cost_estimate=cost(2),compiler_params=cp(16))(index,a,b)


def order_kernel(a,b,o):
    for z in range(o.shape[0]):
        o[z]=(a[:,:,z].astype(f32)+b[:,:,z].astype(f32)).astype(bf)


def order_mem(a,b):
    G,two,M,r,W=a.shape
    v=pl.BlockSpec(memory_space=pltpu.VMEM)
    return pl.pallas_call(order_kernel,in_specs=[v,v],out_specs=v,
        out_shape=jax.ShapeDtypeStruct((M,G,two,r,W),bf),cost_estimate=cost(2),compiler_params=cp(16))(a,b)


class Reduce:
    def __init__(self,send,keep,here):
        G,D,W=send.shape
        NP=here.NP; R=D//NP
        self.here=here; self.r=R//2//here.M
        self.recv=swap_core(send,here.S).reshape(G,NP,R,W)
        self.keep=keep.reshape(G,NP,R,W)
        self.index=jnp.stack([here.slab(s) for s in range(NP)]).astype(jnp.int32)
        self.p=here.bits-1

    def fold(self,dep):
        self.recv,dep=tie(self.recv,dep)
        if self.p<0:
            return dep
        go,keep=fold(self.index,self.keep,self.recv)
        go,self.keep,dep=tie(go,keep,dep)
        self.recv=cross(go,self.p,self.here.S)
        self.index=jnp.arange(1<<self.p,dtype=jnp.int32)
        self.p-=1
        return dep

    def halves(self,dep):
        while self.p>=0:
            dep=self.fold(dep)
        self.recv,dep=tie(self.recv,dep)
        G,_,R,W=self.keep.shape
        shape=(G,2,self.here.M,self.r,W)
        return self.keep.reshape(shape),self.recv.reshape(shape),dep

    def over_mem(self,dep):
        a,b,dep=self.halves(dep)
        parts,dep=tie(order_mem(a,b),dep)
        return lax.psum_scatter(parts,MEM,scatter_dimension=0,tiled=True)[0],dep

    def mem_start(self,dep):
        a,b,dep=self.halves(dep)
        M=self.here.M
        parts=split_mem(jnp.stack([(self.here.z+j)%M for j in range(M)]).astype(jnp.int32),a,b)
        out=tie(*parts,dep)
        parts,dep=out[:-1],out[-1]
        self.got=[parts[0]]+[shift_mem(parts[j],j,M) for j in range(1,M)]
        return dep

    def mem_sum(self,dep):
        out=tie(*self.got,dep)
        total=out[0].astype(f32)
        for p in out[1:-1]:
            total=total+p.astype(f32)
        G,_,_,r,W=total.shape
        return total.reshape(G,2,r,W),out[-1]


def own_rows(total,pl_):
    give=lax.dynamic_index_in_dim(total,1-pl_.core,1,keepdims=False)
    own=lax.dynamic_index_in_dim(total,pl_.core,1,keepdims=False)
    other=swap_core(give,pl_.S)
    low=jnp.where(pl_.core==0,own,other); high=jnp.where(pl_.core==0,other,own)
    return jnp.concatenate([low,high],axis=-1)


def sum_all(x,pl_):
    for b in range(pl_.S.bit_length()-1):
        x=x+lax.ppermute(x,SEQ,[(s,s^(1<<b)) for s in range(pl_.S)])
    for b in range(pl_.M.bit_length()-1):
        x=x+lax.ppermute(x,MEM,[(z,z^(1<<b)) for z in range(pl_.M)])
    return x

STEP=10
CLIP_NORM=1.0
BETA_FIRST=0.9
BETA_SECOND=0.999
ADAM_EPSILON=1e-08
RATE_MATRIX=0.06
RATE_GAIN=0.6
DECAY_MATRIX=0.01


def adam_step(master,grad,first_moment,second_moment,rate,decay):
    first_new=BETA_FIRST*first_moment+(1.0-BETA_FIRST)*grad
    second_new=BETA_SECOND*second_moment+(1.0-BETA_SECOND)*grad*grad
    first_hat=first_new/(1.0-BETA_FIRST**STEP)
    second_hat=second_new/(1.0-BETA_SECOND**STEP)
    master_new=master-rate*(first_hat/(jnp.sqrt(second_hat)+ADAM_EPSILON)+decay*master)
    return (master_new,first_new,second_new)


def columns(stack):
    return jnp.concatenate([stack[i] for i in range(stack.shape[0])],axis=1)


def on_device(seq_size,mem_size,tokens,memory,cotangent,table_len,patch_count,attn_master,attn_first,attn_second,mlp_master,mlp_first,mlp_second,gain_master,gain_first,gain_second):
    here=Place(seq_size,mem_size)
    core=here.core.reshape(1).astype(jnp.int32)
    rows,D=attn_master.shape[1:]
    aw=attn_master.astype(bf)
    gain_cols=jnp.pad(gain_master.T,((0,0),(0,125))).astype(bf)
    x=tokens[0]
    slab=gather_mem_direct(jnp.concatenate([columns(aw[:3]),gain_cols],axis=1),here)
    later=jnp.concatenate([columns(aw[3:]),columns(mlp_master.astype(bf))],axis=1)
    slab,later=tie(slab,later)
    g1=Gather(slab,here)
    ring=Ring(later,here)
    g1.forward()
    g1.pieces[2]=ring.step(g1.pieces[2])
    x=g1.arrived(x)
    g1.swap(); g1.swap_last()
    g1.other[here.NP-1]=ring.step(g1.other[here.NP-1])
    g1.other[here.NP-1],memory=tie(g1.other[here.NP-1],memory)
    mem=lax.all_to_all(memory,"mem",split_axis=0,concat_axis=0,tiled=True).reshape(-1,D)
    w_first=g1.place()
    n1,qkv,gains=norm_proj(x,w_first)
    qkv=ring.finish(qkv)
    g2=Gather(ring.place(0,5*D),here)
    slab_mlp=ring.place(5*D,later.shape[1])
    q,k,v=(qkv,0),(qkv,HEADS),(qkv,2*HEADS)
    o1,lse1=attn_fwd(table_len,q,k,v,True,512,4,(0,8))
    o1=g2.arrived(o1)
    g2.forward(); g2.swap()
    o1,lse1=attn_fwd(table_len,q,k,v,True,512,4,(8,4),(o1,lse1))
    o1,slab_mlp=tie(o1,slab_mlp)
    o1=g2.arrived(o1)
    g2.swap_last()
    g3=Gather(slab_mlp,here)
    w_second=g2.place()
    w_second,mem=tie(w_second,mem)
    mkv=mem_proj(mem,w_second,2*D)
    mkv,o1=tie(mkv,o1)
    o1=g3.arrived(o1)
    g3.forward(); g3.swap()
    h1,n2,cq=post_self(x,o1,w_second,gains)
    q2,k2,v2=(cq,0),(mkv,0),(mkv,HEADS)
    half=HEADS//2
    o2,lse2=attn_fwd(patch_count,q2,k2,v2,False,512,2,(0,half))
    o2=g3.arrived(o2)
    g3.swap_last()
    o2,lse2=attn_fwd(patch_count,q2,k2,v2,False,512,2,(half,half),(o2,lse2))
    o2=g3.arrived(o2)
    w_mlp=g3.place()
    mixed_out,gh2,gm2,gb2,dg3,mlp_send,mlp_keep=mlp(core,table_len,h1,o2,w_second,cotangent[0],gains,w_mlp)
    r1=Reduce(mlp_send,mlp_keep,here)
    part=attn_bwd(patch_count,q2,k2,v2,o2,gm2,lse2,False,256,2,(0,half))
    part=(r1.fold(part[0]),)+tuple(part[1:])
    dcq,dmk,dmv=attn_bwd(patch_count,q2,k2,v2,o2,gm2,lse2,False,256,2,(half,half),part)
    gmem_local,dcq=tie(gmem(dmk,dmv,w_second),dcq)
    grad_memory=lax.all_to_all(gmem_local.reshape(memory.shape),"mem",split_axis=0,concat_axis=0,tiled=True).astype(f32)
    gh1,gm1,gb1,dg2=mid(h1,gh2,dcq,w_second,gains)
    gb1=r1.fold(gb1)
    second_send,second_keep=wgrads(core,[gb1,n2,mem,gb2],[o1,dcq,dmk,dmv,o2],[(0,0),(1,1),(2,2),(2,3),(3,4)])
    second_send,gm1=tie(second_send,gm1)
    r2=Reduce(second_send,second_keep,here)
    gm1=r1.mem_start(gm1)
    part=attn_bwd(table_len,q,k,v,o1,gm1,lse1,True,256,2,(0,half))
    part=(r2.fold(part[0]),)+tuple(part[1:])
    dq,dk,dv=attn_bwd(table_len,q,k,v,o1,gm1,lse1,True,256,2,(half,half),part)
    first_send,first_keep=wgrads(core,[n1],[dq,dk,dv],[(0,0),(0,1),(0,2)])
    r3=Reduce(first_send,first_keep,here)
    dq,first_keep=tie(dq,first_keep)
    dq=r2.fold(dq)
    dq=r3.fold(dq)
    t_mlp,dq=r1.mem_sum(dq)
    grad_tokens,dg1=first(x,gh1,dq,dk,dv,w_first,gains)
    dg1=r3.fold(dg1)
    dg1=r2.mem_start(dg1)
    dg1=r3.mem_start(dg1)
    t_second,dg1=r2.mem_sum(dg1)
    t_first,dg1=r3.mem_sum(dg1)
    totals=(t_first,t_second,t_mlp)
    squares=jnp.sum(t_first*t_first)+(jnp.sum(t_second*t_second)+jnp.sum(t_mlp*t_mlp))
    summed=sum_all(jnp.concatenate([dg1,dg2,dg3,jnp.broadcast_to(squares,(1,D))],axis=0),here)
    gain_all=summed[:3]
    grad_norm=jnp.sqrt(summed[3,0]+jnp.sum(gain_all*gain_all))
    factor=CLIP_NORM/jnp.maximum(grad_norm,CLIP_NORM)
    red=[own_rows(t,here) for t in totals]
    attn_red=jnp.concatenate(red[:2],axis=0)
    mlp_red=red[2]
    device=lax.axis_index("seq")*mem_size+lax.axis_index("mem")
    gain_red=lax.dynamic_slice_in_dim(gain_all,device*rows,rows,1)
    a=adam_step(attn_master,attn_red*factor,attn_first,attn_second,RATE_MATRIX,DECAY_MATRIX)
    m=adam_step(mlp_master,mlp_red*factor,mlp_first,mlp_second,RATE_MATRIX,DECAY_MATRIX)
    gn=adam_step(gain_master,gain_red*factor,gain_first,gain_second,RATE_GAIN,0.0)
    return (mixed_out[None],grad_tokens[None],grad_memory,grad_norm)+a+m+gn


def solution(mesh):
    both=P(("seq","mem"),None,None)
    mid_split=P(None,("seq","mem"),None)
    gain_split=P(None,("seq","mem"))
    return jax.shard_map(functools.partial(on_device,mesh.shape["seq"],mesh.shape["mem"]),mesh=mesh,
        in_specs=(both,P("seq","mem",None),both,P(("seq","mem")),P(("seq","mem")))+(mid_split,)*6+(gain_split,)*3,
        out_specs=(both,both,P("seq","mem",None),P())+(mid_split,)*6+(gain_split,)*3,
        check_vma=False)
```

```python
import functools, math
import jax, jax.numpy as jnp
from jax import lax
from jax.sharding import PartitionSpec as P
from jax.experimental import pallas as pl
from jax.experimental.pallas import tpu as pltpu
bf=jnp.bfloat16; f32=jnp.float32
HD=64; HEADS=12
def cost(us):
    return pl.CostEstimate(flops=int(us*1e+10),bytes_accessed=10**5,transcendentals=0)
NEG=-1e30
VA=16*2**20
VB=60*2**20
LOG2E=math.log2(math.e)
TN=(((0,),(0,)),((),())); NN=(((1,),(0,)),((),())); NT=(((1,),(1,)),((),()))
def dg(a,b,dims): return lax.dot_general(a,b,dims,preferred_element_type=f32)
def rows16(cols, width, pad=16):
    idx=lax.broadcasted_iota(jnp.int32,(pad,width),0)
    out=jnp.zeros((pad,width),f32)
    for i,c in enumerate(cols): out=jnp.where(idx==i,c,out)
    return out.astype(bf)
def split3(x):
    hi=x.astype(bf).astype(f32); r=x-hi; mid=r.astype(bf).astype(f32); lo=r-mid
    return hi,mid,lo
def scaled_query(qT):
    s=qT.astype(f32)*(0.125*LOG2E)
    hi=s.astype(bf); lo=(s-hi.astype(f32)).astype(bf)
    return hi,lo


def causal_mask(x,q0,bq,fill):
    ki=lax.broadcasted_iota(jnp.int32,(bq,bq),0); qi=lax.broadcasted_iota(jnp.int32,(bq,bq),1)
    d=jnp.where(ki<=qi,x[q0:],fill)
    return jnp.concatenate([x[:q0],d],axis=0) if q0 else d

def fwd_kernel(len_ref,qT_ref,kT_ref,vT_ref,oT_ref,lse_ref,*,causal,bq,hs):
    L=qT_ref.shape[1]; K=kT_ref.shape[1]
    n=len_ref[0]
    kpos=lax.broadcasted_iota(jnp.int32,(1,K),1)
    kx=rows16([jnp.where(kpos<n,0.0,NEG)],K); qx=rows16([jnp.ones((1,L),f32)],L); vx=rows16([jnp.ones((1,K),f32)],K)
    ops=[]
    for h in range(hs):
        r=slice(h*HD,(h+1)*HD)
        kT=kT_ref[r,:]
        hi,lo=scaled_query(qT_ref[r,:])
        ops.append((jnp.concatenate([kT,kT,kx],axis=0),jnp.concatenate([hi,lo,qx],axis=0),jnp.concatenate([vT_ref[r,:],vx],axis=0)))
    jobs=[(h,q0) for h in range(hs) for q0 in range(0,L,bq)]
    def score(j):
        h,q0=j; ke=min(K,q0+bq) if causal else K
        return dg(ops[h][0][:,:ke],ops[h][1][:,q0:q0+bq],TN)
    nxt=score(jobs[0])
    for i,(h,q0) in enumerate(jobs):
        s=nxt
        if i+1<len(jobs): nxt=score(jobs[i+1])
        ke=s.shape[0]
        if causal: s=causal_mask(s,q0,bq,NEG)
        m=jnp.max(s,axis=0,keepdims=True)
        p=jnp.exp2(s-m).astype(bf)
        o=dg(ops[h][2][:,:ke],p,NN)
        l=o[HD:HD+1]
        oT_ref[h*HD:(h+1)*HD,q0:q0+bq]=(o[:HD]*(1.0/l)).astype(bf)
        lse_ref[h,:,q0:q0+bq]=m+jnp.log2(l)

def head_block(hs,w,offset=0):
    return pl.BlockSpec((hs*HD,w),lambda h:(h+offset//hs,0))
def fwd_part_kernel(*refs,**kw):
    fwd_kernel(*refs[:4],*refs[6:],**kw)
def attn_fwd(n,q,k,v,causal,bq=256,hs=2,part=None,into=None,vmem=VA):
    L=q[0].shape[1]; K=k[0].shape[1]; D=HEADS*HD
    h0,hn=part or (0,HEADS)
    hb=lambda w,o=0: head_block(hs,w,o+h0)
    specs=[pl.BlockSpec(memory_space=pltpu.SMEM),hb(L,q[1]),hb(K,k[1]),hb(K,v[1])]
    args=(n,q[0],k[0],v[0])
    if into is not None:
        specs+=[pl.BlockSpec(memory_space=pl.ANY)]*2
        args+=tuple(into)
    return pl.pallas_call(functools.partial(fwd_kernel if into is None else fwd_part_kernel,causal=causal,bq=bq,hs=hs),grid=(hn//hs,),
      in_specs=specs,
      out_specs=[hb(L),pl.BlockSpec((hs,1,L),lambda h:(h+h0//hs,0,0))],
      out_shape=[jax.ShapeDtypeStruct((D,L),bf),jax.ShapeDtypeStruct((HEADS,1,L),f32)],
      input_output_aliases={} if into is None else {4:0,5:1},
      cost_estimate=cost(0.3),compiler_params=pltpu.CompilerParams(vmem_limit_bytes=vmem),
    )(*args)

def bwd_kernel(len_ref,qT_ref,kT_ref,vT_ref,oT_ref,gT_ref,lse_ref,dq_ref,dk_ref,dv_ref,dka,dva,*,causal,bq,hs):
    L=qT_ref.shape[1]; K=kT_ref.shape[1]
    n=len_ref[0]
    kpos=lax.broadcasted_iota(jnp.int32,(1,K),1)
    bias=jnp.where(kpos<n,0.0,NEG)
    one_k=jnp.ones((1,K),f32)
    kx=rows16([bias,one_k,one_k,one_k],K); vx=rows16([one_k,one_k,one_k],K)
    ops=[]
    for h in range(hs):
        r=slice(h*HD,(h+1)*HD)
        kT=kT_ref[r,:]; qT=qT_ref[r,:]; gT=gT_ref[r,:]
        hi,lo=scaled_query(qT)
        delta=jnp.sum(oT_ref[r,:].astype(f32)*gT.astype(f32),axis=0,keepdims=True)
        ops.append(dict(k=kT,q=qT,g=gT,kaug=jnp.concatenate([kT,kT,kx],axis=0),
          qaug=jnp.concatenate([hi,lo,rows16([jnp.ones((1,L),f32),*split3(-lse_ref[h])],L)],axis=0),
          vaug=jnp.concatenate([vT_ref[r,:],vx],axis=0),
          gaug=jnp.concatenate([gT,rows16(list(split3(-delta)),L)],axis=0)))
    jobs=[(h,q0) for h in range(hs) for q0 in reversed(range(0,L,bq))]
    def score(j):
        h,q0=j; ke=min(K,q0+bq) if causal else K; sl=slice(q0,q0+bq); o=ops[h]
        return dg(o["kaug"][:,:ke],o["qaug"][:,sl],TN),dg(o["vaug"][:,:ke],o["gaug"][:,sl],TN)
    nxt=score(jobs[0])
    for i,(h,q0) in enumerate(jobs):
        s,dp=nxt
        if i+1<len(jobs): nxt=score(jobs[i+1])
        ke=s.shape[0]; sl=slice(q0,q0+bq); o=ops[h]; r=slice(h*HD,(h+1)*HD)
        p=jnp.exp2(s)
        if causal: p=causal_mask(p,q0,bq,0.0)
        ds=(p*dp).astype(bf)
        pb=p.astype(bf)
        dq_ref[r,sl]=(dg(o["k"][:,:ke],ds,NN)*0.125).astype(bf)
        dv=dg(o["g"][:,sl],pb,NT)
        dk=dg(o["q"][:,sl],ds,NT)
        if q0==L-bq:
            dka[r]=dk; dva[r]=dv
        else:
            dka[r,:ke]+=dk; dva[r,:ke]+=dv
    dk_ref[...]=(dka[...]*0.125).astype(bf)
    dv_ref[...]=dva[...].astype(bf)

def bwd_part_kernel(*refs,**kw):
    bwd_kernel(*refs[:7],*refs[10:],**kw)
def attn_bwd(n,q,k,v,oT,gT,lse,causal,bq=256,hs=2,part=None,into=None):
    L=q[0].shape[1]; K=k[0].shape[1]; D=HEADS*HD
    h0,hn=part or (0,HEADS)
    hb=lambda w,o=0: head_block(hs,w,o+h0)
    S=jax.ShapeDtypeStruct
    specs=[pl.BlockSpec(memory_space=pltpu.SMEM),hb(L,q[1]),hb(K,k[1]),hb(K,v[1]),hb(L),hb(L),pl.BlockSpec((hs,1,L),lambda h:(h+h0//hs,0,0))]
    args=(n,q[0],k[0],v[0],oT,gT,lse)
    if into is not None:
        specs+=[pl.BlockSpec(memory_space=pl.ANY)]*3
        args+=tuple(into)
    return pl.pallas_call(functools.partial(bwd_kernel if into is None else bwd_part_kernel,causal=causal,bq=bq,hs=hs),grid=(hn//hs,),
      in_specs=specs,out_specs=[hb(L),hb(K),hb(K)],
      out_shape=[S((D,L),bf),S((D,K),bf),S((D,K),bf)],
      input_output_aliases={} if into is None else {7:0,8:1,9:2},
      scratch_shapes=[pltpu.VMEM((hs*HD,K),f32),pltpu.VMEM((hs*HD,K),f32)],
      cost_estimate=cost(14),compiler_params=pltpu.CompilerParams(vmem_limit_bytes=VA),
    )(*args)

TT=(((0,),(1,)),((),()))
EPS=1e-6
VL=60*2**20
def cp(mb=24): return pltpu.CompilerParams(vmem_limit_bytes=mb*2**20)
def full(shape): return pl.BlockSpec(shape,lambda i:(0,)*len(shape))
GC=0.7978845608028654

def rms_r(v): return lax.rsqrt(jnp.mean(v*v,axis=-1,keepdims=True)+EPS)

def wcol(D,j): return pl.BlockSpec((D,D),lambda i:(0,j))
def gain_spec(D): return pl.BlockSpec((8,D),lambda i:(0,0))

def proj_kernel(x_ref,e_ref,w_ref,n_ref,yT_ref,g_ref):
    @pl.when(pl.program_id(0)==0)
    def _():
        g=e_ref[...].astype(f32).T[0:8,:]
        g_ref[...]=g
        x=x_ref[...].astype(f32)
        n_ref[...]=(x*rms_r(x)*g[0:1,:]).astype(bf)
    yT_ref[...]=dg(w_ref[...],n_ref[...],TT).astype(bf)
def norm_proj(x,w,fb=384):
    L,D=x.shape; F=3*D
    return pl.pallas_call(proj_kernel,grid=(F//fb,),
      in_specs=[full((L,D)),pl.BlockSpec((D,128),lambda i:(0,F//128)),pl.BlockSpec((D,fb),lambda i:(0,i))],
      out_specs=[full((L,D)),pl.BlockSpec((fb,L),lambda i:(i,0)),gain_spec(D)],
      out_shape=[jax.ShapeDtypeStruct((L,D),bf),jax.ShapeDtypeStruct((F,L),bf),jax.ShapeDtypeStruct((8,D),f32)],cost_estimate=cost(6),compiler_params=cp())(x,w,w)
def memproj_kernel(x_ref,w_ref,yT_ref):
    yT_ref[...]=dg(w_ref[...],x_ref[...],TT).astype(bf)
def mem_proj(x,w,first_col,fb=384):
    L,D=x.shape; F=2*D
    return pl.pallas_call(memproj_kernel,grid=(F//fb,),
      in_specs=[full((L,D)),pl.BlockSpec((D,fb),lambda i:(0,first_col//fb+i))],
      out_specs=pl.BlockSpec((fb,L),lambda i:(i,0)),
      out_shape=jax.ShapeDtypeStruct((F,L),bf),cost_estimate=cost(0.1),compiler_params=cp())(x,w)

def post_self_kernel(x_ref,oT_ref,w3_ref,w4_ref,g_ref,h_ref,n_ref,cT_ref):
    h=x_ref[...].astype(f32)+dg(oT_ref[...],w3_ref[...],TT)
    h_ref[...]=h
    n=(h*rms_r(h)*g_ref[1:2,:]).astype(bf)
    n_ref[...]=n
    cT_ref[...]=dg(n,w4_ref[...],NN).astype(bf).T
def post_self(x,oT,w,g,tb=256):
    L,D=x.shape
    tok=pl.BlockSpec((tb,D),lambda i:(i,0)); tokT=pl.BlockSpec((D,tb),lambda i:(0,i))
    return pl.pallas_call(post_self_kernel,grid=(L//tb,),
      in_specs=[tok,tokT,wcol(D,0),wcol(D,1),gain_spec(D)],
      out_specs=[tok,tok,tokT],
      out_shape=[jax.ShapeDtypeStruct((L,D),f32),jax.ShapeDtypeStruct((L,D),bf),jax.ShapeDtypeStruct((D,L),bf)],cost_estimate=cost(0.3),compiler_params=cp())(x,oT,w,w,g)

def mlp_chunk(n3,gb,wg,wu,wd,dw_ref,inner_s,dgate_s,dup_s,oacc,nacc,tb):
    L=n3.shape[0]; nt=L//tb
    def pre(t):
        sl=slice(t*tb,(t+1)*tb)
        a=n3[sl,:]
        return dg(a,wg[...],NN),dg(a,wu[...],NN),dg(gb[sl,:],wd[...],NN)
    nxt=pre(0)
    for t in range(nt):
        sl=slice(t*tb,(t+1)*tb)
        g,u,di=nxt
        if t+1<nt: nxt=pre(t+1)
        g2=g*g
        th=jnp.tanh(g*(GC+(GC*0.044715)*g2))
        hp=0.5+0.5*th
        ge=g*hp
        dge=hp+(0.5*g)*(1.0-th*th)*(GC+(3*GC*0.044715)*g2)
        inner=(ge*u).astype(bf)
        dgate=(di*u*dge).astype(bf)
        dup=(di*ge).astype(bf)
        inner_s[sl,:]=inner; dgate_s[sl,:]=dgate; dup_s[sl,:]=dup
        oacc[sl,:]+=dg(inner,wd[...],NT)
        nacc[sl,:]+=dg(dgate,wg[...],NT)+dg(dup,wu[...],NT)
    dw_ref[0]=dg(n3[...],dgate_s[...],TN).astype(bf)
    dw_ref[1]=dg(n3[...],dup_s[...],TN).astype(bf)
    dw_ref[2]=dg(gb[...],inner_s[...],TN).astype(bf)

def mlp_kernel(core_ref,len_ref,h1_ref,oT_ref,w7_ref,cot_ref,g_ref,wg_ref,wu_ref,wd_ref,
               out_ref,gh_ref,gmT_ref,gb2_ref,dg_ref,send_ref,keep_ref,
               h2,n3,gb,oacc,nacc,dw,inner_s,dgate_s,dup_s,sems,*,tb):
    L,D=h1_ref.shape
    fc=dw.shape[3]
    i=pl.program_id(0); count=pl.num_programs(0); half=count//2
    slot=lax.rem(i,2)
    def copy(step,to):
        col=pl.multiple_of(lax.rem(step,half)*fc,fc)
        return pltpu.make_async_copy(dw.at[lax.rem(step,2)],to.at[:,:,pl.ds(col,fc)],sems.at[lax.rem(step,2)])
    @pl.when(i==0)
    def _():
        n=len_ref[0]
        for t in range(L//tb):
            sl=slice(t*tb,(t+1)*tb)
            h=h1_ref[sl,:]+dg(oT_ref[:,sl],w7_ref[...],TT)
            h2[sl,:]=h
            oacc[sl,:]=h
            nacc[sl,:]=jnp.zeros((tb,D),f32)
            n3[sl,:]=(h*rms_r(h)*g_ref[2:3,:]).astype(bf)
            row=t*tb+lax.broadcasted_iota(jnp.int32,(tb,1),0)
            gb[sl,:]=jnp.where(row<n,cot_ref[sl,:].astype(f32),0.0).astype(bf)
    @pl.when(i>=2)
    def _():
        copy(i-2,send_ref).wait()
    mlp_chunk(n3,gb,wg_ref,wu_ref,wd_ref,dw.at[slot],inner_s,dgate_s,dup_s,oacc,nacc,tb)
    @pl.when(i<half)
    def _():
        copy(i,send_ref).start()
    @pl.when(i>=half)
    def _():
        copy(i,keep_ref).start()
    @pl.when(i==count-1)
    def _():
        acc=jnp.zeros((1,D),f32)
        for t in range(L//tb):
            sl=slice(t*tb,(t+1)*tb)
            h=h2[sl,:]; uu=nacc[sl,:]
            out_ref[sl,:]=oacc[sl,:].astype(bf)
            r=rms_r(h); ug=uu*g_ref[2:3,:]
            gh=gb[sl,:].astype(f32)+r*ug-h*((r*r*r)*jnp.mean(ug*h,axis=-1,keepdims=True))
            acc=acc+jnp.sum(uu*h*r,axis=0,keepdims=True)
            gh_ref[sl,:]=gh
            b=gh.astype(bf)
            gb2_ref[sl,:]=b
            gmT_ref[:,sl]=dg(b,w7_ref[...],NN).astype(bf).T
        dg_ref[...]=acc
        copy(i-1,keep_ref).wait()
        copy(i,keep_ref).wait()
def mlp(core,n,h1,oT,w_second,cot,g,wm,fc=512,tb=256):
    L,D=h1.shape; F=wm.shape[1]//3; nc=F//fc; hc=nc//2
    whole=lambda shape: pl.BlockSpec(shape,lambda i,c:(0,)*len(shape),pipeline_mode=pl.Buffered(1))
    wb=lambda j: pl.BlockSpec((D,fc),lambda i,c,j=j:(0,j*nc+lax.rem(i+(1-c[0])*hc,nc)))
    S=jax.ShapeDtypeStruct
    hbm=pl.BlockSpec(memory_space=pl.ANY)
    return pl.pallas_call(functools.partial(mlp_kernel,tb=tb),
      grid_spec=pltpu.PrefetchScalarGridSpec(num_scalar_prefetch=1,grid=(nc,),
      in_specs=[pl.BlockSpec(memory_space=pltpu.SMEM),whole((L,D)),whole((D,L)),pl.BlockSpec((D,D),lambda i,c:(0,4),pipeline_mode=pl.Buffered(1)),whole((L,D)),whole((8,D)),wb(0),wb(1),wb(2)],
      out_specs=[whole((L,D)),whole((L,D)),whole((D,L)),whole((L,D)),whole((1,D)),hbm,hbm],
      scratch_shapes=[pltpu.VMEM((L,D),f32),pltpu.VMEM((L,D),bf),pltpu.VMEM((L,D),bf),pltpu.VMEM((L,D),f32),pltpu.VMEM((L,D),f32),
        pltpu.VMEM((2,3,D,fc),bf),pltpu.VMEM((L,fc),bf),pltpu.VMEM((L,fc),bf),pltpu.VMEM((L,fc),bf),pltpu.SemaphoreType.DMA((2,))]),
      out_shape=[S((L,D),bf),S((L,D),f32),S((D,L),bf),S((L,D),bf),S((1,D),f32),S((3,D,F//2),bf),S((3,D,F//2),bf)],
      cost_estimate=cost(42),compiler_params=cp(48))(core,n,h1,oT,w_second,cot,g,wm,wm,wm)

def mid_kernel(h1_ref,gh2_ref,dcT_ref,w4_ref,w3_ref,g_ref,gh1_ref,gmT_ref,gb_ref,dg_ref):
    i=pl.program_id(0)
    u=dg(dcT_ref[...],w4_ref[...],TT)
    h=h1_ref[...]
    r=rms_r(h); ug=u*g_ref[1:2,:]
    gh=gh2_ref[...]+r*ug-h*((r*r*r)*jnp.mean(ug*h,axis=-1,keepdims=True))
    gh1_ref[...]=gh
    b=gh.astype(bf)
    gb_ref[...]=b
    gmT_ref[...]=dg(b,w3_ref[...],NN).astype(bf).T
    s=jnp.sum(u*h*r,axis=0,keepdims=True)
    @pl.when(i==0)
    def _(): dg_ref[...]=s
    @pl.when(i>0)
    def _(): dg_ref[...]+=s
def mid(h1,gh2,dcT,w,g,tb=256):
    L,D=h1.shape
    tok=pl.BlockSpec((tb,D),lambda i:(i,0)); tokT=pl.BlockSpec((D,tb),lambda i:(0,i))
    S=jax.ShapeDtypeStruct
    return pl.pallas_call(mid_kernel,grid=(L//tb,),
      in_specs=[tok,tok,tokT,wcol(D,1),wcol(D,0),gain_spec(D)],
      out_specs=[tok,tokT,tok,full((1,D))],
      out_shape=[S((L,D),f32),S((D,L),bf),S((L,D),bf),S((1,D),f32)],cost_estimate=cost(0.2),compiler_params=cp())(h1,gh2,dcT,w,w,g)

def wgrads_kernel(core_ref,*refs,pairs,na,ng):
    a_refs=refs[:na]; g_refs=refs[na:na+ng]; send_ref,keep_ref=refs[na+ng:]
    k=core_ref[0]
    W=send_ref.shape[2]
    for out,half in ((send_ref,1-k),(keep_ref,k)):
        start=pl.multiple_of(half*W,W)
        for m,(ia,ig) in enumerate(pairs):
            out[m]=dg(a_refs[ia][...],g_refs[ig][pl.ds(start,W),:],TT).astype(bf)
def wgrads(core,a,g,pairs):
    D=a[0].shape[1]; F=g[0].shape[0]
    v=pl.BlockSpec(memory_space=pltpu.VMEM)
    S=jax.ShapeDtypeStruct((len(pairs),D,F//2),bf)
    return pl.pallas_call(functools.partial(wgrads_kernel,pairs=tuple(pairs),na=len(a),ng=len(g)),
      in_specs=[pl.BlockSpec(memory_space=pltpu.SMEM)]+[v]*(len(a)+len(g)),out_specs=[v,v],
      out_shape=[S,S],cost_estimate=cost(8),compiler_params=cp(40))(core,*a,*g)

def gmem_kernel(kT_ref,vT_ref,w5_ref,w6_ref,o_ref):
    o_ref[...]=(dg(kT_ref[...],w5_ref[...],TT)+dg(vT_ref[...],w6_ref[...],TT)).astype(bf)
def gmem(kT,vT,w56,tb=256):
    D,L=kT.shape
    tokT=pl.BlockSpec((D,tb),lambda i:(0,i))
    return pl.pallas_call(gmem_kernel,grid=(L//tb,),
      in_specs=[tokT,tokT,wcol(D,2),wcol(D,3)],
      out_specs=pl.BlockSpec((tb,D),lambda i:(i,0)),
      out_shape=jax.ShapeDtypeStruct((L,D),bf),cost_estimate=cost(0.2),compiler_params=cp())(kT,vT,w56,w56)

def first_kernel(x_ref,gh1_ref,qT_ref,kT_ref,vT_ref,w0_ref,w1_ref,w2_ref,g_ref,gt_ref,dg_ref):
    i=pl.program_id(0)
    u=dg(qT_ref[...],w0_ref[...],TT)+dg(kT_ref[...],w1_ref[...],TT)+dg(vT_ref[...],w2_ref[...],TT)
    h=x_ref[...].astype(f32)
    r=rms_r(h); ug=u*g_ref[0:1,:]
    gt_ref[...]=gh1_ref[...]+r*ug-h*((r*r*r)*jnp.mean(ug*h,axis=-1,keepdims=True))
    s=jnp.sum(u*h*r,axis=0,keepdims=True)
    @pl.when(i==0)
    def _(): dg_ref[...]=s
    @pl.when(i>0)
    def _(): dg_ref[...]+=s
def first(x,gh1,qT,kT,vT,w,g,tb=256):
    L,D=x.shape
    tok=pl.BlockSpec((tb,D),lambda i:(i,0)); tokT=pl.BlockSpec((D,tb),lambda i:(0,i))
    S=jax.ShapeDtypeStruct
    wb=lambda j: pl.BlockSpec((D,D),lambda i,j=j:(0,j))
    return pl.pallas_call(first_kernel,grid=(L//tb,),
      in_specs=[tok,tok,tokT,tokT,tokT,wb(0),wb(1),wb(2),gain_spec(D)],
      out_specs=[tok,full((1,D))],
      out_shape=[S((L,D),f32),S((1,D),f32)],cost_estimate=cost(7),compiler_params=cp())(x,gh1,qT,kT,vT,w,w,w,g)

SEQ="seq"
MEM="mem"


def plane_bits(seq_size):
    return max(0,(seq_size//2).bit_length()-1)


def bit_order(core,bits):
    order=list(range(1,bits+1))
    return order if core==0 else order[::-1]


def subset_mask(core,subset,bits):
    order=bit_order(core,bits)
    mask=0
    for p in range(bits):
        if subset>>p&1:
            mask^=1<<(order[p]-1)
    return mask


def cross(x,position,seq_size):
    bits=plane_bits(seq_size)
    perm=[(s,s^(1<<bit_order(s&1,bits)[position])) for s in range(seq_size)]
    return lax.ppermute(x,SEQ,perm)


def swap_core(x,seq_size):
    return lax.ppermute(x,SEQ,[(s,s^1) for s in range(seq_size)])


def shift_mem(x,step,mem_size):
    return lax.ppermute(x,MEM,[(z,(z+step)%mem_size) for z in range(mem_size)])


def copy_kernel(index_ref,*refs,places,columns):
    count=len(places)
    sources=refs[:count]; out=refs[count]; sems=refs[count+1]
    copies=[]
    for j,(source,place) in enumerate(zip(sources,places)):
        if columns is not None:
            source=source.at[:,pl.ds(columns[0],columns[1]-columns[0])]
        copies.append(pltpu.make_async_copy(source,out.at[index_ref[place]],sems.at[j]))
        copies[-1].start()
    for c in copies:
        c.wait()


def place_rows(index,pieces,places,slots,us,columns=None):
    piece=pieces[0]
    shape=piece.shape if columns is None else (piece.shape[0],columns[1]-columns[0])
    return pl.pallas_call(functools.partial(copy_kernel,places=tuple(places),columns=columns),
        in_specs=[pl.BlockSpec(memory_space=pltpu.SMEM)]+[pl.BlockSpec(memory_space=pl.ANY)]*len(pieces),
        out_specs=pl.BlockSpec(memory_space=pltpu.VMEM),
        out_shape=jax.ShapeDtypeStruct((slots,)+shape,piece.dtype),
        scratch_shapes=[pltpu.SemaphoreType.DMA((len(pieces),))],
        cost_estimate=cost(us),compiler_params=cp(20),
    )(index,*pieces)


class Place:
    def __init__(self,seq_size,mem_size):
        self.S=seq_size; self.M=mem_size; self.bits=plane_bits(seq_size); self.NP=seq_size//2
        s=lax.axis_index(SEQ); self.z=lax.axis_index(MEM)
        self.core=s%2; self.plane=s//2

    def slab(self,subset,own=True):
        m0=subset_mask(0,subset,self.bits); m1=subset_mask(1,subset,self.bits)
        c=self.core if own else 1-self.core
        return self.plane^jnp.where(c==0,m0,m1)


def gather_mem_direct(shard,pl_):
    M=pl_.M
    pieces=[shard]+[shift_mem(shard,j,M) for j in range(1,M)]
    index=jnp.stack([(pl_.z-j)%M for j in range(M)]).astype(jnp.int32)
    return place_rows(index,pieces,range(M),M,3).reshape(M*shard.shape[0],shard.shape[1])


def gather_mem_exchange(shard,here):
    M=here.M
    copies=jnp.broadcast_to(shard[None],(M,)+shard.shape)
    return lax.all_to_all(copies,MEM,split_axis=0,concat_axis=0,tiled=True).reshape(M*shard.shape[0],shard.shape[1])


def tie(*values):
    return lax.optimization_barrier(values)


class Ring:
    def __init__(self,shard,here):
        self.here=here; self.got=[shard]
        self.next()

    def next(self):
        if len(self.got)<self.here.M:
            self.got.append(shift_mem(self.got[-1],1,self.here.M))

    def step(self,dep):
        self.got[-1],dep=tie(self.got[-1],dep)
        self.next()
        return dep

    def finish(self,dep):
        while len(self.got)<self.here.M:
            self.next()
        self.got[-1],dep=tie(self.got[-1],dep)
        return dep

    def place(self,first,end):
        M=self.here.M
        index=jnp.stack([(self.here.z-j)%M for j in range(M)]).astype(jnp.int32)
        rows=self.got[0].shape[0]
        return place_rows(index,self.got,range(M),M,0.05,(first,end)).reshape(M*rows,end-first)


class Gather:
    def __init__(self,slab,here):
        self.here=here; self.pieces={0:slab}; self.other={}
        for p in range(here.bits):
            self.pieces[1<<p]=cross(slab,p,here.S)

    def arrived(self,dep,keys=None):
        keys=sorted(self.pieces) if keys is None else keys
        others=sorted(self.other)
        out=tie(*[self.pieces[s] for s in keys],*[self.other[s] for s in others],dep)
        self.pieces.update(zip(keys,out)); self.other.update(zip(others,out[len(keys):]))
        return out[-1]

    def forward(self):
        here=self.here
        for subset in range(1,here.NP):
            top=subset.bit_length()-1
            if subset not in self.pieces:
                self.pieces[subset]=cross(self.pieces[subset^(1<<top)],top,here.S)

    def swap(self):
        for subset in sorted(self.pieces):
            if subset not in self.other and subset!=self.here.NP-1:
                self.other[subset]=swap_core(self.pieces[subset],self.here.S)

    def swap_last(self):
        end=self.here.NP-1
        if end not in self.other:
            self.other[end]=swap_core(self.pieces[end],self.here.S)

    def place(self):
        here=self.here
        n=here.NP
        idx=[here.slab(s)*2+here.core for s in range(n)]+[here.slab(s,False)*2+1-here.core for s in range(n)]
        index=jnp.stack(idx).astype(jnp.int32)
        parts=[self.pieces[s] for s in range(n)]+[self.other[s] for s in range(n)]
        out=place_rows(index,parts,range(2*n),2*n,0.05)
        return out.reshape(-1,parts[0].shape[1])


def fold_kernel(index_ref,ka,kb,ra,rb,send,keep):
    send[...]=(kb[...].astype(f32)+rb[...].astype(f32)).astype(bf)
    keep[...]=(ka[...].astype(f32)+ra[...].astype(f32)).astype(bf)


def fold(index,keep,recv):
    G,n,R,W=keep.shape; h=n//2
    low=pl.BlockSpec((1,1,R,W),lambda i,m,ix:(m,ix[i],0,0))
    high=pl.BlockSpec((1,1,R,W),lambda i,m,ix:(m,ix[h+i],0,0))
    out=pl.BlockSpec((1,1,R,W),lambda i,m,ix:(m,i,0,0))
    S=jax.ShapeDtypeStruct((G,h,R,W),bf)
    return pl.pallas_call(fold_kernel,
        grid_spec=pltpu.PrefetchScalarGridSpec(num_scalar_prefetch=1,grid=(h,G),in_specs=[low,high,low,high],out_specs=[out,out]),
        out_shape=[S,S],cost_estimate=cost(3),compiler_params=cp(16))(index,keep,keep,recv,recv)


def split_kernel(index_ref,a,b,*outs):
    for j,o in enumerate(outs):
        z=index_ref[j]
        o[...]=(a[:,:,pl.ds(z,1)].astype(f32)+b[:,:,pl.ds(z,1)].astype(f32)).astype(bf)


def split_mem(index,a,b):
    G,two,M,r,W=a.shape
    full_=pl.BlockSpec(memory_space=pltpu.VMEM)
    S=jax.ShapeDtypeStruct((G,two,1,r,W),bf)
    return pl.pallas_call(split_kernel,in_specs=[pl.BlockSpec(memory_space=pltpu.SMEM),full_,full_],out_specs=[full_]*M,
        out_shape=[S]*M,cost_estimate=cost(2),compiler_params=cp(16))(index,a,b)


def order_kernel(a,b,o):
    for z in range(o.shape[0]):
        o[z]=(a[:,:,z].astype(f32)+b[:,:,z].astype(f32)).astype(bf)


def order_mem(a,b):
    G,two,M,r,W=a.shape
    v=pl.BlockSpec(memory_space=pltpu.VMEM)
    return pl.pallas_call(order_kernel,in_specs=[v,v],out_specs=v,
        out_shape=jax.ShapeDtypeStruct((M,G,two,r,W),bf),cost_estimate=cost(2),compiler_params=cp(16))(a,b)


class Reduce:
    def __init__(self,send,keep,here):
        G,D,W=send.shape
        NP=here.NP; R=D//NP
        self.here=here; self.r=R//2//here.M
        self.recv=swap_core(send,here.S).reshape(G,NP,R,W)
        self.keep=keep.reshape(G,NP,R,W)
        self.index=jnp.stack([here.slab(s) for s in range(NP)]).astype(jnp.int32)
        self.p=here.bits-1

    def fold(self,dep):
        self.recv,dep=tie(self.recv,dep)
        if self.p<0:
            return dep
        go,keep=fold(self.index,self.keep,self.recv)
        go,self.keep,dep=tie(go,keep,dep)
        self.recv=cross(go,self.p,self.here.S)
        self.index=jnp.arange(1<<self.p,dtype=jnp.int32)
        self.p-=1
        return dep

    def halves(self,dep):
        while self.p>=0:
            dep=self.fold(dep)
        self.recv,dep=tie(self.recv,dep)
        G,_,R,W=self.keep.shape
        shape=(G,2,self.here.M,self.r,W)
        return self.keep.reshape(shape),self.recv.reshape(shape),dep

    def over_mem(self,dep):
        a,b,dep=self.halves(dep)
        parts,dep=tie(order_mem(a,b),dep)
        return lax.psum_scatter(parts,MEM,scatter_dimension=0,tiled=True)[0],dep

    def mem_start(self,dep):
        a,b,dep=self.halves(dep)
        M=self.here.M
        parts=split_mem(jnp.stack([(self.here.z+j)%M for j in range(M)]).astype(jnp.int32),a,b)
        out=tie(*parts,dep)
        parts,dep=out[:-1],out[-1]
        self.got=[parts[0]]+[shift_mem(parts[j],j,M) for j in range(1,M)]
        return dep

    def mem_sum(self,dep):
        out=tie(*self.got,dep)
        total=out[0].astype(f32)
        for p in out[1:-1]:
            total=total+p.astype(f32)
        G,_,_,r,W=total.shape
        return total.reshape(G,2,r,W),out[-1]


def own_rows(total,pl_):
    give=lax.dynamic_index_in_dim(total,1-pl_.core,1,keepdims=False)
    own=lax.dynamic_index_in_dim(total,pl_.core,1,keepdims=False)
    other=swap_core(give,pl_.S)
    low=jnp.where(pl_.core==0,own,other); high=jnp.where(pl_.core==0,other,own)
    return jnp.concatenate([low,high],axis=-1)


def sum_all(x,pl_):
    for b in range(pl_.S.bit_length()-1):
        x=x+lax.ppermute(x,SEQ,[(s,s^(1<<b)) for s in range(pl_.S)])
    for b in range(pl_.M.bit_length()-1):
        x=x+lax.ppermute(x,MEM,[(z,z^(1<<b)) for z in range(pl_.M)])
    return x

STEP=10
CLIP_NORM=1.0
BETA_FIRST=0.9
BETA_SECOND=0.999
ADAM_EPSILON=1e-08
RATE_MATRIX=0.06
RATE_GAIN=0.6
DECAY_MATRIX=0.01


def adam_step(master,grad,first_moment,second_moment,rate,decay):
    first_new=BETA_FIRST*first_moment+(1.0-BETA_FIRST)*grad
    second_new=BETA_SECOND*second_moment+(1.0-BETA_SECOND)*grad*grad
    first_hat=first_new/(1.0-BETA_FIRST**STEP)
    second_hat=second_new/(1.0-BETA_SECOND**STEP)
    master_new=master-rate*(first_hat/(jnp.sqrt(second_hat)+ADAM_EPSILON)+decay*master)
    return (master_new,first_new,second_new)


def columns(stack):
    return jnp.concatenate([stack[i] for i in range(stack.shape[0])],axis=1)


def on_device(seq_size,mem_size,tokens,memory,cotangent,table_len,patch_count,attn_master,attn_first,attn_second,mlp_master,mlp_first,mlp_second,gain_master,gain_first,gain_second):
    here=Place(seq_size,mem_size)
    core=here.core.reshape(1).astype(jnp.int32)
    rows,D=attn_master.shape[1:]
    aw=attn_master.astype(bf)
    gain_cols=jnp.pad(gain_master.T,((0,0),(0,125))).astype(bf)
    x=tokens[0]
    slab=gather_mem_direct(jnp.concatenate([columns(aw[:3]),gain_cols],axis=1),here)
    later=jnp.concatenate([columns(aw[3:]),columns(mlp_master.astype(bf))],axis=1)
    slab,later=tie(slab,later)
    g1=Gather(slab,here)
    ring=Ring(later,here)
    g1.forward()
    g1.pieces[2]=ring.step(g1.pieces[2])
    x=g1.arrived(x)
    g1.swap(); g1.swap_last()
    g1.other[here.NP-1]=ring.step(g1.other[here.NP-1])
    g1.other[here.NP-1],memory=tie(g1.other[here.NP-1],memory)
    mem=lax.all_to_all(memory,"mem",split_axis=0,concat_axis=0,tiled=True).reshape(-1,D)
    w_first=g1.place()
    n1,qkv,gains=norm_proj(x,w_first)
    qkv=ring.finish(qkv)
    g2=Gather(ring.place(0,5*D),here)
    slab_mlp=ring.place(5*D,later.shape[1])
    q,k,v=(qkv,0),(qkv,HEADS),(qkv,2*HEADS)
    o1,lse1=attn_fwd(table_len,q,k,v,True,512,4,(0,8))
    o1=g2.arrived(o1)
    g2.forward(); g2.swap()
    o1,slab_mlp=tie(o1,slab_mlp)
    g3=Gather(slab_mlp,here)
    o1,lse1=attn_fwd(table_len,q,k,v,True,512,4,(8,4),(o1,lse1))
    o1=g2.arrived(o1)
    g2.swap_last()
    w_second=g2.place()
    w_second,mem=tie(w_second,mem)
    mkv=mem_proj(mem,w_second,2*D)
    mkv,o1=tie(mkv,o1)
    o1=g3.arrived(o1)
    g3.forward(); g3.swap()
    h1,n2,cq=post_self(x,o1,w_second,gains)
    q2,k2,v2=(cq,0),(mkv,0),(mkv,HEADS)
    half=HEADS//2
    o2,lse2=attn_fwd(patch_count,q2,k2,v2,False,512,2,(0,half),None,VB)
    o2=g3.arrived(o2)
    g3.swap_last()
    o2,lse2=attn_fwd(patch_count,q2,k2,v2,False,512,2,(half,half),(o2,lse2),VB)
    o2=g3.arrived(o2)
    w_mlp=g3.place()
    mixed_out,gh2,gm2,gb2,dg3,mlp_send,mlp_keep=mlp(core,table_len,h1,o2,w_second,cotangent[0],gains,w_mlp)
    r1=Reduce(mlp_send,mlp_keep,here)
    part=attn_bwd(patch_count,q2,k2,v2,o2,gm2,lse2,False,256,2,(0,half))
    part=(r1.fold(part[0]),)+tuple(part[1:])
    dcq,dmk,dmv=attn_bwd(patch_count,q2,k2,v2,o2,gm2,lse2,False,256,2,(half,half),part)
    gmem_local,dcq=tie(gmem(dmk,dmv,w_second),dcq)
    grad_memory=lax.all_to_all(gmem_local.reshape(memory.shape),"mem",split_axis=0,concat_axis=0,tiled=True).astype(f32)
    gh1,gm1,gb1,dg2=mid(h1,gh2,dcq,w_second,gains)
    gb1=r1.fold(gb1)
    second_send,second_keep=wgrads(core,[gb1,n2,mem,gb2],[o1,dcq,dmk,dmv,o2],[(0,0),(1,1),(2,2),(2,3),(3,4)])
    second_send,gm1=tie(second_send,gm1)
    r2=Reduce(second_send,second_keep,here)
    gm1=r1.mem_start(gm1)
    gm1=r2.fold(gm1)
    dq,dk,dv=attn_bwd(table_len,q,k,v,o1,gm1,lse1,True,256,2)
    first_send,first_keep=wgrads(core,[n1],[dq,dk,dv],[(0,0),(0,1),(0,2)])
    r3=Reduce(first_send,first_keep,here)
    dq,first_keep=tie(dq,first_keep)
    dq=r2.fold(dq)
    dq=r3.fold(dq)
    grad_tokens,dg1=first(x,gh1,dq,dk,dv,w_first,gains)
    t_mlp,dg1=r1.mem_sum(dg1)
    dg1=r3.fold(dg1)
    dg1=r2.mem_start(dg1)
    dg1=r3.mem_start(dg1)
    t_second,dg1=r2.mem_sum(dg1)
    t_first,dg1=r3.mem_sum(dg1)
    totals=(t_first,t_second,t_mlp)
    squares=jnp.sum(t_first*t_first)+(jnp.sum(t_second*t_second)+jnp.sum(t_mlp*t_mlp))
    summed=sum_all(jnp.concatenate([dg1,dg2,dg3,jnp.broadcast_to(squares,(1,D))],axis=0),here)
    gain_all=summed[:3]
    grad_norm=jnp.sqrt(summed[3,0]+jnp.sum(gain_all*gain_all))
    factor=CLIP_NORM/jnp.maximum(grad_norm,CLIP_NORM)
    red=[own_rows(t,here) for t in totals]
    attn_red=jnp.concatenate(red[:2],axis=0)
    mlp_red=red[2]
    device=lax.axis_index("seq")*mem_size+lax.axis_index("mem")
    gain_red=lax.dynamic_slice_in_dim(gain_all,device*rows,rows,1)
    a=adam_step(attn_master,attn_red*factor,attn_first,attn_second,RATE_MATRIX,DECAY_MATRIX)
    m=adam_step(mlp_master,mlp_red*factor,mlp_first,mlp_second,RATE_MATRIX,DECAY_MATRIX)
    gn=adam_step(gain_master,gain_red*factor,gain_first,gain_second,RATE_GAIN,0.0)
    return (mixed_out[None],grad_tokens[None],grad_memory,grad_norm)+a+m+gn


def solution(mesh):
    both=P(("seq","mem"),None,None)
    mid_split=P(None,("seq","mem"),None)
    gain_split=P(None,("seq","mem"))
    return jax.shard_map(functools.partial(on_device,mesh.shape["seq"],mesh.shape["mem"]),mesh=mesh,
        in_specs=(both,P("seq","mem",None),both,P(("seq","mem")),P(("seq","mem")))+(mid_split,)*6+(gain_split,)*3,
        out_specs=(both,both,P("seq","mem",None),P())+(mid_split,)*6+(gain_split,)*3,
        check_vma=False)
```

```python
import functools, math
import jax, jax.numpy as jnp
from jax import lax
from jax.sharding import PartitionSpec as P
from jax.experimental import pallas as pl
from jax.experimental.pallas import tpu as pltpu
bf=jnp.bfloat16; f32=jnp.float32
HD=64; HEADS=12
def cost(us):
    return pl.CostEstimate(flops=int(us*1e+10),bytes_accessed=10**5,transcendentals=0)
NEG=-1e30
VA=16*2**20
VB=60*2**20
LOG2E=math.log2(math.e)
TN=(((0,),(0,)),((),())); NN=(((1,),(0,)),((),())); NT=(((1,),(1,)),((),()))
def dg(a,b,dims): return lax.dot_general(a,b,dims,preferred_element_type=f32)
def rows16(cols, width, pad=16):
    idx=lax.broadcasted_iota(jnp.int32,(pad,width),0)
    out=jnp.zeros((pad,width),f32)
    for i,c in enumerate(cols): out=jnp.where(idx==i,c,out)
    return out.astype(bf)
def split3(x):
    hi=x.astype(bf).astype(f32); r=x-hi; mid=r.astype(bf).astype(f32); lo=r-mid
    return hi,mid,lo
def scaled_query(qT):
    s=qT.astype(f32)*(0.125*LOG2E)
    hi=s.astype(bf); lo=(s-hi.astype(f32)).astype(bf)
    return hi,lo


def causal_mask(x,q0,bq,fill):
    ki=lax.broadcasted_iota(jnp.int32,(bq,bq),0); qi=lax.broadcasted_iota(jnp.int32,(bq,bq),1)
    d=jnp.where(ki<=qi,x[q0:],fill)
    return jnp.concatenate([x[:q0],d],axis=0) if q0 else d

def fwd_kernel(len_ref,qT_ref,kT_ref,vT_ref,oT_ref,lse_ref,*,causal,bq,hs):
    L=qT_ref.shape[1]; K=kT_ref.shape[1]
    n=len_ref[0]
    kpos=lax.broadcasted_iota(jnp.int32,(1,K),1)
    kx=rows16([jnp.where(kpos<n,0.0,NEG)],K); qx=rows16([jnp.ones((1,L),f32)],L); vx=rows16([jnp.ones((1,K),f32)],K)
    ops=[]
    for h in range(hs):
        r=slice(h*HD,(h+1)*HD)
        kT=kT_ref[r,:]
        hi,lo=scaled_query(qT_ref[r,:])
        ops.append((jnp.concatenate([kT,kT,kx],axis=0),jnp.concatenate([hi,lo,qx],axis=0),jnp.concatenate([vT_ref[r,:],vx],axis=0)))
    jobs=[(h,q0) for h in range(hs) for q0 in range(0,L,bq)]
    def score(j):
        h,q0=j; ke=min(K,q0+bq) if causal else K
        return dg(ops[h][0][:,:ke],ops[h][1][:,q0:q0+bq],TN)
    nxt=score(jobs[0])
    for i,(h,q0) in enumerate(jobs):
        s=nxt
        if i+1<len(jobs): nxt=score(jobs[i+1])
        ke=s.shape[0]
        if causal: s=causal_mask(s,q0,bq,NEG)
        m=jnp.max(s,axis=0,keepdims=True)
        p=jnp.exp2(s-m).astype(bf)
        o=dg(ops[h][2][:,:ke],p,NN)
        l=o[HD:HD+1]
        oT_ref[h*HD:(h+1)*HD,q0:q0+bq]=(o[:HD]*(1.0/l)).astype(bf)
        lse_ref[h,:,q0:q0+bq]=m+jnp.log2(l)

def head_block(hs,w,offset=0):
    return pl.BlockSpec((hs*HD,w),lambda h:(h+offset//hs,0))
def fwd_part_kernel(*refs,**kw):
    fwd_kernel(*refs[:4],*refs[6:],**kw)
def attn_fwd(n,q,k,v,causal,bq=256,hs=2,part=None,into=None,vmem=VA):
    L=q[0].shape[1]; K=k[0].shape[1]; D=HEADS*HD
    h0,hn=part or (0,HEADS)
    hb=lambda w,o=0: head_block(hs,w,o+h0)
    specs=[pl.BlockSpec(memory_space=pltpu.SMEM),hb(L,q[1]),hb(K,k[1]),hb(K,v[1])]
    args=(n,q[0],k[0],v[0])
    if into is not None:
        specs+=[pl.BlockSpec(memory_space=pl.ANY)]*2
        args+=tuple(into)
    return pl.pallas_call(functools.partial(fwd_kernel if into is None else fwd_part_kernel,causal=causal,bq=bq,hs=hs),grid=(hn//hs,),
      in_specs=specs,
      out_specs=[hb(L),pl.BlockSpec((hs,1,L),lambda h:(h+h0//hs,0,0))],
      out_shape=[jax.ShapeDtypeStruct((D,L),bf),jax.ShapeDtypeStruct((HEADS,1,L),f32)],
      input_output_aliases={} if into is None else {4:0,5:1},
      cost_estimate=cost(0.3),compiler_params=pltpu.CompilerParams(vmem_limit_bytes=vmem),
    )(*args)

def bwd_kernel(len_ref,qT_ref,kT_ref,vT_ref,oT_ref,gT_ref,lse_ref,dq_ref,dk_ref,dv_ref,dka,dva,*,causal,bq,hs):
    L=qT_ref.shape[1]; K=kT_ref.shape[1]
    n=len_ref[0]
    kpos=lax.broadcasted_iota(jnp.int32,(1,K),1)
    bias=jnp.where(kpos<n,0.0,NEG)
    one_k=jnp.ones((1,K),f32)
    kx=rows16([bias,one_k,one_k,one_k],K); vx=rows16([one_k,one_k,one_k],K)
    ops=[]
    for h in range(hs):
        r=slice(h*HD,(h+1)*HD)
        kT=kT_ref[r,:]; qT=qT_ref[r,:]; gT=gT_ref[r,:]
        hi,lo=scaled_query(qT)
        delta=jnp.sum(oT_ref[r,:].astype(f32)*gT.astype(f32),axis=0,keepdims=True)
        ops.append(dict(k=kT,q=qT,g=gT,kaug=jnp.concatenate([kT,kT,kx],axis=0),
          qaug=jnp.concatenate([hi,lo,rows16([jnp.ones((1,L),f32),*split3(-lse_ref[h])],L)],axis=0),
          vaug=jnp.concatenate([vT_ref[r,:],vx],axis=0),
          gaug=jnp.concatenate([gT,rows16(list(split3(-delta)),L)],axis=0)))
    jobs=[(h,q0) for h in range(hs) for q0 in reversed(range(0,L,bq))]
    def score(j):
        h,q0=j; ke=min(K,q0+bq) if causal else K; sl=slice(q0,q0+bq); o=ops[h]
        return dg(o["kaug"][:,:ke],o["qaug"][:,sl],TN),dg(o["vaug"][:,:ke],o["gaug"][:,sl],TN)
    nxt=score(jobs[0])
    for i,(h,q0) in enumerate(jobs):
        s,dp=nxt
        if i+1<len(jobs): nxt=score(jobs[i+1])
        ke=s.shape[0]; sl=slice(q0,q0+bq); o=ops[h]; r=slice(h*HD,(h+1)*HD)
        p=jnp.exp2(s)
        if causal: p=causal_mask(p,q0,bq,0.0)
        ds=(p*dp).astype(bf)
        pb=p.astype(bf)
        dq_ref[r,sl]=(dg(o["k"][:,:ke],ds,NN)*0.125).astype(bf)
        dv=dg(o["g"][:,sl],pb,NT)
        dk=dg(o["q"][:,sl],ds,NT)
        if q0==L-bq:
            dka[r]=dk; dva[r]=dv
        else:
            dka[r,:ke]+=dk; dva[r,:ke]+=dv
    dk_ref[...]=(dka[...]*0.125).astype(bf)
    dv_ref[...]=dva[...].astype(bf)

def bwd_part_kernel(*refs,**kw):
    bwd_kernel(*refs[:7],*refs[10:],**kw)
def attn_bwd(n,q,k,v,oT,gT,lse,causal,bq=256,hs=2,part=None,into=None):
    L=q[0].shape[1]; K=k[0].shape[1]; D=HEADS*HD
    h0,hn=part or (0,HEADS)
    hb=lambda w,o=0: head_block(hs,w,o+h0)
    S=jax.ShapeDtypeStruct
    specs=[pl.BlockSpec(memory_space=pltpu.SMEM),hb(L,q[1]),hb(K,k[1]),hb(K,v[1]),hb(L),hb(L),pl.BlockSpec((hs,1,L),lambda h:(h+h0//hs,0,0))]
    args=(n,q[0],k[0],v[0],oT,gT,lse)
    if into is not None:
        specs+=[pl.BlockSpec(memory_space=pl.ANY)]*3
        args+=tuple(into)
    return pl.pallas_call(functools.partial(bwd_kernel if into is None else bwd_part_kernel,causal=causal,bq=bq,hs=hs),grid=(hn//hs,),
      in_specs=specs,out_specs=[hb(L),hb(K),hb(K)],
      out_shape=[S((D,L),bf),S((D,K),bf),S((D,K),bf)],
      input_output_aliases={} if into is None else {7:0,8:1,9:2},
      scratch_shapes=[pltpu.VMEM((hs*HD,K),f32),pltpu.VMEM((hs*HD,K),f32)],
      cost_estimate=cost(14),compiler_params=pltpu.CompilerParams(vmem_limit_bytes=VA),
    )(*args)

TT=(((0,),(1,)),((),()))
EPS=1e-6
VL=60*2**20
def cp(mb=24): return pltpu.CompilerParams(vmem_limit_bytes=mb*2**20)
def full(shape): return pl.BlockSpec(shape,lambda i:(0,)*len(shape))
GC=0.7978845608028654

def rms_r(v): return lax.rsqrt(jnp.mean(v*v,axis=-1,keepdims=True)+EPS)

def wcol(D,j): return pl.BlockSpec((D,D),lambda i:(0,j))
def gain_spec(D): return pl.BlockSpec((8,D),lambda i:(0,0))

def proj_kernel(x_ref,e_ref,w_ref,n_ref,yT_ref,g_ref):
    @pl.when(pl.program_id(0)==0)
    def _():
        g=e_ref[...].astype(f32).T[0:8,:]
        g_ref[...]=g
        x=x_ref[...].astype(f32)
        n_ref[...]=(x*rms_r(x)*g[0:1,:]).astype(bf)
    yT_ref[...]=dg(w_ref[...],n_ref[...],TT).astype(bf)
def norm_proj(x,w,fb=384):
    L,D=x.shape; F=3*D
    return pl.pallas_call(proj_kernel,grid=(F//fb,),
      in_specs=[full((L,D)),pl.BlockSpec((D,128),lambda i:(0,F//128)),pl.BlockSpec((D,fb),lambda i:(0,i))],
      out_specs=[full((L,D)),pl.BlockSpec((fb,L),lambda i:(i,0)),gain_spec(D)],
      out_shape=[jax.ShapeDtypeStruct((L,D),bf),jax.ShapeDtypeStruct((F,L),bf),jax.ShapeDtypeStruct((8,D),f32)],cost_estimate=cost(6),compiler_params=cp())(x,w,w)
def memproj_kernel(x_ref,w_ref,yT_ref):
    yT_ref[...]=dg(w_ref[...],x_ref[...],TT).astype(bf)
def mem_proj(x,w,first_col,fb=384):
    L,D=x.shape; F=2*D
    return pl.pallas_call(memproj_kernel,grid=(F//fb,),
      in_specs=[full((L,D)),pl.BlockSpec((D,fb),lambda i:(0,first_col//fb+i))],
      out_specs=pl.BlockSpec((fb,L),lambda i:(i,0)),
      out_shape=jax.ShapeDtypeStruct((F,L),bf),cost_estimate=cost(0.1),compiler_params=cp())(x,w)

def post_self_kernel(x_ref,oT_ref,w3_ref,w4_ref,g_ref,h_ref,n_ref,cT_ref):
    h=x_ref[...].astype(f32)+dg(oT_ref[...],w3_ref[...],TT)
    h_ref[...]=h
    n=(h*rms_r(h)*g_ref[1:2,:]).astype(bf)
    n_ref[...]=n
    cT_ref[...]=dg(n,w4_ref[...],NN).astype(bf).T
def post_self(x,oT,w,g,tb=256):
    L,D=x.shape
    tok=pl.BlockSpec((tb,D),lambda i:(i,0)); tokT=pl.BlockSpec((D,tb),lambda i:(0,i))
    return pl.pallas_call(post_self_kernel,grid=(L//tb,),
      in_specs=[tok,tokT,wcol(D,0),wcol(D,1),gain_spec(D)],
      out_specs=[tok,tok,tokT],
      out_shape=[jax.ShapeDtypeStruct((L,D),f32),jax.ShapeDtypeStruct((L,D),bf),jax.ShapeDtypeStruct((D,L),bf)],cost_estimate=cost(0.3),compiler_params=cp())(x,oT,w,w,g)

def mlp_chunk(n3,gb,wg,wu,wd,dw_ref,inner_s,dgate_s,dup_s,oacc,nacc,tb):
    L=n3.shape[0]; nt=L//tb
    def pre(t):
        sl=slice(t*tb,(t+1)*tb)
        a=n3[sl,:]
        return dg(a,wg(),NN),dg(a,wu(),NN),dg(gb[sl,:],wd(),NN)
    nxt=pre(0)
    for t in range(nt):
        sl=slice(t*tb,(t+1)*tb)
        g,u,di=nxt
        if t+1<nt: nxt=pre(t+1)
        g2=g*g
        th=jnp.tanh(g*(GC+(GC*0.044715)*g2))
        hp=0.5+0.5*th
        ge=g*hp
        dge=hp+(0.5*g)*(1.0-th*th)*(GC+(3*GC*0.044715)*g2)
        inner=(ge*u).astype(bf)
        dgate=(di*u*dge).astype(bf)
        dup=(di*ge).astype(bf)
        inner_s[sl,:]=inner; dgate_s[sl,:]=dgate; dup_s[sl,:]=dup
        oacc[sl,:]+=dg(inner,wd(),NT)
        nacc[sl,:]+=dg(dgate,wg(),NT)+dg(dup,wu(),NT)
    dw_ref[0]=dg(n3[...],dgate_s[...],TN).astype(bf)
    dw_ref[1]=dg(n3[...],dup_s[...],TN).astype(bf)
    dw_ref[2]=dg(gb[...],inner_s[...],TN).astype(bf)

def mlp_kernel(core_ref,index_ref,len_ref,h1_ref,oT_ref,w7_ref,cot_ref,g_ref,*refs,tb,pieces):
    w_refs=refs[:pieces]
    (out_ref,gh_ref,gmT_ref,gb2_ref,dg_ref,send_ref,keep_ref,
     h2,n3,gb,oacc,nacc,dw,inner_s,dgate_s,dup_s,sems,w,wsems)=refs[pieces:]
    L,D=h1_ref.shape
    F=w_refs[0].shape[1]//3
    fc=dw.shape[3]
    i=pl.program_id(0); count=pl.num_programs(0); half=count//2
    slot=lax.rem(i,2)
    def copy(step,to):
        col=pl.multiple_of(lax.rem(step,half)*fc,fc)
        return pltpu.make_async_copy(dw.at[lax.rem(step,2)],to.at[:,:,pl.ds(col,fc)],sems.at[lax.rem(step,2)])
    def weights(step):
        chunk=lax.rem(step+(1-core_ref[0])*half,count)
        to=lax.rem(step,2)
        return [pltpu.make_async_copy(w_refs[p].at[:,pl.ds(pl.multiple_of(j*F+chunk*fc,fc),fc)],w.at[to,j,index_ref[p]],wsems.at[to,j*pieces+p])
                for j in range(3) for p in range(pieces)]
    @pl.when(i==0)
    def _():
        for c in weights(0): c.start()
    @pl.when(i+1<count)
    def _():
        for c in weights(i+1): c.start()
    @pl.when(i==0)
    def _():
        n=len_ref[0]
        for t in range(L//tb):
            sl=slice(t*tb,(t+1)*tb)
            h=h1_ref[sl,:]+dg(oT_ref[:,sl],w7_ref[...],TT)
            h2[sl,:]=h
            oacc[sl,:]=h
            nacc[sl,:]=jnp.zeros((tb,D),f32)
            n3[sl,:]=(h*rms_r(h)*g_ref[2:3,:]).astype(bf)
            row=t*tb+lax.broadcasted_iota(jnp.int32,(tb,1),0)
            gb[sl,:]=jnp.where(row<n,cot_ref[sl,:].astype(f32),0.0).astype(bf)
    @pl.when(i>=2)
    def _():
        copy(i-2,send_ref).wait()
    for c in weights(i): c.wait()
    wv=[lambda j=j: w[slot,j].reshape(D,fc) for j in range(3)]
    mlp_chunk(n3,gb,wv[0],wv[1],wv[2],dw.at[slot],inner_s,dgate_s,dup_s,oacc,nacc,tb)
    @pl.when(i<half)
    def _():
        copy(i,send_ref).start()
    @pl.when(i>=half)
    def _():
        copy(i,keep_ref).start()
    @pl.when(i==count-1)
    def _():
        acc=jnp.zeros((1,D),f32)
        for t in range(L//tb):
            sl=slice(t*tb,(t+1)*tb)
            h=h2[sl,:]; uu=nacc[sl,:]
            out_ref[sl,:]=oacc[sl,:].astype(bf)
            r=rms_r(h); ug=uu*g_ref[2:3,:]
            gh=gb[sl,:].astype(f32)+r*ug-h*((r*r*r)*jnp.mean(ug*h,axis=-1,keepdims=True))
            acc=acc+jnp.sum(uu*h*r,axis=0,keepdims=True)
            gh_ref[sl,:]=gh
            b=gh.astype(bf)
            gb2_ref[sl,:]=b
            gmT_ref[:,sl]=dg(b,w7_ref[...],NN).astype(bf).T
        dg_ref[...]=acc
        copy(i-1,keep_ref).wait()
        copy(i,keep_ref).wait()
def mlp(core,index,n,h1,oT,w_second,cot,g,parts,fc=512,tb=256):
    L,D=h1.shape; F=parts[0].shape[1]//3; nc=F//fc; count=len(parts)
    whole=lambda shape: pl.BlockSpec(shape,lambda i,c,x:(0,)*len(shape),pipeline_mode=pl.Buffered(1))
    S=jax.ShapeDtypeStruct
    hbm=pl.BlockSpec(memory_space=pl.ANY)
    return pl.pallas_call(functools.partial(mlp_kernel,tb=tb,pieces=count),
      grid_spec=pltpu.PrefetchScalarGridSpec(num_scalar_prefetch=2,grid=(nc,),
      in_specs=[pl.BlockSpec(memory_space=pltpu.SMEM),whole((L,D)),whole((D,L)),pl.BlockSpec((D,D),lambda i,c,x:(0,4),pipeline_mode=pl.Buffered(1)),whole((L,D)),whole((8,D))]+[hbm]*count,
      out_specs=[whole((L,D)),whole((L,D)),whole((D,L)),whole((L,D)),whole((1,D)),hbm,hbm],
      scratch_shapes=[pltpu.VMEM((L,D),f32),pltpu.VMEM((L,D),bf),pltpu.VMEM((L,D),bf),pltpu.VMEM((L,D),f32),pltpu.VMEM((L,D),f32),
        pltpu.VMEM((2,3,D,fc),bf),pltpu.VMEM((L,fc),bf),pltpu.VMEM((L,fc),bf),pltpu.VMEM((L,fc),bf),pltpu.SemaphoreType.DMA((2,)),
        pltpu.VMEM((2,3,count,D//count,fc),bf),pltpu.SemaphoreType.DMA((2,3*count))]),
      out_shape=[S((L,D),bf),S((L,D),f32),S((D,L),bf),S((L,D),bf),S((1,D),f32),S((3,D,F//2),bf),S((3,D,F//2),bf)],
      cost_estimate=cost(42),compiler_params=cp(48))(core,index,n,h1,oT,w_second,cot,g,*parts)

def mid_kernel(h1_ref,gh2_ref,dcT_ref,w4_ref,w3_ref,g_ref,gh1_ref,gmT_ref,gb_ref,dg_ref):
    i=pl.program_id(0)
    u=dg(dcT_ref[...],w4_ref[...],TT)
    h=h1_ref[...]
    r=rms_r(h); ug=u*g_ref[1:2,:]
    gh=gh2_ref[...]+r*ug-h*((r*r*r)*jnp.mean(ug*h,axis=-1,keepdims=True))
    gh1_ref[...]=gh
    b=gh.astype(bf)
    gb_ref[...]=b
    gmT_ref[...]=dg(b,w3_ref[...],NN).astype(bf).T
    s=jnp.sum(u*h*r,axis=0,keepdims=True)
    @pl.when(i==0)
    def _(): dg_ref[...]=s
    @pl.when(i>0)
    def _(): dg_ref[...]+=s
def mid(h1,gh2,dcT,w,g,tb=256):
    L,D=h1.shape
    tok=pl.BlockSpec((tb,D),lambda i:(i,0)); tokT=pl.BlockSpec((D,tb),lambda i:(0,i))
    S=jax.ShapeDtypeStruct
    return pl.pallas_call(mid_kernel,grid=(L//tb,),
      in_specs=[tok,tok,tokT,wcol(D,1),wcol(D,0),gain_spec(D)],
      out_specs=[tok,tokT,tok,full((1,D))],
      out_shape=[S((L,D),f32),S((D,L),bf),S((L,D),bf),S((1,D),f32)],cost_estimate=cost(0.2),compiler_params=cp())(h1,gh2,dcT,w,w,g)

def wgrads_kernel(core_ref,*refs,pairs,na,ng):
    a_refs=refs[:na]; g_refs=refs[na:na+ng]; send_ref,keep_ref=refs[na+ng:]
    k=core_ref[0]
    W=send_ref.shape[2]
    for out,half in ((send_ref,1-k),(keep_ref,k)):
        start=pl.multiple_of(half*W,W)
        for m,(ia,ig) in enumerate(pairs):
            out[m]=dg(a_refs[ia][...],g_refs[ig][pl.ds(start,W),:],TT).astype(bf)
def wgrads(core,a,g,pairs):
    D=a[0].shape[1]; F=g[0].shape[0]
    v=pl.BlockSpec(memory_space=pltpu.VMEM)
    S=jax.ShapeDtypeStruct((len(pairs),D,F//2),bf)
    return pl.pallas_call(functools.partial(wgrads_kernel,pairs=tuple(pairs),na=len(a),ng=len(g)),
      in_specs=[pl.BlockSpec(memory_space=pltpu.SMEM)]+[v]*(len(a)+len(g)),out_specs=[v,v],
      out_shape=[S,S],cost_estimate=cost(8),compiler_params=cp(40))(core,*a,*g)

def gmem_kernel(kT_ref,vT_ref,w5_ref,w6_ref,o_ref):
    o_ref[...]=(dg(kT_ref[...],w5_ref[...],TT)+dg(vT_ref[...],w6_ref[...],TT)).astype(bf)
def gmem(kT,vT,w56,tb=256):
    D,L=kT.shape
    tokT=pl.BlockSpec((D,tb),lambda i:(0,i))
    return pl.pallas_call(gmem_kernel,grid=(L//tb,),
      in_specs=[tokT,tokT,wcol(D,2),wcol(D,3)],
      out_specs=pl.BlockSpec((tb,D),lambda i:(i,0)),
      out_shape=jax.ShapeDtypeStruct((L,D),bf),cost_estimate=cost(0.2),compiler_params=cp())(kT,vT,w56,w56)

def first_kernel(x_ref,gh1_ref,qT_ref,kT_ref,vT_ref,w0_ref,w1_ref,w2_ref,g_ref,gt_ref,dg_ref):
    i=pl.program_id(0)
    u=dg(qT_ref[...],w0_ref[...],TT)+dg(kT_ref[...],w1_ref[...],TT)+dg(vT_ref[...],w2_ref[...],TT)
    h=x_ref[...].astype(f32)
    r=rms_r(h); ug=u*g_ref[0:1,:]
    gt_ref[...]=gh1_ref[...]+r*ug-h*((r*r*r)*jnp.mean(ug*h,axis=-1,keepdims=True))
    s=jnp.sum(u*h*r,axis=0,keepdims=True)
    @pl.when(i==0)
    def _(): dg_ref[...]=s
    @pl.when(i>0)
    def _(): dg_ref[...]+=s
def first(x,gh1,qT,kT,vT,w,g,tb=256):
    L,D=x.shape
    tok=pl.BlockSpec((tb,D),lambda i:(i,0)); tokT=pl.BlockSpec((D,tb),lambda i:(0,i))
    S=jax.ShapeDtypeStruct
    wb=lambda j: pl.BlockSpec((D,D),lambda i,j=j:(0,j))
    return pl.pallas_call(first_kernel,grid=(L//tb,),
      in_specs=[tok,tok,tokT,tokT,tokT,wb(0),wb(1),wb(2),gain_spec(D)],
      out_specs=[tok,full((1,D))],
      out_shape=[S((L,D),f32),S((1,D),f32)],cost_estimate=cost(7),compiler_params=cp())(x,gh1,qT,kT,vT,w,w,w,g)

SEQ="seq"
MEM="mem"


def plane_bits(seq_size):
    return max(0,(seq_size//2).bit_length()-1)


def bit_order(core,bits):
    order=list(range(1,bits+1))
    return order if core==0 else order[::-1]


def subset_mask(core,subset,bits):
    order=bit_order(core,bits)
    mask=0
    for p in range(bits):
        if subset>>p&1:
            mask^=1<<(order[p]-1)
    return mask


def cross(x,position,seq_size):
    bits=plane_bits(seq_size)
    perm=[(s,s^(1<<bit_order(s&1,bits)[position])) for s in range(seq_size)]
    return lax.ppermute(x,SEQ,perm)


def swap_core(x,seq_size):
    return lax.ppermute(x,SEQ,[(s,s^1) for s in range(seq_size)])


def shift_mem(x,step,mem_size):
    return lax.ppermute(x,MEM,[(z,(z+step)%mem_size) for z in range(mem_size)])


def copy_kernel(index_ref,*refs,places,columns):
    count=len(places)
    sources=refs[:count]; out=refs[count]; sems=refs[count+1]
    copies=[]
    for j,(source,place) in enumerate(zip(sources,places)):
        if columns is not None:
            source=source.at[:,pl.ds(columns[0],columns[1]-columns[0])]
        copies.append(pltpu.make_async_copy(source,out.at[index_ref[place]],sems.at[j]))
        copies[-1].start()
    for c in copies:
        c.wait()


def place_rows(index,pieces,places,slots,us,columns=None):
    piece=pieces[0]
    shape=piece.shape if columns is None else (piece.shape[0],columns[1]-columns[0])
    return pl.pallas_call(functools.partial(copy_kernel,places=tuple(places),columns=columns),
        in_specs=[pl.BlockSpec(memory_space=pltpu.SMEM)]+[pl.BlockSpec(memory_space=pl.ANY)]*len(pieces),
        out_specs=pl.BlockSpec(memory_space=pltpu.VMEM),
        out_shape=jax.ShapeDtypeStruct((slots,)+shape,piece.dtype),
        scratch_shapes=[pltpu.SemaphoreType.DMA((len(pieces),))],
        cost_estimate=cost(us),compiler_params=cp(20),
    )(index,*pieces)


class Place:
    def __init__(self,seq_size,mem_size):
        self.S=seq_size; self.M=mem_size; self.bits=plane_bits(seq_size); self.NP=seq_size//2
        s=lax.axis_index(SEQ); self.z=lax.axis_index(MEM)
        self.core=s%2; self.plane=s//2

    def slab(self,subset,own=True):
        m0=subset_mask(0,subset,self.bits); m1=subset_mask(1,subset,self.bits)
        c=self.core if own else 1-self.core
        return self.plane^jnp.where(c==0,m0,m1)


def gather_mem_direct(shard,pl_):
    M=pl_.M
    pieces=[shard]+[shift_mem(shard,j,M) for j in range(1,M)]
    index=jnp.stack([(pl_.z-j)%M for j in range(M)]).astype(jnp.int32)
    return place_rows(index,pieces,range(M),M,3).reshape(M*shard.shape[0],shard.shape[1])


def gather_mem_exchange(shard,here):
    M=here.M
    copies=jnp.broadcast_to(shard[None],(M,)+shard.shape)
    return lax.all_to_all(copies,MEM,split_axis=0,concat_axis=0,tiled=True).reshape(M*shard.shape[0],shard.shape[1])


def tie(*values):
    return lax.optimization_barrier(values)


class Ring:
    def __init__(self,shard,here):
        self.here=here; self.got=[shard]
        self.next()

    def next(self):
        if len(self.got)<self.here.M:
            self.got.append(shift_mem(self.got[-1],1,self.here.M))

    def step(self,dep):
        self.got[-1],dep=tie(self.got[-1],dep)
        self.next()
        return dep

    def finish(self,dep):
        while len(self.got)<self.here.M:
            self.next()
        self.got[-1],dep=tie(self.got[-1],dep)
        return dep

    def place(self,first,end):
        M=self.here.M
        index=jnp.stack([(self.here.z-j)%M for j in range(M)]).astype(jnp.int32)
        rows=self.got[0].shape[0]
        return place_rows(index,self.got,range(M),M,0.05,(first,end)).reshape(M*rows,end-first)


class Gather:
    def __init__(self,slab,here):
        self.here=here; self.pieces={0:slab}; self.other={}
        for p in range(here.bits):
            self.pieces[1<<p]=cross(slab,p,here.S)

    def arrived(self,dep,keys=None):
        keys=sorted(self.pieces) if keys is None else keys
        others=sorted(self.other)
        out=tie(*[self.pieces[s] for s in keys],*[self.other[s] for s in others],dep)
        self.pieces.update(zip(keys,out)); self.other.update(zip(others,out[len(keys):]))
        return out[-1]

    def forward(self):
        here=self.here
        for subset in range(1,here.NP):
            top=subset.bit_length()-1
            if subset not in self.pieces:
                self.pieces[subset]=cross(self.pieces[subset^(1<<top)],top,here.S)

    def swap(self):
        for subset in sorted(self.pieces):
            if subset not in self.other and subset!=self.here.NP-1:
                self.other[subset]=swap_core(self.pieces[subset],self.here.S)

    def swap_last(self):
        end=self.here.NP-1
        if end not in self.other:
            self.other[end]=swap_core(self.pieces[end],self.here.S)

    def parts(self):
        here=self.here
        n=here.NP
        idx=[here.slab(s)*2+here.core for s in range(n)]+[here.slab(s,False)*2+1-here.core for s in range(n)]
        index=jnp.stack(idx).astype(jnp.int32)
        parts=[self.pieces[s] for s in range(n)]+[self.other[s] for s in range(n)]
        return index,parts

    def place(self):
        index,parts=self.parts()
        out=place_rows(index,parts,range(len(parts)),len(parts),0.05)
        return out.reshape(-1,parts[0].shape[1])


def fold_kernel(index_ref,ka,kb,ra,rb,send,keep):
    send[...]=(kb[...].astype(f32)+rb[...].astype(f32)).astype(bf)
    keep[...]=(ka[...].astype(f32)+ra[...].astype(f32)).astype(bf)


def fold(index,keep,recv):
    G,n,R,W=keep.shape; h=n//2
    low=pl.BlockSpec((1,1,R,W),lambda i,m,ix:(m,ix[i],0,0))
    high=pl.BlockSpec((1,1,R,W),lambda i,m,ix:(m,ix[h+i],0,0))
    out=pl.BlockSpec((1,1,R,W),lambda i,m,ix:(m,i,0,0))
    S=jax.ShapeDtypeStruct((G,h,R,W),bf)
    return pl.pallas_call(fold_kernel,
        grid_spec=pltpu.PrefetchScalarGridSpec(num_scalar_prefetch=1,grid=(h,G),in_specs=[low,high,low,high],out_specs=[out,out]),
        out_shape=[S,S],cost_estimate=cost(3),compiler_params=cp(16))(index,keep,keep,recv,recv)


def split_kernel(index_ref,a,b,*outs):
    for j,o in enumerate(outs):
        z=index_ref[j]
        o[...]=(a[:,:,pl.ds(z,1)].astype(f32)+b[:,:,pl.ds(z,1)].astype(f32)).astype(bf)


def split_mem(index,a,b):
    G,two,M,r,W=a.shape
    full_=pl.BlockSpec(memory_space=pltpu.VMEM)
    S=jax.ShapeDtypeStruct((G,two,1,r,W),bf)
    return pl.pallas_call(split_kernel,in_specs=[pl.BlockSpec(memory_space=pltpu.SMEM),full_,full_],out_specs=[full_]*M,
        out_shape=[S]*M,cost_estimate=cost(2),compiler_params=cp(16))(index,a,b)


def order_kernel(a,b,o):
    for z in range(o.shape[0]):
        o[z]=(a[:,:,z].astype(f32)+b[:,:,z].astype(f32)).astype(bf)


def order_mem(a,b):
    G,two,M,r,W=a.shape
    v=pl.BlockSpec(memory_space=pltpu.VMEM)
    return pl.pallas_call(order_kernel,in_specs=[v,v],out_specs=v,
        out_shape=jax.ShapeDtypeStruct((M,G,two,r,W),bf),cost_estimate=cost(2),compiler_params=cp(16))(a,b)


class Reduce:
    def __init__(self,send,keep,here):
        G,D,W=send.shape
        NP=here.NP; R=D//NP
        self.here=here; self.r=R//2//here.M
        self.recv=swap_core(send,here.S).reshape(G,NP,R,W)
        self.keep=keep.reshape(G,NP,R,W)
        self.index=jnp.stack([here.slab(s) for s in range(NP)]).astype(jnp.int32)
        self.p=here.bits-1

    def fold(self,dep):
        self.recv,dep=tie(self.recv,dep)
        if self.p<0:
            return dep
        go,keep=fold(self.index,self.keep,self.recv)
        go,self.keep,dep=tie(go,keep,dep)
        self.recv=cross(go,self.p,self.here.S)
        self.index=jnp.arange(1<<self.p,dtype=jnp.int32)
        self.p-=1
        return dep

    def halves(self,dep):
        while self.p>=0:
            dep=self.fold(dep)
        self.recv,dep=tie(self.recv,dep)
        G,_,R,W=self.keep.shape
        shape=(G,2,self.here.M,self.r,W)
        return self.keep.reshape(shape),self.recv.reshape(shape),dep

    def over_mem(self,dep):
        a,b,dep=self.halves(dep)
        parts,dep=tie(order_mem(a,b),dep)
        return lax.psum_scatter(parts,MEM,scatter_dimension=0,tiled=True)[0],dep

    def mem_start(self,dep):
        a,b,dep=self.halves(dep)
        M=self.here.M
        parts=split_mem(jnp.stack([(self.here.z+j)%M for j in range(M)]).astype(jnp.int32),a,b)
        out=tie(*parts,dep)
        parts,dep=out[:-1],out[-1]
        self.got=[parts[0]]+[shift_mem(parts[j],j,M) for j in range(1,M)]
        return dep

    def mem_sum(self,dep):
        out=tie(*self.got,dep)
        total=out[0].astype(f32)
        for p in out[1:-1]:
            total=total+p.astype(f32)
        G,_,_,r,W=total.shape
        return total.reshape(G,2,r,W),out[-1]


def own_rows(total,pl_):
    give=lax.dynamic_index_in_dim(total,1-pl_.core,1,keepdims=False)
    own=lax.dynamic_index_in_dim(total,pl_.core,1,keepdims=False)
    other=swap_core(give,pl_.S)
    low=jnp.where(pl_.core==0,own,other); high=jnp.where(pl_.core==0,other,own)
    return jnp.concatenate([low,high],axis=-1)


def sum_all(x,pl_):
    for b in range(pl_.S.bit_length()-1):
        x=x+lax.ppermute(x,SEQ,[(s,s^(1<<b)) for s in range(pl_.S)])
    for b in range(pl_.M.bit_length()-1):
        x=x+lax.ppermute(x,MEM,[(z,z^(1<<b)) for z in range(pl_.M)])
    return x

STEP=10
CLIP_NORM=1.0
BETA_FIRST=0.9
BETA_SECOND=0.999
ADAM_EPSILON=1e-08
RATE_MATRIX=0.06
RATE_GAIN=0.6
DECAY_MATRIX=0.01


def adam_step(master,grad,first_moment,second_moment,rate,decay):
    first_new=BETA_FIRST*first_moment+(1.0-BETA_FIRST)*grad
    second_new=BETA_SECOND*second_moment+(1.0-BETA_SECOND)*grad*grad
    first_hat=first_new/(1.0-BETA_FIRST**STEP)
    second_hat=second_new/(1.0-BETA_SECOND**STEP)
    master_new=master-rate*(first_hat/(jnp.sqrt(second_hat)+ADAM_EPSILON)+decay*master)
    return (master_new,first_new,second_new)


def columns(stack):
    return jnp.concatenate([stack[i] for i in range(stack.shape[0])],axis=1)


def on_device(seq_size,mem_size,tokens,memory,cotangent,table_len,patch_count,attn_master,attn_first,attn_second,mlp_master,mlp_first,mlp_second,gain_master,gain_first,gain_second):
    here=Place(seq_size,mem_size)
    core=here.core.reshape(1).astype(jnp.int32)
    rows,D=attn_master.shape[1:]
    aw=attn_master.astype(bf)
    gain_cols=jnp.pad(gain_master.T,((0,0),(0,125))).astype(bf)
    x=tokens[0]
    slab=gather_mem_direct(jnp.concatenate([columns(aw[:3]),gain_cols],axis=1),here)
    later=jnp.concatenate([columns(aw[3:]),columns(mlp_master.astype(bf))],axis=1)
    slab,later=tie(slab,later)
    g1=Gather(slab,here)
    ring=Ring(later,here)
    g1.forward()
    g1.pieces[2]=ring.step(g1.pieces[2])
    x=g1.arrived(x)
    g1.swap(); g1.swap_last()
    g1.other[here.NP-1]=ring.step(g1.other[here.NP-1])
    g1.other[here.NP-1],memory=tie(g1.other[here.NP-1],memory)
    mem=lax.all_to_all(memory,"mem",split_axis=0,concat_axis=0,tiled=True).reshape(-1,D)
    w_first=g1.place()
    n1,qkv,gains=norm_proj(x,w_first)
    qkv=ring.finish(qkv)
    g2=Gather(ring.place(0,5*D),here)
    slab_mlp=ring.place(5*D,later.shape[1])
    q,k,v=(qkv,0),(qkv,HEADS),(qkv,2*HEADS)
    o1,lse1=attn_fwd(table_len,q,k,v,True,512,4,(0,8))
    o1=g2.arrived(o1)
    g2.forward(); g2.swap()
    o1,slab_mlp=tie(o1,slab_mlp)
    g3=Gather(slab_mlp,here)
    o1,lse1=attn_fwd(table_len,q,k,v,True,512,4,(8,4),(o1,lse1))
    o1=g2.arrived(o1)
    g2.swap_last()
    w_second=g2.place()
    w_second,mem=tie(w_second,mem)
    mkv=mem_proj(mem,w_second,2*D)
    mkv,o1=tie(mkv,o1)
    o1=g3.arrived(o1)
    g3.forward(); g3.swap()
    h1,n2,cq=post_self(x,o1,w_second,gains)
    q2,k2,v2=(cq,0),(mkv,0),(mkv,HEADS)
    half=HEADS//2
    o2,lse2=attn_fwd(patch_count,q2,k2,v2,False,512,2,(0,half),None,VB)
    o2=g3.arrived(o2)
    g3.swap_last()
    o2,lse2=attn_fwd(patch_count,q2,k2,v2,False,512,2,(half,half),(o2,lse2),VB)
    o2=g3.arrived(o2)
    w_index,w_parts=g3.parts()
    mixed_out,gh2,gm2,gb2,dg3,mlp_send,mlp_keep=mlp(core,w_index,table_len,h1,o2,w_second,cotangent[0],gains,w_parts)
    r1=Reduce(mlp_send,mlp_keep,here)
    part=attn_bwd(patch_count,q2,k2,v2,o2,gm2,lse2,False,256,2,(0,half))
    part=(r1.fold(part[0]),)+tuple(part[1:])
    dcq,dmk,dmv=attn_bwd(patch_count,q2,k2,v2,o2,gm2,lse2,False,256,2,(half,half),part)
    gmem_local,dcq=tie(gmem(dmk,dmv,w_second),dcq)
    grad_memory=lax.all_to_all(gmem_local.reshape(memory.shape),"mem",split_axis=0,concat_axis=0,tiled=True).astype(f32)
    gh1,gm1,gb1,dg2=mid(h1,gh2,dcq,w_second,gains)
    gb1=r1.fold(gb1)
    second_send,second_keep=wgrads(core,[gb1,n2,mem,gb2],[o1,dcq,dmk,dmv,o2],[(0,0),(1,1),(2,2),(2,3),(3,4)])
    second_send,gm1=tie(second_send,gm1)
    r2=Reduce(second_send,second_keep,here)
    gm1=r1.mem_start(gm1)
    gm1=r2.fold(gm1)
    dq,dk,dv=attn_bwd(table_len,q,k,v,o1,gm1,lse1,True,256,2)
    first_send,first_keep=wgrads(core,[n1],[dq,dk,dv],[(0,0),(0,1),(0,2)])
    r3=Reduce(first_send,first_keep,here)
    dq,first_keep=tie(dq,first_keep)
    dq=r2.fold(dq)
    dq=r3.fold(dq)
    grad_tokens,dg1=first(x,gh1,dq,dk,dv,w_first,gains)
    t_mlp,dg1=r1.mem_sum(dg1)
    dg1=r3.fold(dg1)
    dg1=r2.mem_start(dg1)
    dg1=r3.mem_start(dg1)
    t_second,dg1=r2.mem_sum(dg1)
    t_first,dg1=r3.mem_sum(dg1)
    totals=(t_first,t_second,t_mlp)
    squares=jnp.sum(t_first*t_first)+(jnp.sum(t_second*t_second)+jnp.sum(t_mlp*t_mlp))
    summed=sum_all(jnp.concatenate([dg1,dg2,dg3,jnp.broadcast_to(squares,(1,D))],axis=0),here)
    gain_all=summed[:3]
    grad_norm=jnp.sqrt(summed[3,0]+jnp.sum(gain_all*gain_all))
    factor=CLIP_NORM/jnp.maximum(grad_norm,CLIP_NORM)
    red=[own_rows(t,here) for t in totals]
    attn_red=jnp.concatenate(red[:2],axis=0)
    mlp_red=red[2]
    device=lax.axis_index("seq")*mem_size+lax.axis_index("mem")
    gain_red=lax.dynamic_slice_in_dim(gain_all,device*rows,rows,1)
    a=adam_step(attn_master,attn_red*factor,attn_first,attn_second,RATE_MATRIX,DECAY_MATRIX)
    m=adam_step(mlp_master,mlp_red*factor,mlp_first,mlp_second,RATE_MATRIX,DECAY_MATRIX)
    gn=adam_step(gain_master,gain_red*factor,gain_first,gain_second,RATE_GAIN,0.0)
    return (mixed_out[None],grad_tokens[None],grad_memory,grad_norm)+a+m+gn


def solution(mesh):
    both=P(("seq","mem"),None,None)
    mid_split=P(None,("seq","mem"),None)
    gain_split=P(None,("seq","mem"))
    return jax.shard_map(functools.partial(on_device,mesh.shape["seq"],mesh.shape["mem"]),mesh=mesh,
        in_specs=(both,P("seq","mem",None),both,P(("seq","mem")),P(("seq","mem")))+(mid_split,)*6+(gain_split,)*3,
        out_specs=(both,both,P("seq","mem",None),P())+(mid_split,)*6+(gain_split,)*3,
        check_vma=False)
```

```python
import functools, math
import jax, jax.numpy as jnp
from jax import lax
from jax.sharding import PartitionSpec as P
from jax.experimental import pallas as pl
from jax.experimental.pallas import tpu as pltpu
bf=jnp.bfloat16; f32=jnp.float32
HD=64; HEADS=12
def cost(us):
    return pl.CostEstimate(flops=int(us*1e+10),bytes_accessed=10**5,transcendentals=0)
NEG=-1e30
VA=16*2**20
VB=60*2**20
LOG2E=math.log2(math.e)
TN=(((0,),(0,)),((),())); NN=(((1,),(0,)),((),())); NT=(((1,),(1,)),((),()))
def dg(a,b,dims): return lax.dot_general(a,b,dims,preferred_element_type=f32)
def rows16(cols, width, pad=16):
    idx=lax.broadcasted_iota(jnp.int32,(pad,width),0)
    out=jnp.zeros((pad,width),f32)
    for i,c in enumerate(cols): out=jnp.where(idx==i,c,out)
    return out.astype(bf)
def split3(x):
    hi=x.astype(bf).astype(f32); r=x-hi; mid=r.astype(bf).astype(f32); lo=r-mid
    return hi,mid,lo
def scaled_query(qT):
    s=qT.astype(f32)*(0.125*LOG2E)
    hi=s.astype(bf); lo=(s-hi.astype(f32)).astype(bf)
    return hi,lo


def causal_mask(x,q0,bq,fill):
    ki=lax.broadcasted_iota(jnp.int32,(bq,bq),0); qi=lax.broadcasted_iota(jnp.int32,(bq,bq),1)
    d=jnp.where(ki<=qi,x[q0:],fill)
    return jnp.concatenate([x[:q0],d],axis=0) if q0 else d

def fwd_kernel(len_ref,qT_ref,kT_ref,vT_ref,oT_ref,lse_ref,*,causal,bq,hs):
    L=qT_ref.shape[1]; K=kT_ref.shape[1]
    n=len_ref[0]
    kpos=lax.broadcasted_iota(jnp.int32,(1,K),1)
    kx=rows16([jnp.where(kpos<n,0.0,NEG)],K); qx=rows16([jnp.ones((1,L),f32)],L); vx=rows16([jnp.ones((1,K),f32)],K)
    ops=[]
    for h in range(hs):
        r=slice(h*HD,(h+1)*HD)
        kT=kT_ref[r,:]
        hi,lo=scaled_query(qT_ref[r,:])
        ops.append((jnp.concatenate([kT,kT,kx],axis=0),jnp.concatenate([hi,lo,qx],axis=0),jnp.concatenate([vT_ref[r,:],vx],axis=0)))
    jobs=[(h,q0) for h in range(hs) for q0 in range(0,L,bq)]
    def score(j):
        h,q0=j; ke=min(K,q0+bq) if causal else K
        return dg(ops[h][0][:,:ke],ops[h][1][:,q0:q0+bq],TN)
    nxt=score(jobs[0])
    for i,(h,q0) in enumerate(jobs):
        s=nxt
        if i+1<len(jobs): nxt=score(jobs[i+1])
        ke=s.shape[0]
        if causal: s=causal_mask(s,q0,bq,NEG)
        m=jnp.max(s,axis=0,keepdims=True)
        p=jnp.exp2(s-m).astype(bf)
        o=dg(ops[h][2][:,:ke],p,NN)
        l=o[HD:HD+1]
        oT_ref[h*HD:(h+1)*HD,q0:q0+bq]=(o[:HD]*(1.0/l)).astype(bf)
        lse_ref[h,:,q0:q0+bq]=m+jnp.log2(l)

def head_block(hs,w,offset=0):
    return pl.BlockSpec((hs*HD,w),lambda h:(h+offset//hs,0))
def fwd_part_kernel(*refs,**kw):
    fwd_kernel(*refs[:4],*refs[6:],**kw)
def attn_fwd(n,q,k,v,causal,bq=256,hs=2,part=None,into=None,vmem=VA):
    L=q[0].shape[1]; K=k[0].shape[1]; D=HEADS*HD
    h0,hn=part or (0,HEADS)
    hb=lambda w,o=0: head_block(hs,w,o+h0)
    specs=[pl.BlockSpec(memory_space=pltpu.SMEM),hb(L,q[1]),hb(K,k[1]),hb(K,v[1])]
    args=(n,q[0],k[0],v[0])
    if into is not None:
        specs+=[pl.BlockSpec(memory_space=pl.ANY)]*2
        args+=tuple(into)
    return pl.pallas_call(functools.partial(fwd_kernel if into is None else fwd_part_kernel,causal=causal,bq=bq,hs=hs),grid=(hn//hs,),
      in_specs=specs,
      out_specs=[hb(L),pl.BlockSpec((hs,1,L),lambda h:(h+h0//hs,0,0))],
      out_shape=[jax.ShapeDtypeStruct((D,L),bf),jax.ShapeDtypeStruct((HEADS,1,L),f32)],
      input_output_aliases={} if into is None else {4:0,5:1},
      cost_estimate=cost(0.3),compiler_params=pltpu.CompilerParams(vmem_limit_bytes=vmem),
    )(*args)

def bwd_kernel(len_ref,qT_ref,kT_ref,vT_ref,oT_ref,gT_ref,lse_ref,dq_ref,dk_ref,dv_ref,dka,dva,*,causal,bq,hs):
    L=qT_ref.shape[1]; K=kT_ref.shape[1]
    n=len_ref[0]
    kpos=lax.broadcasted_iota(jnp.int32,(1,K),1)
    bias=jnp.where(kpos<n,0.0,NEG)
    one_k=jnp.ones((1,K),f32)
    kx=rows16([bias,one_k,one_k,one_k],K); vx=rows16([one_k,one_k,one_k],K)
    ops=[]
    for h in range(hs):
        r=slice(h*HD,(h+1)*HD)
        kT=kT_ref[r,:]; qT=qT_ref[r,:]; gT=gT_ref[r,:]
        hi,lo=scaled_query(qT)
        delta=jnp.sum(oT_ref[r,:].astype(f32)*gT.astype(f32),axis=0,keepdims=True)
        ops.append(dict(k=kT,q=qT,g=gT,kaug=jnp.concatenate([kT,kT,kx],axis=0),
          qaug=jnp.concatenate([hi,lo,rows16([jnp.ones((1,L),f32),*split3(-lse_ref[h])],L)],axis=0),
          vaug=jnp.concatenate([vT_ref[r,:],vx],axis=0),
          gaug=jnp.concatenate([gT,rows16(list(split3(-delta)),L)],axis=0)))
    jobs=[(h,q0) for h in range(hs) for q0 in reversed(range(0,L,bq))]
    def score(j):
        h,q0=j; ke=min(K,q0+bq) if causal else K; sl=slice(q0,q0+bq); o=ops[h]
        return dg(o["kaug"][:,:ke],o["qaug"][:,sl],TN),dg(o["vaug"][:,:ke],o["gaug"][:,sl],TN)
    nxt=score(jobs[0])
    for i,(h,q0) in enumerate(jobs):
        s,dp=nxt
        if i+1<len(jobs): nxt=score(jobs[i+1])
        ke=s.shape[0]; sl=slice(q0,q0+bq); o=ops[h]; r=slice(h*HD,(h+1)*HD)
        p=jnp.exp2(s)
        if causal: p=causal_mask(p,q0,bq,0.0)
        ds=(p*dp).astype(bf)
        pb=p.astype(bf)
        dq_ref[r,sl]=(dg(o["k"][:,:ke],ds,NN)*0.125).astype(bf)
        dv=dg(o["g"][:,sl],pb,NT)
        dk=dg(o["q"][:,sl],ds,NT)
        if q0==L-bq:
            dka[r]=dk; dva[r]=dv
        else:
            dka[r,:ke]+=dk; dva[r,:ke]+=dv
    dk_ref[...]=(dka[...]*0.125).astype(bf)
    dv_ref[...]=dva[...].astype(bf)

def bwd_part_kernel(*refs,**kw):
    bwd_kernel(*refs[:7],*refs[10:],**kw)
def attn_bwd(n,q,k,v,oT,gT,lse,causal,bq=256,hs=2,part=None,into=None,vmem=VA):
    L=q[0].shape[1]; K=k[0].shape[1]; D=HEADS*HD
    h0,hn=part or (0,HEADS)
    hb=lambda w,o=0: head_block(hs,w,o+h0)
    S=jax.ShapeDtypeStruct
    specs=[pl.BlockSpec(memory_space=pltpu.SMEM),hb(L,q[1]),hb(K,k[1]),hb(K,v[1]),hb(L),hb(L),pl.BlockSpec((hs,1,L),lambda h:(h+h0//hs,0,0))]
    args=(n,q[0],k[0],v[0],oT,gT,lse)
    if into is not None:
        specs+=[pl.BlockSpec(memory_space=pl.ANY)]*3
        args+=tuple(into)
    return pl.pallas_call(functools.partial(bwd_kernel if into is None else bwd_part_kernel,causal=causal,bq=bq,hs=hs),grid=(hn//hs,),
      in_specs=specs,out_specs=[hb(L),hb(K),hb(K)],
      out_shape=[S((D,L),bf),S((D,K),bf),S((D,K),bf)],
      input_output_aliases={} if into is None else {7:0,8:1,9:2},
      scratch_shapes=[pltpu.VMEM((hs*HD,K),f32),pltpu.VMEM((hs*HD,K),f32)],
      cost_estimate=cost(14),compiler_params=pltpu.CompilerParams(vmem_limit_bytes=vmem),
    )(*args)

TT=(((0,),(1,)),((),()))
EPS=1e-6
VL=60*2**20
def cp(mb=24): return pltpu.CompilerParams(vmem_limit_bytes=mb*2**20)
def full(shape): return pl.BlockSpec(shape,lambda i:(0,)*len(shape))
GC=0.7978845608028654

def rms_r(v): return lax.rsqrt(jnp.mean(v*v,axis=-1,keepdims=True)+EPS)

def wcol(D,j): return pl.BlockSpec((D,D),lambda i:(0,j))
def gain_spec(D): return pl.BlockSpec((8,D),lambda i:(0,0))

def proj_kernel(x_ref,e_ref,w_ref,n_ref,yT_ref,g_ref):
    @pl.when(pl.program_id(0)==0)
    def _():
        g=e_ref[...].astype(f32).T[0:8,:]
        g_ref[...]=g
        x=x_ref[...].astype(f32)
        n_ref[...]=(x*rms_r(x)*g[0:1,:]).astype(bf)
    yT_ref[...]=dg(w_ref[...],n_ref[...],TT).astype(bf)
def norm_proj(x,w,fb=384):
    L,D=x.shape; F=3*D
    return pl.pallas_call(proj_kernel,grid=(F//fb,),
      in_specs=[full((L,D)),pl.BlockSpec((D,128),lambda i:(0,F//128)),pl.BlockSpec((D,fb),lambda i:(0,i))],
      out_specs=[full((L,D)),pl.BlockSpec((fb,L),lambda i:(i,0)),gain_spec(D)],
      out_shape=[jax.ShapeDtypeStruct((L,D),bf),jax.ShapeDtypeStruct((F,L),bf),jax.ShapeDtypeStruct((8,D),f32)],cost_estimate=cost(6),compiler_params=cp())(x,w,w)
def memproj_kernel(x_ref,w_ref,yT_ref):
    yT_ref[...]=dg(w_ref[...],x_ref[...],TT).astype(bf)
def mem_proj(x,w,first_col,fb=384):
    L,D=x.shape; F=2*D
    return pl.pallas_call(memproj_kernel,grid=(F//fb,),
      in_specs=[full((L,D)),pl.BlockSpec((D,fb),lambda i:(0,first_col//fb+i))],
      out_specs=pl.BlockSpec((fb,L),lambda i:(i,0)),
      out_shape=jax.ShapeDtypeStruct((F,L),bf),cost_estimate=cost(0.1),compiler_params=cp())(x,w)

def post_self_kernel(x_ref,oT_ref,w3_ref,w4_ref,g_ref,h_ref,n_ref,cT_ref):
    h=x_ref[...].astype(f32)+dg(oT_ref[...],w3_ref[...],TT)
    h_ref[...]=h
    n=(h*rms_r(h)*g_ref[1:2,:]).astype(bf)
    n_ref[...]=n
    cT_ref[...]=dg(n,w4_ref[...],NN).astype(bf).T
def post_self(x,oT,w,g,tb=256):
    L,D=x.shape
    tok=pl.BlockSpec((tb,D),lambda i:(i,0)); tokT=pl.BlockSpec((D,tb),lambda i:(0,i))
    return pl.pallas_call(post_self_kernel,grid=(L//tb,),
      in_specs=[tok,tokT,wcol(D,0),wcol(D,1),gain_spec(D)],
      out_specs=[tok,tok,tokT],
      out_shape=[jax.ShapeDtypeStruct((L,D),f32),jax.ShapeDtypeStruct((L,D),bf),jax.ShapeDtypeStruct((D,L),bf)],cost_estimate=cost(0.3),compiler_params=cp())(x,oT,w,w,g)

def mlp_chunk(n3,gb,wg,wu,wd,dw_ref,inner_s,dgate_s,dup_s,oacc,nacc,tb):
    L=n3.shape[0]; nt=L//tb
    def pre(t):
        sl=slice(t*tb,(t+1)*tb)
        a=n3[sl,:]
        return dg(a,wg(),NN),dg(a,wu(),NN),dg(gb[sl,:],wd(),NN)
    nxt=pre(0)
    for t in range(nt):
        sl=slice(t*tb,(t+1)*tb)
        g,u,di=nxt
        if t+1<nt: nxt=pre(t+1)
        g2=g*g
        th=jnp.tanh(g*(GC+(GC*0.044715)*g2))
        hp=0.5+0.5*th
        ge=g*hp
        dge=hp+(0.5*g)*(1.0-th*th)*(GC+(3*GC*0.044715)*g2)
        inner=(ge*u).astype(bf)
        dgate=(di*u*dge).astype(bf)
        dup=(di*ge).astype(bf)
        inner_s[sl,:]=inner; dgate_s[sl,:]=dgate; dup_s[sl,:]=dup
        oacc[sl,:]+=dg(inner,wd(),NT)
        nacc[sl,:]+=dg(dgate,wg(),NT)+dg(dup,wu(),NT)
    dw_ref[0]=dg(n3[...],dgate_s[...],TN).astype(bf)
    dw_ref[1]=dg(n3[...],dup_s[...],TN).astype(bf)
    dw_ref[2]=dg(gb[...],inner_s[...],TN).astype(bf)

def mlp_kernel(core_ref,index_ref,len_ref,h1_ref,oT_ref,w7_ref,cot_ref,g_ref,*refs,tb,pieces):
    w_refs=refs[:pieces]
    (out_ref,gh_ref,gmT_ref,gb2_ref,dg_ref,send_ref,keep_ref,
     h2,n3,gb,oacc,nacc,dw,inner_s,dgate_s,dup_s,sems,w,wsems)=refs[pieces:]
    L,D=h1_ref.shape
    F=w_refs[0].shape[1]//3
    fc=dw.shape[3]
    i=pl.program_id(0); count=pl.num_programs(0); half=count//2
    slot=lax.rem(i,2)
    def copy(step,to):
        col=pl.multiple_of(lax.rem(step,half)*fc,fc)
        return pltpu.make_async_copy(dw.at[lax.rem(step,2)],to.at[:,:,pl.ds(col,fc)],sems.at[lax.rem(step,2)])
    def weights(step):
        chunk=lax.rem(step+(1-core_ref[0])*half,count)
        to=lax.rem(step,2)
        return [pltpu.make_async_copy(w_refs[p].at[:,pl.ds(pl.multiple_of(j*F+chunk*fc,fc),fc)],w.at[to,j,index_ref[p]],wsems.at[to,j*pieces+p])
                for j in range(3) for p in range(pieces)]
    @pl.when(i==0)
    def _():
        for c in weights(0): c.start()
    @pl.when(i+1<count)
    def _():
        for c in weights(i+1): c.start()
    @pl.when(i==0)
    def _():
        n=len_ref[0]
        for t in range(L//tb):
            sl=slice(t*tb,(t+1)*tb)
            h=h1_ref[sl,:]+dg(oT_ref[:,sl],w7_ref[...],TT)
            h2[sl,:]=h
            oacc[sl,:]=h
            nacc[sl,:]=jnp.zeros((tb,D),f32)
            n3[sl,:]=(h*rms_r(h)*g_ref[2:3,:]).astype(bf)
            row=t*tb+lax.broadcasted_iota(jnp.int32,(tb,1),0)
            gb[sl,:]=jnp.where(row<n,cot_ref[sl,:].astype(f32),0.0).astype(bf)
    @pl.when(i>=2)
    def _():
        copy(i-2,send_ref).wait()
    for c in weights(i): c.wait()
    wv=[lambda j=j: w[slot,j].reshape(D,fc) for j in range(3)]
    mlp_chunk(n3,gb,wv[0],wv[1],wv[2],dw.at[slot],inner_s,dgate_s,dup_s,oacc,nacc,tb)
    @pl.when(i<half)
    def _():
        copy(i,send_ref).start()
    @pl.when(i>=half)
    def _():
        copy(i,keep_ref).start()
    @pl.when(i==count-1)
    def _():
        acc=jnp.zeros((1,D),f32)
        for t in range(L//tb):
            sl=slice(t*tb,(t+1)*tb)
            h=h2[sl,:]; uu=nacc[sl,:]
            out_ref[sl,:]=oacc[sl,:].astype(bf)
            r=rms_r(h); ug=uu*g_ref[2:3,:]
            gh=gb[sl,:].astype(f32)+r*ug-h*((r*r*r)*jnp.mean(ug*h,axis=-1,keepdims=True))
            acc=acc+jnp.sum(uu*h*r,axis=0,keepdims=True)
            gh_ref[sl,:]=gh
            b=gh.astype(bf)
            gb2_ref[sl,:]=b
            gmT_ref[:,sl]=dg(b,w7_ref[...],NN).astype(bf).T
        dg_ref[...]=acc
        copy(i-1,keep_ref).wait()
        copy(i,keep_ref).wait()
def mlp(core,index,n,h1,oT,w_second,cot,g,parts,fc=512,tb=256):
    L,D=h1.shape; F=parts[0].shape[1]//3; nc=F//fc; count=len(parts)
    whole=lambda shape: pl.BlockSpec(shape,lambda i,c,x:(0,)*len(shape),pipeline_mode=pl.Buffered(1))
    S=jax.ShapeDtypeStruct
    hbm=pl.BlockSpec(memory_space=pl.ANY)
    return pl.pallas_call(functools.partial(mlp_kernel,tb=tb,pieces=count),
      grid_spec=pltpu.PrefetchScalarGridSpec(num_scalar_prefetch=2,grid=(nc,),
      in_specs=[pl.BlockSpec(memory_space=pltpu.SMEM),whole((L,D)),whole((D,L)),pl.BlockSpec((D,D),lambda i,c,x:(0,4),pipeline_mode=pl.Buffered(1)),whole((L,D)),whole((8,D))]+[hbm]*count,
      out_specs=[whole((L,D)),whole((L,D)),whole((D,L)),whole((L,D)),whole((1,D)),hbm,hbm],
      scratch_shapes=[pltpu.VMEM((L,D),f32),pltpu.VMEM((L,D),bf),pltpu.VMEM((L,D),bf),pltpu.VMEM((L,D),f32),pltpu.VMEM((L,D),f32),
        pltpu.VMEM((2,3,D,fc),bf),pltpu.VMEM((L,fc),bf),pltpu.VMEM((L,fc),bf),pltpu.VMEM((L,fc),bf),pltpu.SemaphoreType.DMA((2,)),
        pltpu.VMEM((2,3,count,D//count,fc),bf),pltpu.SemaphoreType.DMA((2,3*count))]),
      out_shape=[S((L,D),bf),S((L,D),f32),S((D,L),bf),S((L,D),bf),S((1,D),f32),S((3,D,F//2),bf),S((3,D,F//2),bf)],
      cost_estimate=cost(42),compiler_params=cp(48))(core,index,n,h1,oT,w_second,cot,g,*parts)

def mid_kernel(h1_ref,gh2_ref,dcT_ref,w4_ref,w3_ref,g_ref,gh1_ref,gmT_ref,gb_ref,dg_ref):
    i=pl.program_id(0)
    u=dg(dcT_ref[...],w4_ref[...],TT)
    h=h1_ref[...]
    r=rms_r(h); ug=u*g_ref[1:2,:]
    gh=gh2_ref[...]+r*ug-h*((r*r*r)*jnp.mean(ug*h,axis=-1,keepdims=True))
    gh1_ref[...]=gh
    b=gh.astype(bf)
    gb_ref[...]=b
    gmT_ref[...]=dg(b,w3_ref[...],NN).astype(bf).T
    s=jnp.sum(u*h*r,axis=0,keepdims=True)
    @pl.when(i==0)
    def _(): dg_ref[...]=s
    @pl.when(i>0)
    def _(): dg_ref[...]+=s
def mid(h1,gh2,dcT,w,g,tb=256):
    L,D=h1.shape
    tok=pl.BlockSpec((tb,D),lambda i:(i,0)); tokT=pl.BlockSpec((D,tb),lambda i:(0,i))
    S=jax.ShapeDtypeStruct
    return pl.pallas_call(mid_kernel,grid=(L//tb,),
      in_specs=[tok,tok,tokT,wcol(D,1),wcol(D,0),gain_spec(D)],
      out_specs=[tok,tokT,tok,full((1,D))],
      out_shape=[S((L,D),f32),S((D,L),bf),S((L,D),bf),S((1,D),f32)],cost_estimate=cost(0.2),compiler_params=cp())(h1,gh2,dcT,w,w,g)

def wgrads_kernel(core_ref,*refs,pairs,na,ng):
    a_refs=refs[:na]; g_refs=refs[na:na+ng]; send_ref,keep_ref=refs[na+ng:]
    k=core_ref[0]
    W=send_ref.shape[2]
    for out,half in ((send_ref,1-k),(keep_ref,k)):
        start=pl.multiple_of(half*W,W)
        for m,(ia,ig) in enumerate(pairs):
            out[m]=dg(a_refs[ia][...],g_refs[ig][pl.ds(start,W),:],TT).astype(bf)
def wgrads(core,a,g,pairs):
    D=a[0].shape[1]; F=g[0].shape[0]
    v=pl.BlockSpec(memory_space=pltpu.VMEM)
    S=jax.ShapeDtypeStruct((len(pairs),D,F//2),bf)
    return pl.pallas_call(functools.partial(wgrads_kernel,pairs=tuple(pairs),na=len(a),ng=len(g)),
      in_specs=[pl.BlockSpec(memory_space=pltpu.SMEM)]+[v]*(len(a)+len(g)),out_specs=[v,v],
      out_shape=[S,S],cost_estimate=cost(8),compiler_params=cp(40))(core,*a,*g)

def gmem_kernel(kT_ref,vT_ref,w5_ref,w6_ref,o_ref):
    o_ref[...]=(dg(kT_ref[...],w5_ref[...],TT)+dg(vT_ref[...],w6_ref[...],TT)).astype(bf)
def gmem(kT,vT,w56,tb=256):
    D,L=kT.shape
    tokT=pl.BlockSpec((D,tb),lambda i:(0,i))
    return pl.pallas_call(gmem_kernel,grid=(L//tb,),
      in_specs=[tokT,tokT,wcol(D,2),wcol(D,3)],
      out_specs=pl.BlockSpec((tb,D),lambda i:(i,0)),
      out_shape=jax.ShapeDtypeStruct((L,D),bf),cost_estimate=cost(0.2),compiler_params=cp())(kT,vT,w56,w56)

def first_kernel(x_ref,gh1_ref,qT_ref,kT_ref,vT_ref,w0_ref,w1_ref,w2_ref,g_ref,gt_ref,dg_ref):
    i=pl.program_id(0)
    u=dg(qT_ref[...],w0_ref[...],TT)+dg(kT_ref[...],w1_ref[...],TT)+dg(vT_ref[...],w2_ref[...],TT)
    h=x_ref[...].astype(f32)
    r=rms_r(h); ug=u*g_ref[0:1,:]
    gt_ref[...]=gh1_ref[...]+r*ug-h*((r*r*r)*jnp.mean(ug*h,axis=-1,keepdims=True))
    s=jnp.sum(u*h*r,axis=0,keepdims=True)
    @pl.when(i==0)
    def _(): dg_ref[...]=s
    @pl.when(i>0)
    def _(): dg_ref[...]+=s
def first(x,gh1,qT,kT,vT,w,g,tb=256):
    L,D=x.shape
    tok=pl.BlockSpec((tb,D),lambda i:(i,0)); tokT=pl.BlockSpec((D,tb),lambda i:(0,i))
    S=jax.ShapeDtypeStruct
    wb=lambda j: pl.BlockSpec((D,D),lambda i,j=j:(0,j))
    return pl.pallas_call(first_kernel,grid=(L//tb,),
      in_specs=[tok,tok,tokT,tokT,tokT,wb(0),wb(1),wb(2),gain_spec(D)],
      out_specs=[tok,full((1,D))],
      out_shape=[S((L,D),f32),S((1,D),f32)],cost_estimate=cost(7),compiler_params=cp())(x,gh1,qT,kT,vT,w,w,w,g)

SEQ="seq"
MEM="mem"


def plane_bits(seq_size):
    return max(0,(seq_size//2).bit_length()-1)


def bit_order(core,bits):
    order=list(range(1,bits+1))
    return order if core==0 else order[::-1]


def subset_mask(core,subset,bits):
    order=bit_order(core,bits)
    mask=0
    for p in range(bits):
        if subset>>p&1:
            mask^=1<<(order[p]-1)
    return mask


def cross(x,position,seq_size):
    bits=plane_bits(seq_size)
    perm=[(s,s^(1<<bit_order(s&1,bits)[position])) for s in range(seq_size)]
    return lax.ppermute(x,SEQ,perm)


def swap_core(x,seq_size):
    return lax.ppermute(x,SEQ,[(s,s^1) for s in range(seq_size)])


def shift_mem(x,step,mem_size):
    return lax.ppermute(x,MEM,[(z,(z+step)%mem_size) for z in range(mem_size)])


def copy_kernel(index_ref,*refs,places,columns):
    count=len(places)
    sources=refs[:count]; out=refs[count]; sems=refs[count+1]
    copies=[]
    for j,(source,place) in enumerate(zip(sources,places)):
        if columns is not None:
            source=source.at[:,pl.ds(columns[0],columns[1]-columns[0])]
        copies.append(pltpu.make_async_copy(source,out.at[index_ref[place]],sems.at[j]))
        copies[-1].start()
    for c in copies:
        c.wait()


def place_rows(index,pieces,places,slots,us,columns=None):
    piece=pieces[0]
    shape=piece.shape if columns is None else (piece.shape[0],columns[1]-columns[0])
    return pl.pallas_call(functools.partial(copy_kernel,places=tuple(places),columns=columns),
        in_specs=[pl.BlockSpec(memory_space=pltpu.SMEM)]+[pl.BlockSpec(memory_space=pl.ANY)]*len(pieces),
        out_specs=pl.BlockSpec(memory_space=pltpu.VMEM),
        out_shape=jax.ShapeDtypeStruct((slots,)+shape,piece.dtype),
        scratch_shapes=[pltpu.SemaphoreType.DMA((len(pieces),))],
        cost_estimate=cost(us),compiler_params=cp(20),
    )(index,*pieces)


class Place:
    def __init__(self,seq_size,mem_size):
        self.S=seq_size; self.M=mem_size; self.bits=plane_bits(seq_size); self.NP=seq_size//2
        s=lax.axis_index(SEQ); self.z=lax.axis_index(MEM)
        self.core=s%2; self.plane=s//2

    def slab(self,subset,own=True):
        m0=subset_mask(0,subset,self.bits); m1=subset_mask(1,subset,self.bits)
        c=self.core if own else 1-self.core
        return self.plane^jnp.where(c==0,m0,m1)


def gather_mem_direct(shard,pl_):
    M=pl_.M
    pieces=[shard]+[shift_mem(shard,j,M) for j in range(1,M)]
    index=jnp.stack([(pl_.z-j)%M for j in range(M)]).astype(jnp.int32)
    return place_rows(index,pieces,range(M),M,3).reshape(M*shard.shape[0],shard.shape[1])


def gather_mem_exchange(shard,here):
    M=here.M
    copies=jnp.broadcast_to(shard[None],(M,)+shard.shape)
    return lax.all_to_all(copies,MEM,split_axis=0,concat_axis=0,tiled=True).reshape(M*shard.shape[0],shard.shape[1])


def tie(*values):
    return lax.optimization_barrier(values)


class Ring:
    def __init__(self,shard,here):
        self.here=here; self.got=[shard]
        self.next()

    def next(self):
        if len(self.got)<self.here.M:
            self.got.append(shift_mem(self.got[-1],1,self.here.M))

    def step(self,dep):
        self.got[-1],dep=tie(self.got[-1],dep)
        self.next()
        return dep

    def finish(self,dep):
        while len(self.got)<self.here.M:
            self.next()
        self.got[-1],dep=tie(self.got[-1],dep)
        return dep

    def place(self,first,end):
        M=self.here.M
        index=jnp.stack([(self.here.z-j)%M for j in range(M)]).astype(jnp.int32)
        rows=self.got[0].shape[0]
        return place_rows(index,self.got,range(M),M,0.05,(first,end)).reshape(M*rows,end-first)


class Gather:
    def __init__(self,slab,here):
        self.here=here; self.pieces={0:slab}; self.other={}
        for p in range(here.bits):
            self.pieces[1<<p]=cross(slab,p,here.S)

    def arrived(self,dep,keys=None):
        keys=sorted(self.pieces) if keys is None else keys
        others=sorted(self.other)
        out=tie(*[self.pieces[s] for s in keys],*[self.other[s] for s in others],dep)
        self.pieces.update(zip(keys,out)); self.other.update(zip(others,out[len(keys):]))
        return out[-1]

    def forward(self):
        here=self.here
        for subset in range(1,here.NP):
            top=subset.bit_length()-1
            if subset not in self.pieces:
                self.pieces[subset]=cross(self.pieces[subset^(1<<top)],top,here.S)

    def swap(self):
        for subset in sorted(self.pieces):
            if subset not in self.other and subset!=self.here.NP-1:
                self.other[subset]=swap_core(self.pieces[subset],self.here.S)

    def swap_last(self):
        end=self.here.NP-1
        if end not in self.other:
            self.other[end]=swap_core(self.pieces[end],self.here.S)

    def parts(self):
        here=self.here
        n=here.NP
        idx=[here.slab(s)*2+here.core for s in range(n)]+[here.slab(s,False)*2+1-here.core for s in range(n)]
        index=jnp.stack(idx).astype(jnp.int32)
        parts=[self.pieces[s] for s in range(n)]+[self.other[s] for s in range(n)]
        return index,parts

    def place(self):
        index,parts=self.parts()
        out=place_rows(index,parts,range(len(parts)),len(parts),0.05)
        return out.reshape(-1,parts[0].shape[1])


def fold_kernel(index_ref,ka,kb,ra,rb,send,keep):
    send[...]=(kb[...].astype(f32)+rb[...].astype(f32)).astype(bf)
    keep[...]=(ka[...].astype(f32)+ra[...].astype(f32)).astype(bf)


def fold(index,keep,recv):
    G,n,R,W=keep.shape; h=n//2
    low=pl.BlockSpec((1,1,R,W),lambda i,m,ix:(m,ix[i],0,0))
    high=pl.BlockSpec((1,1,R,W),lambda i,m,ix:(m,ix[h+i],0,0))
    out=pl.BlockSpec((1,1,R,W),lambda i,m,ix:(m,i,0,0))
    S=jax.ShapeDtypeStruct((G,h,R,W),bf)
    return pl.pallas_call(fold_kernel,
        grid_spec=pltpu.PrefetchScalarGridSpec(num_scalar_prefetch=1,grid=(h,G),in_specs=[low,high,low,high],out_specs=[out,out]),
        out_shape=[S,S],cost_estimate=cost(3),compiler_params=cp(16))(index,keep,keep,recv,recv)


def split_kernel(index_ref,a,b,*outs):
    for j,o in enumerate(outs):
        z=index_ref[j]
        o[...]=(a[:,:,pl.ds(z,1)].astype(f32)+b[:,:,pl.ds(z,1)].astype(f32)).astype(bf)


def split_mem(index,a,b):
    G,two,M,r,W=a.shape
    full_=pl.BlockSpec(memory_space=pltpu.VMEM)
    S=jax.ShapeDtypeStruct((G,two,1,r,W),bf)
    return pl.pallas_call(split_kernel,in_specs=[pl.BlockSpec(memory_space=pltpu.SMEM),full_,full_],out_specs=[full_]*M,
        out_shape=[S]*M,cost_estimate=cost(2),compiler_params=cp(16))(index,a,b)


def order_kernel(a,b,o):
    for z in range(o.shape[0]):
        o[z]=(a[:,:,z].astype(f32)+b[:,:,z].astype(f32)).astype(bf)


def order_mem(a,b):
    G,two,M,r,W=a.shape
    v=pl.BlockSpec(memory_space=pltpu.VMEM)
    return pl.pallas_call(order_kernel,in_specs=[v,v],out_specs=v,
        out_shape=jax.ShapeDtypeStruct((M,G,two,r,W),bf),cost_estimate=cost(2),compiler_params=cp(16))(a,b)


class Reduce:
    def __init__(self,send,keep,here):
        G,D,W=send.shape
        NP=here.NP; R=D//NP
        self.here=here; self.r=R//2//here.M
        self.recv=swap_core(send,here.S).reshape(G,NP,R,W)
        self.keep=keep.reshape(G,NP,R,W)
        self.index=jnp.stack([here.slab(s) for s in range(NP)]).astype(jnp.int32)
        self.p=here.bits-1

    def fold(self,dep):
        self.recv,dep=tie(self.recv,dep)
        if self.p<0:
            return dep
        go,keep=fold(self.index,self.keep,self.recv)
        go,self.keep,dep=tie(go,keep,dep)
        self.recv=cross(go,self.p,self.here.S)
        self.index=jnp.arange(1<<self.p,dtype=jnp.int32)
        self.p-=1
        return dep

    def halves(self,dep):
        while self.p>=0:
            dep=self.fold(dep)
        self.recv,dep=tie(self.recv,dep)
        G,_,R,W=self.keep.shape
        shape=(G,2,self.here.M,self.r,W)
        return self.keep.reshape(shape),self.recv.reshape(shape),dep

    def over_mem(self,dep):
        a,b,dep=self.halves(dep)
        parts,dep=tie(order_mem(a,b),dep)
        return lax.psum_scatter(parts,MEM,scatter_dimension=0,tiled=True)[0],dep

    def mem_start(self,dep):
        a,b,dep=self.halves(dep)
        M=self.here.M
        parts=split_mem(jnp.stack([(self.here.z+j)%M for j in range(M)]).astype(jnp.int32),a,b)
        out=tie(*parts,dep)
        parts,dep=out[:-1],out[-1]
        self.got=[parts[0]]+[shift_mem(parts[j],j,M) for j in range(1,M)]
        return dep

    def mem_sum(self,dep):
        out=tie(*self.got,dep)
        total=out[0].astype(f32)
        for p in out[1:-1]:
            total=total+p.astype(f32)
        G,_,_,r,W=total.shape
        return total.reshape(G,2,r,W),out[-1]


def own_rows(total,pl_):
    give=lax.dynamic_index_in_dim(total,1-pl_.core,1,keepdims=False)
    own=lax.dynamic_index_in_dim(total,pl_.core,1,keepdims=False)
    other=swap_core(give,pl_.S)
    low=jnp.where(pl_.core==0,own,other); high=jnp.where(pl_.core==0,other,own)
    return jnp.concatenate([low,high],axis=-1)


def sum_all(x,pl_):
    for b in range(pl_.S.bit_length()-1):
        x=x+lax.ppermute(x,SEQ,[(s,s^(1<<b)) for s in range(pl_.S)])
    for b in range(pl_.M.bit_length()-1):
        x=x+lax.ppermute(x,MEM,[(z,z^(1<<b)) for z in range(pl_.M)])
    return x

STEP=10
CLIP_NORM=1.0
BETA_FIRST=0.9
BETA_SECOND=0.999
ADAM_EPSILON=1e-08
RATE_MATRIX=0.06
RATE_GAIN=0.6
DECAY_MATRIX=0.01


def adam_step(master,grad,first_moment,second_moment,rate,decay):
    first_new=BETA_FIRST*first_moment+(1.0-BETA_FIRST)*grad
    second_new=BETA_SECOND*second_moment+(1.0-BETA_SECOND)*grad*grad
    first_hat=first_new/(1.0-BETA_FIRST**STEP)
    second_hat=second_new/(1.0-BETA_SECOND**STEP)
    master_new=master-rate*(first_hat/(jnp.sqrt(second_hat)+ADAM_EPSILON)+decay*master)
    return (master_new,first_new,second_new)


def columns(stack):
    return jnp.concatenate([stack[i] for i in range(stack.shape[0])],axis=1)


def on_device(seq_size,mem_size,tokens,memory,cotangent,table_len,patch_count,attn_master,attn_first,attn_second,mlp_master,mlp_first,mlp_second,gain_master,gain_first,gain_second):
    here=Place(seq_size,mem_size)
    core=here.core.reshape(1).astype(jnp.int32)
    rows,D=attn_master.shape[1:]
    aw=attn_master.astype(bf)
    gain_cols=jnp.pad(gain_master.T,((0,0),(0,125))).astype(bf)
    x=tokens[0]
    slab=gather_mem_direct(jnp.concatenate([columns(aw[:3]),gain_cols],axis=1),here)
    later=jnp.concatenate([columns(aw[3:]),columns(mlp_master.astype(bf))],axis=1)
    slab,later=tie(slab,later)
    g1=Gather(slab,here)
    ring=Ring(later,here)
    g1.forward()
    g1.pieces[2]=ring.step(g1.pieces[2])
    x=g1.arrived(x)
    g1.swap(); g1.swap_last()
    g1.other[here.NP-1]=ring.step(g1.other[here.NP-1])
    g1.other[here.NP-1],memory=tie(g1.other[here.NP-1],memory)
    mem=lax.all_to_all(memory,"mem",split_axis=0,concat_axis=0,tiled=True).reshape(-1,D)
    w_first=g1.place()
    n1,qkv,gains=norm_proj(x,w_first)
    qkv=ring.finish(qkv)
    g2=Gather(ring.place(0,5*D),here)
    slab_mlp=ring.place(5*D,later.shape[1])
    q,k,v=(qkv,0),(qkv,HEADS),(qkv,2*HEADS)
    o1,lse1=attn_fwd(table_len,q,k,v,True,512,4,(0,8))
    o1=g2.arrived(o1)
    g2.forward(); g2.swap()
    o1,slab_mlp=tie(o1,slab_mlp)
    g3=Gather(slab_mlp,here)
    o1,lse1=attn_fwd(table_len,q,k,v,True,512,4,(8,4),(o1,lse1))
    o1=g2.arrived(o1)
    g2.swap_last()
    w_second=g2.place()
    w_second,mem=tie(w_second,mem)
    mkv=mem_proj(mem,w_second,2*D)
    mkv,o1=tie(mkv,o1)
    o1=g3.arrived(o1)
    g3.forward(); g3.swap()
    h1,n2,cq=post_self(x,o1,w_second,gains)
    q2,k2,v2=(cq,0),(mkv,0),(mkv,HEADS)
    half=HEADS//2
    o2,lse2=attn_fwd(patch_count,q2,k2,v2,False,512,2,(0,half),None,VB)
    o2=g3.arrived(o2)
    g3.swap_last()
    o2,lse2=attn_fwd(patch_count,q2,k2,v2,False,512,2,(half,half),(o2,lse2),VB)
    o2=g3.arrived(o2)
    w_index,w_parts=g3.parts()
    mixed_out,gh2,gm2,gb2,dg3,mlp_send,mlp_keep=mlp(core,w_index,table_len,h1,o2,w_second,cotangent[0],gains,w_parts)
    r1=Reduce(mlp_send,mlp_keep,here)
    part=attn_bwd(patch_count,q2,k2,v2,o2,gm2,lse2,False,256,2,(0,half),None,VB)
    part=(r1.fold(part[0]),)+tuple(part[1:])
    dcq,dmk,dmv=attn_bwd(patch_count,q2,k2,v2,o2,gm2,lse2,False,256,2,(half,half),part)
    gmem_local,dcq=tie(gmem(dmk,dmv,w_second),dcq)
    grad_memory=lax.all_to_all(gmem_local.reshape(memory.shape),"mem",split_axis=0,concat_axis=0,tiled=True).astype(f32)
    gh1,gm1,gb1,dg2=mid(h1,gh2,dcq,w_second,gains)
    gb1=r1.fold(gb1)
    second_send,second_keep=wgrads(core,[gb1,n2,mem,gb2],[o1,dcq,dmk,dmv,o2],[(0,0),(1,1),(2,2),(2,3),(3,4)])
    second_send,gm1=tie(second_send,gm1)
    r2=Reduce(second_send,second_keep,here)
    gm1=r1.mem_start(gm1)
    gm1=r2.fold(gm1)
    dq,dk,dv=attn_bwd(table_len,q,k,v,o1,gm1,lse1,True,256,2)
    first_send,first_keep=wgrads(core,[n1],[dq,dk,dv],[(0,0),(0,1),(0,2)])
    r3=Reduce(first_send,first_keep,here)
    dq,first_keep=tie(dq,first_keep)
    dq=r2.fold(dq)
    dq=r3.fold(dq)
    grad_tokens,dg1=first(x,gh1,dq,dk,dv,w_first,gains)
    t_mlp,dg1=r1.mem_sum(dg1)
    dg1=r3.fold(dg1)
    dg1=r2.mem_start(dg1)
    dg1=r3.mem_start(dg1)
    t_second,dg1=r2.mem_sum(dg1)
    t_first,dg1=r3.mem_sum(dg1)
    totals=(t_first,t_second,t_mlp)
    squares=jnp.sum(t_first*t_first)+(jnp.sum(t_second*t_second)+jnp.sum(t_mlp*t_mlp))
    summed=sum_all(jnp.concatenate([dg1,dg2,dg3,jnp.broadcast_to(squares,(1,D))],axis=0),here)
    gain_all=summed[:3]
    grad_norm=jnp.sqrt(summed[3,0]+jnp.sum(gain_all*gain_all))
    factor=CLIP_NORM/jnp.maximum(grad_norm,CLIP_NORM)
    red=[own_rows(t,here) for t in totals]
    attn_red=jnp.concatenate(red[:2],axis=0)
    mlp_red=red[2]
    device=lax.axis_index("seq")*mem_size+lax.axis_index("mem")
    gain_red=lax.dynamic_slice_in_dim(gain_all,device*rows,rows,1)
    a=adam_step(attn_master,attn_red*factor,attn_first,attn_second,RATE_MATRIX,DECAY_MATRIX)
    m=adam_step(mlp_master,mlp_red*factor,mlp_first,mlp_second,RATE_MATRIX,DECAY_MATRIX)
    gn=adam_step(gain_master,gain_red*factor,gain_first,gain_second,RATE_GAIN,0.0)
    return (mixed_out[None],grad_tokens[None],grad_memory,grad_norm)+a+m+gn


def solution(mesh):
    both=P(("seq","mem"),None,None)
    mid_split=P(None,("seq","mem"),None)
    gain_split=P(None,("seq","mem"))
    return jax.shard_map(functools.partial(on_device,mesh.shape["seq"],mesh.shape["mem"]),mesh=mesh,
        in_specs=(both,P("seq","mem",None),both,P(("seq","mem")),P(("seq","mem")))+(mid_split,)*6+(gain_split,)*3,
        out_specs=(both,both,P("seq","mem",None),P())+(mid_split,)*6+(gain_split,)*3,
        check_vma=False)
```
